32 devices in a mesh: gx: 8 (over y, x, core), gy: 4 (over z).
Axes of the slice: x: 2, y: 2, z: 4, core: 2. Of those that a mesh axis runs over, the one named last changes fastest.
Arguments:
- state_now: float32 [32, 128, 4096], P(('gx', 'gy')), may hold values from -6 to 6
- state_prev: float32 [32, 128, 4096], P(('gx', 'gy')), may hold values from -6 to 6
- pml_flags: int32 [32], P(('gx', 'gy')), may hold values 0 or 1
- interfaces: int32 [64, 6], P(('gx', 'gy')), may hold values from -16 to 16, as said below
Outputs:
- new_state: float32 [32, 128, 4096], P(('gx', 'gy'))
- face_pressure: float32 [32, 6, 4096], P(('gx', 'gy'))
The draws below stay inside these ranges and needn't reach their ends.
Inputs may be any that keep to these rules, and one draw needn't show every extreme that they name: `interfaces`: column 0 and column 1 are always 0 (each device holds one box); column 1 names the box of the device one step further along gx and g = column 2 steps across gy; g is -1, 0 or 1 and that device exists whenever column 5 is 1. Columns 3 and 4 are offsets from -16 to 16. Column 5 is 0 exactly on the rows of the last index of gx, which join nothing, and 1 elsewhere.
All inputs are finite; a program needn't handle non-finite values. No bound on the sum of `pml_flags` on one device may be relied on, other than what follows from the above.
Results may differ from the reference program's by a relative error of at most 0.0003.
Values sent between devices are 32-bit elements; how exact they have to be, the bound alone decides.
No kernel may reach another device: no remote copies, remote signals or barrier semaphores. Data moves between devices by JAX's collectives and lax.ppermute only.
A program may use at most 128 MiB of HBM per device.

```python
import math
import jax
import jax.numpy as jnp
from jax import lax

S0 = 128
S1 = 64
S2 = 64
BOX_DEV = 1
STEPS = 3
CROSS = 4096
OFF = 16
IF_DEV = 2
BOXES = 32
IFACES = 64
N_GX = 8
N_GY = 4


def draw_interfaces(key, part):
    row_count = IFACES
    subkeys = jax.random.split(jax.random.fold_in(key, 11), 5)
    row_ids = jnp.arange(row_count, dtype=jnp.int32)
    owners = row_ids // IF_DEV
    across_pos = owners % N_GY
    along_pos = owners // N_GY
    source_box = jax.random.randint(subkeys[0], (row_count,), 0, BOX_DEV).astype(jnp.int32)
    target_box = jax.random.randint(subkeys[1], (row_count,), 0, BOX_DEV).astype(jnp.int32)
    across_step = jax.random.randint(subkeys[2], (row_count,), -1, 2).astype(jnp.int32)
    across_step = jnp.clip(across_pos + across_step, 0, N_GY - 1) - across_pos
    first_displacement = jax.random.randint(subkeys[3], (row_count,), -OFF, OFF + 1).astype(jnp.int32)
    second_displacement = jax.random.randint(subkeys[4], (row_count,), -OFF, OFF + 1).astype(jnp.int32)
    first_displacement = first_displacement.at[0].set(-OFF)
    second_displacement = second_displacement.at[0].set(OFF)
    active = (along_pos < N_GX - 1).astype(jnp.int32)
    return jnp.stack([source_box, target_box, across_step, first_displacement, second_displacement, active], axis=1).astype(jnp.int32)


def place_ends(result, key, low, top_value):
    shape = result.shape
    index_at = [jax.random.randint(jax.random.fold_in(key, axis), (), 0, shape[axis]) for axis in range(len(shape))]
    result = result.at[tuple(index_at)].set(low)
    longest = shape.index(max(shape))
    index_at[longest] = (index_at[longest] + 1) % shape[longest]
    return result.at[tuple(index_at)].set(top_value)


def levels(stream_key, extent, cuts, smallest, largest):
    factor_of = 1.0
    for axis_at, blocks in cuts:
        steps = jax.random.uniform(jax.random.fold_in(jax.random.fold_in(stream_key, 6), axis_at), (blocks,), jnp.float32, smallest / len(cuts), largest / len(cuts))
        factor_of = factor_of * jnp.repeat(jnp.exp(steps), extent[axis_at] // blocks).reshape((-1,) + (1,) * (len(extent) - 1 - axis_at))
    return factor_of


def centred(stream_key, shape, spread, limit, shards=(), held_as=jnp.bfloat16):
    drawn = jax.random.normal(stream_key, shape, jnp.float32) * spread
    if len(shards) > 0:
        drawn = levels(stream_key, shape, shards, -0.22, 0.18) * drawn
    return jnp.clip(drawn, min=-limit, max=limit).astype(held_as)


def setup_inputs(seed: int = 0) -> dict:
    streams_of = jax.random.split(jax.random.key(seed), 5)
    return {
        "state_now": centred(streams_of[0], (BOXES, S0, CROSS), 1.0, 6.0, ((0, 32),), jnp.float32),
        "state_prev": centred(streams_of[1], (BOXES, S0, CROSS), 1.0, 6.0, ((0, 32),), jnp.float32),
        "pml_flags": place_ends((jax.random.randint(streams_of[2], (BOXES,), 0, 4) < 1).astype(jnp.int32), jax.random.fold_in(streams_of[2], 1), 0, 1),
        "interfaces": draw_interfaces(jax.random.fold_in(streams_of[4], 71), 0),
    }


COURANT = 0.4
DAMPING = 0.5
CENTER = -490.0 / 180.0
TOP_PRECISION = lax.Precision.HIGHEST

def cosine_basis(count):
    freqs = jnp.arange(count, dtype=jnp.float32)[:, None]
    cells = jnp.arange(count, dtype=jnp.float32)[None, :]
    weight = jnp.where(freqs == 0.0, jnp.sqrt(1.0 / count), jnp.sqrt(2.0 / count))
    return (weight * jnp.cos(math.pi * freqs * (cells + 0.5) / count)).astype(jnp.float32)

def face_rows():
    return jnp.array([0, 1, 2, S0 - 1, S0 - 2, S0 - 3], dtype=jnp.int32)

def coupling():
    return jnp.array([[1.5, -0.15, 1.0 / 90.0], [-0.15, 1.0 / 90.0, 0.0], [1.0 / 90.0, 0.0, 0.0]], dtype=jnp.float32)

def make_tables():
    basis_zero = cosine_basis(S0)
    basis_one = cosine_basis(S1)
    basis_two = cosine_basis(S2)
    face_basis = basis_zero[:, face_rows()]
    wave_zero = (math.pi * jnp.arange(S0, dtype=jnp.float32) / S0) ** 2
    wave_one = (math.pi * jnp.arange(S1, dtype=jnp.float32) / S1) ** 2
    wave_two = (math.pi * jnp.arange(S2, dtype=jnp.float32) / S2) ** 2
    wave = wave_zero[:, None, None] + wave_one[None, :, None] + wave_two[None, None, :]
    wave = wave.reshape(S0, S1 * S2)
    rooted = jnp.sqrt(wave)
    cosine = jnp.cos(COURANT * rooted)
    safe_wave = jnp.where(wave > 0.0, wave, 1.0)
    gain = jnp.where(wave > 0.0, 4.0 * jnp.sin(0.5 * COURANT * rooted) ** 2 / safe_wave, COURANT * COURANT)
    damping = DAMPING * ((jnp.arange(S0, dtype=jnp.float32) + 0.5) / S0) ** 2
    return (face_basis, basis_one, basis_two, cosine, gain, damping)

def cross_forward(slab, basis_one, basis_two):
    planes = slab.reshape(slab.shape[0], S1, S2)
    inner = jnp.einsum('rab,kb->rak', planes, basis_two, precision=TOP_PRECISION)
    outer = jnp.einsum('ja,rak->rjk', basis_one, inner, precision=TOP_PRECISION)
    return outer.reshape(slab.shape[0], S1 * S2)

def cross_inverse(slab, basis_one, basis_two):
    planes = slab.reshape(slab.shape[0], S1, S2)
    inner = jnp.einsum('rjk,kb->rjb', planes, basis_two, precision=TOP_PRECISION)
    outer = jnp.einsum('ja,rjb->rab', basis_one, inner, precision=TOP_PRECISION)
    return outer.reshape(slab.shape[0], S1 * S2)

def spectral_layers(values, tables):
    face_basis, basis_one, basis_two = (tables[0], tables[1], tables[2])
    coarse = jnp.einsum('kr,kc->rc', face_basis, values, precision=TOP_PRECISION)
    return cross_inverse(coarse, basis_one, basis_two)

def laplacian(values):
    volume = values.reshape(S0, S1, S2)
    padded = jnp.pad(volume, 3)
    summed = 3.0 * CENTER * volume
    for distance, factor in ((1, 1.5), (2, -0.15), (3, 1.0 / 90.0)):
        near = padded[3 + distance:3 + distance + S0, 3:3 + S1, 3:3 + S2] + padded[3 - distance:3 - distance + S0, 3:3 + S1, 3:3 + S2]
        near = near + padded[3:3 + S0, 3 + distance:3 + distance + S1, 3:3 + S2] + padded[3:3 + S0, 3 - distance:3 - distance + S1, 3:3 + S2]
        near = near + padded[3:3 + S0, 3:3 + S1, 3 + distance:3 + distance + S2] + padded[3:3 + S0, 3:3 + S1, 3 - distance:3 - distance + S2]
        summed = summed + factor * near
    return summed.reshape(S0, S1 * S2)

def modal_advance(current, previous, forcing, tables):
    face_basis, basis_one, basis_two, cosine, gain = (tables[0], tables[1], tables[2], tables[3], tables[4])
    slab_hat = cross_forward(forcing, basis_one, basis_two)
    forcing_hat = jnp.einsum('kr,rc->kc', face_basis, slab_hat, precision=TOP_PRECISION)
    return 2.0 * cosine * current - previous + gain * forcing_hat

def damped_advance(current, previous, forcing, tables):
    damping = tables[5]
    middle = jnp.zeros((S0 - 6, S1 * S2), jnp.float32)
    spread_force = jnp.concatenate([forcing[0:3], middle, forcing[3:6][::-1]], axis=0)
    rate = damping[:, None]
    return (2.0 * current - (1.0 - rate) * previous + COURANT * COURANT * (laplacian(current) + spread_force)) / (1.0 + rate)

def shift_face(layer, first_displacement, second_displacement):
    planes = layer.reshape(3, S1, S2)
    padded = jnp.pad(planes, ((0, 0), (OFF, OFF), (OFF, OFF)))
    start_one = (OFF - first_displacement).astype(jnp.int32)
    start_two = (OFF - second_displacement).astype(jnp.int32)
    moved = lax.dynamic_slice(padded, (jnp.zeros((), jnp.int32), start_one, start_two), (3, S1, S2))
    return moved.reshape(3, S1 * S2)

def reference(state_now, state_prev, pml_flags, interfaces):
    tables = make_tables()
    rows_face = face_rows()
    blend_weights = coupling()
    boxes_all = state_now.shape[0]

    def layers_one(packed):
        values, flag = packed
        return jnp.where(flag > 0, values[rows_face], spectral_layers(values, tables))

    def layers_all(current):
        return lax.map(layers_one, (current, pml_flags))

    def interface_forces(layers):

        def add_one(row_id, forces):
            row_id = jnp.asarray(row_id).astype(jnp.int32)
            entry = interfaces[row_id]
            owner = row_id // IF_DEV
            box_high = (owner * BOX_DEV + entry[0]).astype(jnp.int32)
            box_low = jnp.clip((owner + N_GY + entry[2]) * BOX_DEV + entry[1], 0, boxes_all - 1).astype(jnp.int32)
            active = entry[5].astype(jnp.float32)
            high_side = lax.dynamic_index_in_dim(layers, box_high, 0, keepdims=False)[3:6]
            lower_boundary_side = lax.dynamic_index_in_dim(layers, box_low, 0, keepdims=False)[0:3]
            toward_high = active * jnp.einsum('de,ec->dc', blend_weights, shift_face(lower_boundary_side, entry[3], entry[4]), precision=TOP_PRECISION)
            lowerward_direction = active * jnp.einsum('de,dc->ec', blend_weights, shift_face(high_side, -entry[3], -entry[4]), precision=TOP_PRECISION)
            forces = forces.at[box_high, 3:6].add(toward_high)
            forces = forces.at[box_low, 0:3].add(lowerward_direction)
            return forces
        return lax.fori_loop(0, IFACES, add_one, jnp.zeros_like(layers))

    def advance_one(packed):
        current, previous, forcing, flag = packed
        return jnp.where(flag > 0, damped_advance(current, previous, forcing, tables), modal_advance(current, previous, forcing, tables))
    current, previous = (state_now, state_prev)
    for repeat in range(STEPS):
        layers = layers_all(current)
        forces = interface_forces(layers)
        following = lax.map(advance_one, (current, previous, forces, pml_flags))
        previous, current = (current, following)
    return (current, layers_all(current))
```

```python
import functools
import math

import jax
import jax.numpy as jnp
import ml_dtypes
import numpy as np
from jax import lax
from jax.experimental import pallas as pl
from jax.experimental.pallas import tpu as pltpu
from jax.sharding import PartitionSpec as P

STEPS = 3
OFF = 16
COURANT = 0.4
DAMPING = 0.5
STENCIL = (-490.0, 270.0, -27.0, 2.0)
BLEND = ((1.5, -0.15, 1.0 / 90.0), (-0.15, 1.0 / 90.0, 0.0), (1.0 / 90.0, 0.0, 0.0))
SHIFTS = (-1, 0, 1)
CHUNK = 512
BF16 = ml_dtypes.bfloat16


def cosine_basis(count):
    freqs = np.arange(count)[:, None]
    cells = np.arange(count)[None, :]
    weight = np.where(freqs == 0, np.sqrt(1.0 / count), np.sqrt(2.0 / count))
    return weight * np.cos(math.pi * freqs * (cells + 0.5) / count)


def halves(values):
    high = values.astype(BF16)
    return high, (values - high.astype(np.float64)).astype(BF16)


def twice(block):
    zero = np.zeros_like(block)
    return np.block([[block, zero], [zero, block]])


def banded(count):
    distance = np.abs(np.arange(count)[:, None] - np.arange(count)[None, :])
    weights = np.zeros((count, count))
    for near in (1, 2, 3):
        weights[distance == near] = STENCIL[near]
    return weights


@functools.lru_cache(maxsize=None)
def make_tables(s0, side):
    along = cosine_basis(s0)
    cross = cosine_basis(side)
    wave = (
        ((math.pi * np.arange(s0) / s0) ** 2)[:, None, None]
        + ((math.pi * np.arange(side) / side) ** 2)[None, :, None]
        + ((math.pi * np.arange(side) / side) ** 2)[None, None, :]
    )
    rooted = np.sqrt(wave)
    safe = np.where(wave > 0.0, wave, 1.0)
    gain = np.where(
        wave > 0.0, 4.0 * np.sin(0.5 * COURANT * rooted) ** 2 / safe, COURANT * COURANT
    )
    twice_cosine = 2.0 * np.cos(COURANT * rooted)
    parity = np.arange(s0) % 2
    face = np.zeros((8, s0))
    for r in range(3):
        face[r] = along[:, r] * (parity == 0)
        face[3 + r] = along[:, r] * (parity == 1)
    face_high, face_low = halves(face)
    zero = np.zeros_like(face_low)
    collect = np.block([[face_high, face_high], [face_low, zero]])
    inject = np.concatenate([face_high.T, face_high.T, face_low.T, zero.T], axis=1)
    order = np.concatenate([np.arange(0, side, 2), np.arange(1, side, 2)])
    coupled = []
    for r in range(3):
        for s in range(r, 3):
            parts = [
                np.einsum("k,kab,k->ab", face[3 * o + r], gain, face[3 * o + s])[order] for o in (0, 1)
            ]
            coupled.append(np.concatenate(parts, axis=1))
    forward_one = np.concatenate([*([halves(cross[order])[0]] * 2), halves(cross[order])[1]], axis=1)
    inverse = cross[order].T
    inverse_one = np.concatenate([*([halves(inverse)[0]] * 2), halves(inverse)[1]], axis=1)
    forward_two = np.concatenate([*([halves(twice(cross.T))[0]] * 2), halves(twice(cross.T))[1]], axis=0)
    inverse_two = np.concatenate([*([halves(twice(cross))[0]] * 2), halves(twice(cross))[1]], axis=0)
    rate = DAMPING * ((np.arange(s0) + 0.5) / s0) ** 2
    first = (2.0 + COURANT * COURANT * 3.0 * STENCIL[0] / 180.0) / (1.0 + rate)
    second = -(1.0 - rate) / (1.0 + rate)
    third = COURANT * COURANT / (1.0 + rate)
    rows = [np.broadcast_to(v[:, None], (s0, 128)) for v in (first, second, third)]
    down = np.concatenate([banded(s0)] * 2, axis=1).astype(BF16)
    inside = np.concatenate([twice(banded(side))] * 2, axis=0).astype(BF16)
    face_third = np.stack(
        [np.concatenate([np.full(side, third[r]), np.full(side, third[s0 - 1 - r])]) for r in range(3)]
    )
    face_third = np.concatenate([face_third, np.zeros((5, 2 * side))])
    f32 = np.float32
    return {
        "cosine": twice_cosine.reshape(s0, side * side).astype(f32),
        "gain": gain.reshape(s0, side * side).astype(f32),
        "collect": collect,
        "inject": inject,
        "coupled": np.concatenate(coupled, axis=0).astype(f32),
        "forward_one": forward_one,
        "forward_two": forward_two,
        "inverse_one": inverse_one,
        "inverse_two": inverse_two,
        "rows": np.concatenate(rows, axis=0).astype(f32),
        "down": down,
        "inside": inside,
        "face_third": face_third.astype(f32),
    }


def pairing(nx, ny, parity, across):
    taken = {}
    for x in range(parity, nx - 1, 2):
        for y in range(ny):
            if 0 <= y + across < ny:
                taken[(x, y)] = (x + 1, y + across)
                taken[(x + 1, y + across)] = (x, y)
    rest = [(x, y) for x in range(nx) for y in range(ny) if (x, y) not in taken]
    while len(rest) > 1:
        x, y = rest.pop(0)
        mate = min(rest, key=lambda d: (abs(d[1] - y) + abs(d[0] // 2 - x // 2), d))
        if parity == 1 and x == 0:
            wrapped = [d for d in rest if d == (nx - 1, y - across)]
            mate = wrapped[0] if wrapped else mate
        rest.remove(mate)
        taken[(x, y)] = mate
        taken[mate] = (x, y)
    return [(x * ny + y, u * ny + v) for (x, y), (u, v) in sorted(taken.items())]


def left_lanes(shape):
    return lax.broadcasted_iota(jnp.int32, shape, len(shape) - 1) < shape[-1] // 2


def turned(block):
    return pltpu.roll(block, block.shape[-1] // 2, block.ndim - 1)


def two_halves(block):
    high = block.astype(jnp.bfloat16)
    low = (block - high.astype(jnp.float32)).astype(jnp.bfloat16)
    return high, low


def product(a, b):
    return jnp.dot(a, b, preferred_element_type=jnp.float32)


def over_rows(table, block):
    high, low = two_halves(block)
    return product(table, jnp.concatenate([high, low, high], axis=0))


def over_lanes(block, table):
    high, low = two_halves(block)
    return product(jnp.concatenate([high, low, high], axis=1), table)


def beside(planes):
    side = planes.shape[0] // 3
    return jnp.concatenate([planes[r * side : (r + 1) * side] for r in range(3)], axis=1)


def below(planes):
    wide = planes.shape[1] // 3
    return jnp.concatenate([planes[:, r * wide : (r + 1) * wide] for r in range(3)], axis=0)


def sum_difference(block):
    other = turned(block)
    return jnp.where(left_lanes(block.shape), block + other, other - block)


def mirrored_inverse(modes, inverse_one, inverse_two):
    cells = over_rows(inverse_one[...], beside(over_lanes(modes, inverse_two[...])))
    return sum_difference(below(cells))


def mirrored_forward(planes, forward_one, forward_two):
    cells = sum_difference(planes)
    return over_lanes(below(over_rows(forward_one[...], beside(cells))), forward_two[...])


def weave(first, second):
    left = left_lanes(first.shape)
    return jnp.where(left, first, turned(second)), jnp.where(left, turned(first), second)


def blended(planes):
    return [
        sum(BLEND[d][e] * planes[e] for e in range(3) if BLEND[d][e] != 0.0) for d in range(3)
    ]


def emit_payloads(layers, listed, place, outs, pads):
    side = layers.shape[0] // 3
    half = side // 2
    wide = layers.shape[1]
    left = left_lanes((half, wide))
    planes = [layers[r * side : (r + 1) * side] for r in range(3)]
    low = [jnp.where(left, p[:half], turned(p[half:])) for p in planes]
    low = jnp.concatenate(low, axis=0)
    whole = left_lanes((side, wide))
    for r, plane in enumerate(blended(planes)):
        pads[0, r, OFF : OFF + side] = jnp.where(whole, turned(plane), 0.0)
    packed = []
    for s in range(listed.shape[0]):
        start = OFF + listed[s, 3]
        roll = (wide - listed[s, 4]) % wide
        opposite = (wide + half * 2 - listed[s, 4]) % wide
        parts = []
        for r in range(3):
            top = pltpu.roll(pads[0, r, pl.ds(start, half)], roll, 1)
            bottom = pltpu.roll(pads[0, r, pl.ds(start + half, half)], opposite, 1)
            parts.append(jnp.where(left, top, bottom))
        packed.append(jnp.concatenate(parts, axis=0))
    even = place[0] == 1
    for i, g in enumerate(SHIFTS):
        force = jnp.zeros_like(low)
        for s in range(listed.shape[0]):
            wanted = (listed[s, 2] == g) & (listed[s, 5] != 0)
            force = force + jnp.where(wanted, packed[s], 0.0)
        outs[i][...] = jnp.where(even, force, low)
        outs[3 + i][...] = jnp.where(even, low, force)


def clear_pads(pads):
    side = pads.shape[2] - 2 * OFF
    blank = jnp.zeros((OFF, pads.shape[3]), jnp.float32)
    for n in range(pads.shape[0]):
        for r in range(3):
            pads[n, r, 0:OFF] = blank
            pads[n, r, OFF + side : 2 * OFF + side] = blank


def take_forces(arrived, listed, place, pads):
    wide = arrived[0].shape[1]
    half = arrived[0].shape[0] // 3
    side = 2 * half
    left = left_lanes((half, wide))
    even = place[0] == 1
    lows = [jnp.where(even, arrived[i][...], arrived[3 + i][...]) for i in range(3)]
    pushes = [jnp.where(even, arrived[3 + i][...], arrived[i][...]) for i in range(3)]
    pushed = jnp.zeros_like(lows[0])
    for i in range(3):
        pushed = pushed + jnp.where(place[1 + i] == 1, pushes[i], 0.0)
    high = [None] * 3
    for s in range(listed.shape[0]):
        g = listed[s, 2]
        chosen = jnp.where(g == 0, lows[1], jnp.where(g < 0, lows[0], lows[2]))
        chosen = jnp.where(listed[s, 5] != 0, chosen, 0.0)
        for r in range(3):
            part = chosen[r * half : (r + 1) * half]
            pads[1 + s, r, OFF : OFF + half] = jnp.where(left, part, 0.0)
            pads[1 + s, r, OFF + half : OFF + side] = jnp.where(left, turned(part), 0.0)
        start = OFF - listed[s, 3]
        roll = (listed[s, 4] + wide + side) % wide
        for r in range(3):
            moved = pltpu.roll(pads[1 + s, r, pl.ds(start, side)], roll, 1)
            high[r] = moved if high[r] is None else high[r] + moved
    high = blended(high)
    planes = []
    for r in range(3):
        part = pushed[r * half : (r + 1) * half]
        lower = jnp.concatenate([part, turned(part)], axis=0)
        planes.append(jnp.where(left_lanes((side, wide)), lower, high[r]))
    return jnp.concatenate(planes, axis=0)


def modal_response(force_modes, coupled):
    side = force_modes.shape[0] // 3
    planes = [force_modes[r * side : (r + 1) * side] for r in range(3)]
    index, n = {}, 0
    for r in range(3):
        for s in range(r, 3):
            index[r, s] = index[s, r] = n
            n += 1
    rows = []
    for r in range(3):
        total = None
        for s in range(3):
            i = index[r, s]
            term = coupled[i * side : (i + 1) * side, :] * planes[s]
            total = term if total is None else total + term
        rows.append(total)
    return jnp.concatenate(rows, axis=0)


def tile_count(ref):
    return ref.shape[1] // 128


def planes_of_modes(gathered, tiles):
    planes = []
    for r in range(3):
        planes += weave(
            gathered[r * tiles : (r + 1) * tiles, :], gathered[(3 + r) * tiles : (4 + r) * tiles, :]
        )
    return jnp.concatenate(planes, axis=0)


def collected(block, collect):
    high, low = two_halves(block)
    both = product(collect[...], jnp.concatenate([high, low], axis=0))
    return both[0:8] + both[8:16]


def scatter_tiles(rows, gathered, column):
    tiles = gathered.shape[0] // 8
    for i in range(rows.shape[1] // 128):
        gathered[pl.ds(column // 128 + i, 8, stride=tiles), :] = rows[:, i * 128 : (i + 1) * 128]


def gather_tiles(gathered, column, width):
    tiles = gathered.shape[0] // 8
    return jnp.concatenate(
        [gathered[pl.ds(column // 128 + i, 8, stride=tiles), :] for i in range(width // 128)], axis=1
    )


def pml_planes(state, gathered, woven):
    s0 = state.shape[0]
    tiles = tile_count(state)
    for start, base in ((0, 0), (s0 - 8, 8 * tiles)):
        for J in range(tiles):
            gathered[pl.ds(base + J, 8, stride=tiles), :] = state[
                start : start + 8, J * 128 : (J + 1) * 128
            ]
    for r in range(3):
        high = (8 + 7 - r) * tiles
        first, second = weave(
            gathered[r * tiles : (r + 1) * tiles, :], gathered[high : high + tiles, :]
        )
        woven[pl.ds(r * 2 * tiles, tiles, stride=2), :] = first
        woven[pl.ds(r * 2 * tiles + 1, tiles, stride=2), :] = second
    return woven[...]


def low_high_rows(planes, woven, tiles):
    woven[...] = planes
    rows = []
    for r in range(3):
        first = woven[pl.ds(r * 2 * tiles, tiles, stride=2), :]
        second = woven[pl.ds(r * 2 * tiles + 1, tiles, stride=2), :]
        rows.append(weave(first, second))
    return rows


def spread_pml_forces(planes, gathered, woven):
    tiles = gathered.shape[0] // 16
    rows = low_high_rows(planes, woven, tiles)
    blank = jnp.zeros((tiles, 128), jnp.float32)
    for s in range(8):
        gathered[s * tiles : (s + 1) * tiles, :] = rows[s][0] if s < 3 else blank
        gathered[(8 + s) * tiles : (9 + s) * tiles, :] = rows[7 - s][1] if s > 4 else blank


def spread_modal_forces(modes, gathered):
    tiles = gathered.shape[0] // 16
    side = modes.shape[0] // 3
    half = side // 2
    blank = jnp.zeros((tiles, 128), jnp.float32)
    for r in range(3):
        plane = modes[r * side : (r + 1) * side]
        even, odd = weave(plane[:half], plane[half:])
        gathered[r * tiles : (r + 1) * tiles, :] = even
        gathered[(3 + r) * tiles : (4 + r) * tiles, :] = odd
    for s in (6, 7):
        gathered[s * tiles : (s + 1) * tiles, :] = blank


def injected(gathered, inject, column, width):
    tiles = gathered.shape[0] // 16
    rows = jnp.concatenate(
        [gathered[pl.ds(column // 128 + i, 8, stride=tiles), :] for i in range(width // 128)], axis=1
    )
    high = rows.astype(jnp.bfloat16).astype(jnp.float32)
    stacked = jnp.concatenate([high, rows - high, high, jnp.zeros_like(rows)], axis=0)
    return product(inject[...], stacked.astype(jnp.bfloat16))


def pml_rows(gathered, column, width, base):
    tiles = gathered.shape[0] // 16
    return jnp.concatenate(
        [
            gathered[pl.ds(base * tiles + column // 128 + i, 8, stride=tiles), :]
            for i in range(width // 128)
        ],
        axis=1,
    )


def wide(rows, width):
    return jnp.concatenate([rows] * (width // 128), axis=1)


def stencil_sums(state, column, width, down, inside):
    total = state.shape[1]
    tiles = width // 128
    strip = state[:, column : column + width]
    high, low = two_halves(strip)
    sums = product(down[...], jnp.concatenate([high, low], axis=0))
    rows = [
        product(
            jnp.concatenate(
                [high[:, i * 128 : (i + 1) * 128], low[:, i * 128 : (i + 1) * 128]], axis=1
            ),
            inside[...],
        )
        for i in range(tiles)
    ]
    sums = sums + jnp.concatenate(rows, axis=1)

    def tile(i):
        at = column + i * 128
        if at < 0 or at >= total:
            return None
        return state[:, at : at + 128]

    near = {i: tile(i) for i in range(-2, tiles + 2)}
    spun = {i: None if v is None else turned(v) for i, v in near.items()}
    left = left_lanes((state.shape[0], 128))

    def between(i):
        a, b = spun.get(i - 1), spun.get(i)
        a = jnp.zeros(left.shape, jnp.float32) if a is None else a
        b = jnp.zeros(left.shape, jnp.float32) if b is None else b
        return jnp.where(left, a, b)

    def plus(a, b):
        return b if a is None else a if b is None else a + b

    moved = {i: between(i) for i in range(-1, tiles + 2)}
    across = [
        STENCIL[1] * (moved[i] + moved[i + 1])
        + STENCIL[2] * plus(near[i - 1], near[i + 1])
        + STENCIL[3] * (moved[i - 1] + moved[i + 2])
        for i in range(tiles)
    ]
    return sums + jnp.concatenate(across, axis=1)


def start_kernel(flag, listed, place, state, collect, inverse_one, inverse_two, *rest):
    outs, (layers, pads, gathered, woven) = rest[:6], rest[6:]
    clear_pads(pads)

    @pl.when(flag[0] > 0)
    def _():
        layers[...] = pml_planes(state, gathered, woven)

    @pl.when(flag[0] <= 0)
    def _():
        for column in range(0, state.shape[1], CHUNK):
            rows = collected(state[:, column : column + CHUNK], collect)
            scatter_tiles(rows, gathered.at[0 : 8 * tile_count(state)], column)
        modes = planes_of_modes(gathered, tile_count(state))
        layers[...] = mirrored_inverse(modes, inverse_one, inverse_two)

    emit_payloads(layers[...], listed, place, outs, pads)


def free_kernel(first, keep, flag, *refs):
    refs = list(refs)
    forces = None if first else refs.pop(0)
    current, before, cosine = refs[:3]
    refs = refs[3:]
    gain, inject = (None, None) if first else (refs.pop(0), refs.pop(0))
    collect, inverse_one, inverse_two, rows, down, inside = refs[:6]
    refs = refs[6:]
    whole = refs.pop(0) if keep else current
    free, layers, gathered, woven = refs
    s0, total = current.shape
    tiles = total // 128

    @pl.when(flag[0] > 0)
    def _():
        if keep:
            spread_pml_forces(forces[...], gathered, woven)
            for column in range(0, total, CHUNK):
                span = slice(column, column + CHUNK)
                whole[8 : s0 - 8, span] = current[8 : s0 - 8, span]
                for at, base in ((0, 0), (s0 - 8, 8)):
                    scale = wide(rows[2 * s0 + at : 2 * s0 + at + 8, :], CHUNK)
                    whole[at : at + 8, span] = current[at : at + 8, span] + scale * pml_rows(
                        gathered, column, CHUNK, base
                    )
        for column in range(0, total, CHUNK):
            span = slice(column, column + CHUNK)
            sums = stencil_sums(whole, column, CHUNK, down, inside)
            free[:, span] = (
                wide(rows[0:s0, :], CHUNK) * whole[:, span]
                + wide(rows[s0 : 2 * s0, :], CHUNK) * before[:, span]
                + wide(rows[2 * s0 : 3 * s0, :], CHUNK) * (sums * (1.0 / 180.0))
            )
        layers[...] = pml_planes(free, gathered, woven)

    @pl.when(flag[0] <= 0)
    def _():
        if keep:
            spread_modal_forces(forces[...], gathered)
        parts = []
        for column in range(0, total, CHUNK):
            span = slice(column, column + CHUNK)
            value = current[:, span]
            if keep:
                value = value + gain[:, span] * injected(gathered, inject, column, CHUNK)
                whole[:, span] = value
            value = cosine[:, span] * value - before[:, span]
            free[:, span] = value
            parts.append(collected(value, collect))
        for i, part in enumerate(parts):
            scatter_tiles(part, gathered.at[0 : 8 * tiles], i * CHUNK)
        layers[...] = mirrored_inverse(planes_of_modes(gathered, tiles), inverse_one, inverse_two)


def advance_layers(flag, listed, place, arrived, layers, tables, forces, next_layers, pads):
    coupled, forward_one, forward_two, inverse_one, inverse_two, face_third = tables
    clear_pads(pads)
    push = take_forces(arrived, listed, place, pads)
    side = push.shape[0] // 3

    @pl.when(flag[0] > 0)
    def _():
        forces[...] = push
        for r in range(3):
            span = slice(r * side, (r + 1) * side)
            next_layers[span, :] = layers[span, :] + face_third[r : r + 1, :] * push[span]

    @pl.when(flag[0] <= 0)
    def _():
        modes = mirrored_forward(push, forward_one, forward_two)
        forces[...] = modes
        answer = mirrored_inverse(modal_response(modes, coupled), inverse_one, inverse_two)
        next_layers[...] = layers[...] + answer


def force_kernel(flag, listed, place, *refs):
    arrived, layers, tables = refs[:6], refs[6], refs[7:13]
    forces, outs, (next_layers, pads) = refs[13], refs[14:20], refs[20:]
    advance_layers(flag, listed, place, arrived, layers, tables, forces, next_layers, pads)
    emit_payloads(next_layers[...], listed, place, outs, pads)


def last_kernel(flag, listed, place, *refs):
    arrived, layers, tables = refs[:6], refs[6], refs[7:13]
    free, gain, inject, rows = refs[13:17]
    state, faces, forces, next_layers, pads, gathered, woven = refs[17:]
    advance_layers(flag, listed, place, arrived, layers, tables, forces, next_layers, pads)
    s0, total = free.shape
    tiles = total // 128

    @pl.when(flag[0] > 0)
    def _():
        spread_pml_forces(forces[...], gathered, woven)
        state[8 : s0 - 8, :] = free[8 : s0 - 8, :]
        for column in range(0, total, CHUNK):
            span = slice(column, column + CHUNK)
            for at, base in ((0, 0), (s0 - 8, 8)):
                scale = wide(rows[2 * s0 + at : 2 * s0 + at + 8, :], CHUNK)
                state[at : at + 8, span] = free[at : at + 8, span] + scale * pml_rows(
                    gathered, column, CHUNK, base
                )

    @pl.when(flag[0] <= 0)
    def _():
        spread_modal_forces(forces[...], gathered)
        for column in range(0, total, CHUNK):
            span = slice(column, column + CHUNK)
            state[:, span] = free[:, span] + gain[:, span] * injected(gathered, inject, column, CHUNK)

    shown = low_high_rows(next_layers[...], woven, tiles)
    for r in range(3):
        gathered[r * tiles : (r + 1) * tiles, :] = shown[r][0]
        gathered[(3 + r) * tiles : (4 + r) * tiles, :] = shown[r][1]
    for J in range(tiles):
        faces[:, J * 128 : (J + 1) * 128] = gathered[pl.ds(J, 8, stride=tiles), :][0:6]


SCALAR = pl.BlockSpec(memory_space=pltpu.SMEM)
BLOCK = pl.BlockSpec(memory_space=pltpu.VMEM)


def run(body, scalars, blocks, outs, scratch, flops=0):
    moved = sum(b.size * b.dtype.itemsize for b in blocks)
    return pl.pallas_call(
        body,
        out_shape=[jax.ShapeDtypeStruct(s, jnp.float32) for s in outs],
        in_specs=[SCALAR] * len(scalars) + [BLOCK] * len(blocks),
        out_specs=[BLOCK] * len(outs),
        scratch_shapes=[pltpu.VMEM(s, jnp.float32) for s in scratch],
        compiler_params=pltpu.CompilerParams(vmem_limit_bytes=32 * 1024 * 1024),
        cost_estimate=pl.CostEstimate(flops=flops, bytes_accessed=moved, transcendentals=0),
    )(*scalars, *blocks)


def local(nx, ny, state_now, state_prev, pml_flags, interfaces):
    _, s0, cross = state_now.shape
    side = math.isqrt(cross)
    t = {k: jnp.asarray(v) for k, v in make_tables(s0, side).items()}
    tiles = cross // 128
    now, before = state_now[0], state_prev[0]
    gx, gy = lax.axis_index("gx"), lax.axis_index("gy")
    reach = [(gx > 0) & (gy - g >= 0) & (gy - g < ny) for g in SHIFTS]
    place = jnp.stack([gx % 2 == 0, *reach]).astype(jnp.int32)
    scalars = (pml_flags, interfaces, place)
    planes = (3 * side, 128)
    packed = (3 * side // 2, 128)
    pads = (1 + interfaces.shape[0], 3, side + 2 * OFF, 128)
    gathered = (16 * tiles, 128)
    routes = [pairing(nx, ny, parity, g) for parity in (0, 1) for g in SHIFTS]
    send_order = (5, 3, 4, 2, 0, 1)

    def exchange(payloads):
        arrived = [None] * 6
        for i in send_order:
            arrived[i] = lax.ppermute(payloads[i], ("gx", "gy"), routes[i])
        return arrived

    payloads = run(
        start_kernel,
        scalars,
        (now, t["collect"], t["inverse_one"], t["inverse_two"]),
        [packed] * 6,
        [planes, pads, gathered, planes],
    )
    tables = [
        t[k]
        for k in ("coupled", "forward_one", "forward_two", "inverse_one", "inverse_two", "face_third")
    ]
    shared = [t[k] for k in ("collect", "inverse_one", "inverse_two", "rows", "down", "inside")]
    forces = None
    current = now
    for step in range(STEPS):
        arrived = exchange(payloads)
        full = (s0, cross)
        if step == 0:
            free, layers = run(
                functools.partial(free_kernel, True, False),
                scalars[:1],
                (current, before, t["cosine"], *shared),
                [full, planes],
                [gathered, planes],
                flops=10**9,
            )
        else:
            whole, free, layers = run(
                functools.partial(free_kernel, False, True),
                scalars[:1],
                (forces, free, current, t["cosine"], t["gain"], t["inject"], *shared),
                [full, full, planes],
                [gathered, planes],
                flops=10**9,
            )
            current = whole
        if step < STEPS - 1:
            forces, *payloads = run(
                force_kernel,
                scalars,
                (*arrived, layers, *tables),
                [planes] + [packed] * 6,
                [planes, pads],
            )
        else:
            state, faces = run(
                last_kernel,
                scalars,
                (*arrived, layers, *tables, free, t["gain"], t["inject"], t["rows"]),
                [full, (6, cross)],
                [planes, planes, pads, gathered, planes],
            )
    return state[None], faces[None]


def solution(mesh):
    placed = (
        P(("gx", "gy"), None, None),
        P(("gx", "gy"), None, None),
        P(("gx", "gy")),
        P(("gx", "gy"), None),
    )
    return jax.shard_map(
        functools.partial(local, mesh.shape["gx"], mesh.shape["gy"]),
        mesh=mesh,
        in_specs=placed,
        out_specs=(P(("gx", "gy"), None, None), P(("gx", "gy"), None, None)),
        check_vma=False,
    )
```

```python
import functools
import math

import jax
import jax.numpy as jnp
import ml_dtypes
import numpy as np
from jax import lax
from jax.experimental import pallas as pl
from jax.experimental.pallas import tpu as pltpu
from jax.sharding import PartitionSpec as P

STEPS = 3
OFF = 16
COURANT = 0.4
DAMPING = 0.5
STENCIL = (-490.0, 270.0, -27.0, 2.0)
BLEND = ((1.5, -0.15, 1.0 / 90.0), (-0.15, 1.0 / 90.0, 0.0), (1.0 / 90.0, 0.0, 0.0))
SHIFTS = (-1, 0, 1)
CHUNK = 512
BF16 = ml_dtypes.bfloat16


def cosine_basis(count):
    freqs = np.arange(count)[:, None]
    cells = np.arange(count)[None, :]
    weight = np.where(freqs == 0, np.sqrt(1.0 / count), np.sqrt(2.0 / count))
    return weight * np.cos(math.pi * freqs * (cells + 0.5) / count)


def halves(values):
    high = values.astype(BF16)
    return high, (values - high.astype(np.float64)).astype(BF16)


def twice(block):
    zero = np.zeros_like(block)
    return np.block([[block, zero], [zero, block]])


def banded(count):
    distance = np.abs(np.arange(count)[:, None] - np.arange(count)[None, :])
    weights = np.zeros((count, count))
    for near in (1, 2, 3):
        weights[distance == near] = STENCIL[near]
    return weights


@functools.lru_cache(maxsize=None)
def make_tables(s0, side):
    along = cosine_basis(s0)
    cross = cosine_basis(side)
    wave = (
        ((math.pi * np.arange(s0) / s0) ** 2)[:, None, None]
        + ((math.pi * np.arange(side) / side) ** 2)[None, :, None]
        + ((math.pi * np.arange(side) / side) ** 2)[None, None, :]
    )
    rooted = np.sqrt(wave)
    safe = np.where(wave > 0.0, wave, 1.0)
    gain = np.where(
        wave > 0.0, 4.0 * np.sin(0.5 * COURANT * rooted) ** 2 / safe, COURANT * COURANT
    )
    twice_cosine = 2.0 * np.cos(COURANT * rooted)
    parity = np.arange(s0) % 2
    face = np.zeros((8, s0))
    for r in range(3):
        face[r] = along[:, r] * (parity == 0)
        face[3 + r] = along[:, r] * (parity == 1)
    face_high, face_low = halves(face)
    zero = np.zeros_like(face_low)
    collect = np.block([[face_high, face_high], [face_low, zero]])
    inject = np.concatenate([face_high.T, face_high.T, face_low.T, zero.T], axis=1)
    order = np.concatenate([np.arange(0, side, 2), np.arange(1, side, 2)])
    coupled = []
    for r in range(3):
        for s in range(r, 3):
            parts = [
                np.einsum("k,kab,k->ab", face[3 * o + r], gain, face[3 * o + s])[order] for o in (0, 1)
            ]
            coupled.append(np.concatenate(parts, axis=1))
    forward_one = np.concatenate([*([halves(cross[order])[0]] * 2), halves(cross[order])[1]], axis=1)
    inverse = cross[order].T
    inverse_one = np.concatenate([*([halves(inverse)[0]] * 2), halves(inverse)[1]], axis=1)
    forward_two = np.concatenate([*([halves(twice(cross.T))[0]] * 2), halves(twice(cross.T))[1]], axis=0)
    inverse_two = np.concatenate([*([halves(twice(cross))[0]] * 2), halves(twice(cross))[1]], axis=0)
    rate = DAMPING * ((np.arange(s0) + 0.5) / s0) ** 2
    first = (2.0 + COURANT * COURANT * 3.0 * STENCIL[0] / 180.0) / (1.0 + rate)
    second = -(1.0 - rate) / (1.0 + rate)
    third = COURANT * COURANT / (1.0 + rate)
    rows = [np.broadcast_to(v[:, None], (s0, 128)) for v in (first, second, third)]
    down = np.concatenate([banded(s0)] * 2, axis=1).astype(BF16)
    inside = np.concatenate([twice(banded(side))] * 2, axis=0).astype(BF16)
    face_third = np.stack(
        [np.concatenate([np.full(side, third[r]), np.full(side, third[s0 - 1 - r])]) for r in range(3)]
    )
    face_third = np.concatenate([face_third, np.zeros((5, 2 * side))])
    f32 = np.float32
    return {
        "cosine": twice_cosine.reshape(s0, side * side).astype(f32),
        "gain": gain.reshape(s0, side * side).astype(f32),
        "collect": collect,
        "inject": inject,
        "coupled": np.concatenate(coupled, axis=0).astype(f32),
        "forward_one": forward_one,
        "forward_two": forward_two,
        "inverse_one": inverse_one,
        "inverse_two": inverse_two,
        "rows": np.concatenate(rows, axis=0).astype(f32),
        "down": down,
        "inside": inside,
        "face_third": face_third.astype(f32),
    }


def pairing(nx, ny, parity, across):
    taken = {}
    for x in range(parity, nx - 1, 2):
        for y in range(ny):
            if 0 <= y + across < ny:
                taken[(x, y)] = (x + 1, y + across)
                taken[(x + 1, y + across)] = (x, y)
    rest = [(x, y) for x in range(nx) for y in range(ny) if (x, y) not in taken]
    while len(rest) > 1:
        x, y = rest.pop(0)
        mate = min(rest, key=lambda d: (abs(d[1] - y) + abs(d[0] // 2 - x // 2), d))
        if parity == 1 and x == 0:
            wrapped = [d for d in rest if d == (nx - 1, y - across)]
            mate = wrapped[0] if wrapped else mate
        rest.remove(mate)
        taken[(x, y)] = mate
        taken[mate] = (x, y)
    return [(x * ny + y, u * ny + v) for (x, y), (u, v) in sorted(taken.items())]


def noted(card):
    bits = card[1][0]
    return card[0][0] > 0, bits & 1 == 1, [bits & (2 << i) != 0 for i in range(len(SHIFTS))]


def position(shape, along, across):
    bits = 1 - along % 2
    for i, g in enumerate(SHIFTS):
        met = (along > 0) & (across - g >= 0) & (across - g < shape[1])
        bits = bits + jnp.where(met, 2 << i, 0)
    return bits


def folded(step, one, two, live):
    return (step + 1) + ((one + OFF) << 2) + ((two + OFF) << 8) + (jnp.where(live, 1, 0) << 14)


def joints(rows_folded, count):
    rows = []
    for n in range(count):
        bits = rows_folded[n, 0]
        rows.append(
            (
                (bits & 3) - 1,
                ((bits >> 2) & 63) - OFF,
                ((bits >> 8) & 63) - OFF,
                (bits >> 14) & 1 == 1,
            )
        )
    return rows


def left_lanes(shape):
    return lax.broadcasted_iota(jnp.int32, shape, len(shape) - 1) < shape[-1] // 2


def turned(block):
    return pltpu.roll(block, block.shape[-1] // 2, block.ndim - 1)


def two_halves(block):
    high = block.astype(jnp.bfloat16)
    low = (block - high.astype(jnp.float32)).astype(jnp.bfloat16)
    return high, low


def product(a, b):
    return jnp.dot(a, b, preferred_element_type=jnp.float32)


def over_rows(table, block):
    high, low = two_halves(block)
    return product(table, jnp.concatenate([high, low, high], axis=0))


def over_lanes(block, table):
    high, low = two_halves(block)
    return product(jnp.concatenate([high, low, high], axis=1), table)


def beside(planes):
    side = planes.shape[0] // 3
    return jnp.concatenate([planes[r * side : (r + 1) * side] for r in range(3)], axis=1)


def below(planes):
    wide = planes.shape[1] // 3
    return jnp.concatenate([planes[:, r * wide : (r + 1) * wide] for r in range(3)], axis=0)


def sum_difference(block):
    other = turned(block)
    return jnp.where(left_lanes(block.shape), block + other, other - block)


def mirrored_inverse(modes, inverse_one, inverse_two):
    cells = over_rows(inverse_one[...], beside(over_lanes(modes, inverse_two[...])))
    return sum_difference(below(cells))


def mirrored_forward(planes, forward_one, forward_two):
    cells = sum_difference(planes)
    return over_lanes(below(over_rows(forward_one[...], beside(cells))), forward_two[...])


def weave(first, second):
    left = left_lanes(first.shape)
    return jnp.where(left, first, turned(second)), jnp.where(left, turned(first), second)


def blended(planes):
    return [
        sum(BLEND[d][e] * planes[e] for e in range(3) if BLEND[d][e] != 0.0) for d in range(3)
    ]


def emit_payloads(layers, even, listed, outs, pads):
    side = layers.shape[0] // 3
    half = side // 2
    wide = layers.shape[1]
    left = left_lanes((half, wide))
    planes = [layers[r * side : (r + 1) * side] for r in range(3)]
    low = [jnp.where(left, p[:half], turned(p[half:])) for p in planes]
    low = jnp.concatenate(low, axis=0)
    whole = left_lanes((side, wide))
    for r, plane in enumerate(blended(planes)):
        pads[0, r, OFF : OFF + side] = jnp.where(whole, turned(plane), 0.0)
    packed = []
    for _, one, two, _ in listed:
        start = OFF + one
        roll = (wide - two) % wide
        opposite = (wide + side - two) % wide
        parts = []
        for r in range(3):
            top = pltpu.roll(pads[0, r, pl.ds(start, half)], roll, 1)
            bottom = pltpu.roll(pads[0, r, pl.ds(start + half, half)], opposite, 1)
            parts.append(jnp.where(left, top, bottom))
        packed.append(jnp.concatenate(parts, axis=0))
    for i, g in enumerate(SHIFTS):
        force = jnp.zeros_like(low)
        for part, (step, _, _, live) in zip(packed, listed):
            force = force + jnp.where((step == g) & live, part, 0.0)
        outs[i][...] = jnp.where(even, force, low)
        outs[3 + i][...] = jnp.where(even, low, force)


def clear_pads(pads):
    side = pads.shape[2] - 2 * OFF
    blank = jnp.zeros((OFF, pads.shape[3]), jnp.float32)
    for n in range(pads.shape[0]):
        for r in range(3):
            pads[n, r, 0:OFF] = blank
            pads[n, r, OFF + side : 2 * OFF + side] = blank


def take_forces(arrived, even, met, listed, pads):
    wide = arrived[0].shape[1]
    half = arrived[0].shape[0] // 3
    side = 2 * half
    left = left_lanes((half, wide))
    lows = [jnp.where(even, arrived[i][...], arrived[3 + i][...]) for i in range(3)]
    pushes = [jnp.where(even, arrived[3 + i][...], arrived[i][...]) for i in range(3)]
    pushed = jnp.zeros_like(lows[0])
    for i in range(3):
        pushed = pushed + jnp.where(met[i], pushes[i], 0.0)
    high = [None] * 3
    for s, (g, one, two, live) in enumerate(listed):
        chosen = jnp.where(g == 0, lows[1], jnp.where(g < 0, lows[0], lows[2]))
        chosen = jnp.where(live, chosen, 0.0)
        for r in range(3):
            part = chosen[r * half : (r + 1) * half]
            pads[1 + s, r, OFF : OFF + half] = jnp.where(left, part, 0.0)
            pads[1 + s, r, OFF + half : OFF + side] = jnp.where(left, turned(part), 0.0)
        start = OFF - one
        roll = (two + wide + side) % wide
        for r in range(3):
            moved = pltpu.roll(pads[1 + s, r, pl.ds(start, side)], roll, 1)
            high[r] = moved if high[r] is None else high[r] + moved
    high = blended(high)
    planes = []
    for r in range(3):
        part = pushed[r * half : (r + 1) * half]
        lower = jnp.concatenate([part, turned(part)], axis=0)
        planes.append(jnp.where(left_lanes((side, wide)), lower, high[r]))
    return jnp.concatenate(planes, axis=0)


def modal_response(force_modes, coupled):
    side = force_modes.shape[0] // 3
    planes = [force_modes[r * side : (r + 1) * side] for r in range(3)]
    index, n = {}, 0
    for r in range(3):
        for s in range(r, 3):
            index[r, s] = index[s, r] = n
            n += 1
    rows = []
    for r in range(3):
        total = None
        for s in range(3):
            i = index[r, s]
            term = coupled[i * side : (i + 1) * side, :] * planes[s]
            total = term if total is None else total + term
        rows.append(total)
    return jnp.concatenate(rows, axis=0)


def tile_count(ref):
    return ref.shape[1] // 128


def planes_of_modes(gathered, tiles):
    planes = []
    for r in range(3):
        planes += weave(
            gathered[r * tiles : (r + 1) * tiles, :], gathered[(3 + r) * tiles : (4 + r) * tiles, :]
        )
    return jnp.concatenate(planes, axis=0)


def collected(block, collect):
    high, low = two_halves(block)
    both = product(collect[...], jnp.concatenate([high, low], axis=0))
    return both[0:8] + both[8:16]


def scatter_tiles(rows, gathered, column):
    tiles = gathered.shape[0] // 8
    for i in range(rows.shape[1] // 128):
        gathered[pl.ds(column // 128 + i, 8, stride=tiles), :] = rows[:, i * 128 : (i + 1) * 128]


def gather_tiles(gathered, column, width):
    tiles = gathered.shape[0] // 8
    return jnp.concatenate(
        [gathered[pl.ds(column // 128 + i, 8, stride=tiles), :] for i in range(width // 128)], axis=1
    )


def pml_planes(state, gathered, woven):
    s0 = state.shape[0]
    tiles = tile_count(state)
    for start, base in ((0, 0), (s0 - 8, 8 * tiles)):
        for J in range(tiles):
            gathered[pl.ds(base + J, 8, stride=tiles), :] = state[
                start : start + 8, J * 128 : (J + 1) * 128
            ]
    for r in range(3):
        high = (8 + 7 - r) * tiles
        first, second = weave(
            gathered[r * tiles : (r + 1) * tiles, :], gathered[high : high + tiles, :]
        )
        woven[pl.ds(r * 2 * tiles, tiles, stride=2), :] = first
        woven[pl.ds(r * 2 * tiles + 1, tiles, stride=2), :] = second
    return woven[...]


def low_high_rows(planes, woven, tiles):
    woven[...] = planes
    rows = []
    for r in range(3):
        first = woven[pl.ds(r * 2 * tiles, tiles, stride=2), :]
        second = woven[pl.ds(r * 2 * tiles + 1, tiles, stride=2), :]
        rows.append(weave(first, second))
    return rows


def spread_pml_forces(planes, gathered, woven):
    tiles = gathered.shape[0] // 16
    rows = low_high_rows(planes, woven, tiles)
    blank = jnp.zeros((tiles, 128), jnp.float32)
    for s in range(8):
        gathered[s * tiles : (s + 1) * tiles, :] = rows[s][0] if s < 3 else blank
        gathered[(8 + s) * tiles : (9 + s) * tiles, :] = rows[7 - s][1] if s > 4 else blank


def spread_modal_forces(modes, gathered):
    tiles = gathered.shape[0] // 16
    side = modes.shape[0] // 3
    half = side // 2
    blank = jnp.zeros((tiles, 128), jnp.float32)
    for r in range(3):
        plane = modes[r * side : (r + 1) * side]
        even, odd = weave(plane[:half], plane[half:])
        gathered[r * tiles : (r + 1) * tiles, :] = even
        gathered[(3 + r) * tiles : (4 + r) * tiles, :] = odd
    for s in (6, 7):
        gathered[s * tiles : (s + 1) * tiles, :] = blank


def injected(gathered, inject, column, width):
    tiles = gathered.shape[0] // 16
    rows = jnp.concatenate(
        [gathered[pl.ds(column // 128 + i, 8, stride=tiles), :] for i in range(width // 128)], axis=1
    )
    high = rows.astype(jnp.bfloat16).astype(jnp.float32)
    stacked = jnp.concatenate([high, rows - high, high, jnp.zeros_like(rows)], axis=0)
    return product(inject[...], stacked.astype(jnp.bfloat16))


def pml_rows(gathered, column, width, base):
    tiles = gathered.shape[0] // 16
    return jnp.concatenate(
        [
            gathered[pl.ds(base * tiles + column // 128 + i, 8, stride=tiles), :]
            for i in range(width // 128)
        ],
        axis=1,
    )


def wide(rows, width):
    return jnp.concatenate([rows] * (width // 128), axis=1)


def stencil_sums(state, column, width, down, inside):
    total = state.shape[1]
    tiles = width // 128
    strip = state[:, column : column + width]
    high, low = two_halves(strip)
    sums = product(down[...], jnp.concatenate([high, low], axis=0))
    rows = [
        product(
            jnp.concatenate(
                [high[:, i * 128 : (i + 1) * 128], low[:, i * 128 : (i + 1) * 128]], axis=1
            ),
            inside[...],
        )
        for i in range(tiles)
    ]
    sums = sums + jnp.concatenate(rows, axis=1)

    def tile(i):
        at = column + i * 128
        if at < 0 or at >= total:
            return None
        return state[:, at : at + 128]

    near = {i: tile(i) for i in range(-2, tiles + 2)}
    spun = {i: None if v is None else turned(v) for i, v in near.items()}
    left = left_lanes((state.shape[0], 128))

    def between(i):
        a, b = spun.get(i - 1), spun.get(i)
        a = jnp.zeros(left.shape, jnp.float32) if a is None else a
        b = jnp.zeros(left.shape, jnp.float32) if b is None else b
        return jnp.where(left, a, b)

    def plus(a, b):
        return b if a is None else a if b is None else a + b

    moved = {i: between(i) for i in range(-1, tiles + 2)}
    across = [
        STENCIL[1] * (moved[i] + moved[i + 1])
        + STENCIL[2] * plus(near[i - 1], near[i + 1])
        + STENCIL[3] * (moved[i - 1] + moved[i + 2])
        for i in range(tiles)
    ]
    return sums + jnp.concatenate(across, axis=1)


def copies(pairs, sems, first=0):
    return [
        pltpu.make_async_copy(source, target, sems.at[first + i])
        for i, (source, target) in enumerate(pairs)
    ]


def strips(ref, width=CHUNK):
    return [slice(column, column + width) for column in range(0, ref.shape[-1], width)]


def start_kernel(flags, place, listed, now, before, cosine, *refs):
    sources, outs, folds, refs = refs[:3], refs[3:9], refs[9], refs[10:]
    held, prior, factor, layers, pads, gathered, woven, rows, sems = refs[:9]
    collect, inverse_one, inverse_two = refs[9:]
    s0, total = held.shape
    tiles = total // 128
    spans = strips(held, 2 * CHUNK)
    first = copies([(listed, rows)], sems)
    tables = copies(zip(sources, (collect, inverse_one, inverse_two)), sems, 1)
    moves = copies([(now.at[0, :, p], held.at[:, p]) for p in spans], sems, 4)
    past = copies([(before.at[0], prior)], sems, 4 + len(spans))[0]
    more = copies([(cosine, factor)], sems, 5 + len(spans))[0]
    for m in tables[:1] + moves + tables[1:] + first:
        m.start()
    clear_pads(pads)
    for m in moves[: len(moves) // 2]:
        m.wait()
    past.start()
    _, even, _ = noted((flags, place))
    first[0].wait()
    entries = []
    for n in range(listed.shape[0]):
        entries.append((rows[n, 2], rows[n, 3], rows[n, 4], rows[n, 5] != 0))
        folds[n : n + 1, :] = jnp.full((1, 128), folded(*entries[n]), jnp.int32)

    for m in tables:
        m.wait()

    @pl.when(flags[0] > 0)
    def _():
        for m in moves[len(moves) // 2 :]:
            m.wait()
        layers[...] = pml_planes(held, gathered, woven)

    @pl.when(flags[0] <= 0)
    def _():
        more.start()
        for i, p in enumerate(spans):
            if i >= len(moves) // 2:
                moves[i].wait()
            scatter_tiles(collected(held[:, p], collect), gathered.at[0 : 8 * tiles], p.start)
        modes = planes_of_modes(gathered, tiles)
        layers[...] = mirrored_inverse(modes, inverse_one, inverse_two)

    emit_payloads(layers[...], even, entries, outs, pads)

    past.wait()

    @pl.when(flags[0] <= 0)
    def _():
        more.wait()


def free_kernel(pushed, flag, *refs):
    if pushed:
        forces, _, before, cosine, gain, inject = refs[:6]
        refs = refs[6:]
        collect, inverse_one, inverse_two, rows, down, inside, whole = refs[:7]
    else:
        whole, before, cosine, collect, inverse_one, inverse_two, rows = refs[:7]
        down, inside = refs[7:9]
        refs = refs[2:]
    free, layers, gathered, woven = refs[7:]
    s0, total = free.shape
    tiles = total // 128

    @pl.when(flag[0] > 0)
    def _():
        if pushed:
            spread_pml_forces(forces[...], gathered, woven)
        for p in strips(free) if pushed else ():
            for at, base in ((0, 0), (s0 - 8, 8)):
                scale = wide(rows[2 * s0 + at : 2 * s0 + at + 8, :], CHUNK)
                whole[at : at + 8, p] = whole[at : at + 8, p] + scale * pml_rows(
                    gathered, p.start, CHUNK, base
                )
        for p in strips(free):
            sums = stencil_sums(whole, p.start, CHUNK, down, inside)
            free[:, p] = (
                wide(rows[0:s0, :], CHUNK) * whole[:, p]
                + wide(rows[s0 : 2 * s0, :], CHUNK) * before[:, p]
                + wide(rows[2 * s0 : 3 * s0, :], CHUNK) * (sums * (1.0 / 180.0))
            )
        layers[...] = pml_planes(free, gathered, woven)

    @pl.when(flag[0] <= 0)
    def _():
        if pushed:
            spread_modal_forces(forces[...], gathered)
        parts = []
        for p in strips(free):
            value = whole[:, p]
            if pushed:
                value = value + gain[:, p] * injected(gathered, inject, p.start, CHUNK)
                whole[:, p] = value
            value = cosine[:, p] * value - before[:, p]
            free[:, p] = value
            parts.append(collected(value, collect))
        for i, part in enumerate(parts):
            scatter_tiles(part, gathered.at[0 : 8 * tiles], i * CHUNK)
        layers[...] = mirrored_inverse(planes_of_modes(gathered, tiles), inverse_one, inverse_two)


def face_forces(card, folds, arrived, tables, forces, pads):
    clear_pads(pads)
    _, even, met = noted(card)
    push = take_forces(arrived, even, met, joints(folds, pads.shape[0] - 1), pads)

    @pl.when(noted(card)[0])
    def _():
        forces[...] = push

    @pl.when(jnp.logical_not(noted(card)[0]))
    def _():
        forces[...] = mirrored_forward(push, tables[1], tables[2])


def advance_layers(card, layers, tables, forces, next_layers):
    coupled, _, _, inverse_one, inverse_two, face_third = tables
    side = layers.shape[0] // 3

    @pl.when(noted(card)[0])
    def _():
        for r in range(3):
            span = slice(r * side, (r + 1) * side)
            next_layers[span, :] = layers[span, :] + face_third[r : r + 1, :] * forces[span, :]

    @pl.when(jnp.logical_not(noted(card)[0]))
    def _():
        answer = mirrored_inverse(modal_response(forces[...], coupled), inverse_one, inverse_two)
        next_layers[...] = layers[...] + answer


def force_kernel(*refs):
    card, folds, refs = refs[:2], refs[2], refs[3:]
    arrived, layers, tables = refs[:6], refs[6], refs[7:13]
    forces, outs, (next_layers, pads) = refs[13], refs[14:20], refs[20:]
    face_forces(card, folds, arrived, tables, forces, pads)
    advance_layers(card, layers, tables, forces, next_layers)
    listed = joints(folds, pads.shape[0] - 1)
    emit_payloads(next_layers[...], noted(card)[1], listed, outs, pads)


def last_kernel(*refs):
    card, folds, refs = refs[:2], refs[2], refs[3:]
    arrived, layers, tables = refs[:6], refs[6], refs[7:13]
    free, gain, inject, rows = refs[13:17]
    state, faces, forces, next_layers, pads, gathered, woven, held, sems = refs[17:]
    s0, total = free.shape
    tiles = total // 128
    spans = strips(free)
    middle = slice(8, s0 - 8)
    ends = ((0, 0), (s0 - 8, 8))
    inner = copies([(free.at[middle], state.at[0, middle])], sems)
    outer = copies(
        [(held.at[at : at + 8], state.at[0, at : at + 8]) for at, _ in ends], sems, 1
    )
    moves = copies([(held.at[:, p], state.at[0, :, p]) for p in spans], sems)

    @pl.when(noted(card)[0])
    def _():
        inner[0].start()

    face_forces(card, folds, arrived, tables, forces, pads)

    @pl.when(noted(card)[0])
    def _():
        spread_pml_forces(forces[...], gathered, woven)
        for p in spans:
            for at, base in ends:
                scale = wide(rows[2 * s0 + at : 2 * s0 + at + 8, :], CHUNK)
                held[at : at + 8, p] = free[at : at + 8, p] + scale * pml_rows(
                    gathered, p.start, CHUNK, base
                )
        for m in outer:
            m.start()

    @pl.when(jnp.logical_not(noted(card)[0]))
    def _():
        spread_modal_forces(forces[...], gathered)
        for m, p in zip(moves, spans):
            held[:, p] = free[:, p] + gain[:, p] * injected(gathered, inject, p.start, CHUNK)
            m.start()

    advance_layers(card, layers, tables, forces, next_layers)
    shown = low_high_rows(next_layers[...], woven, tiles)
    for r in range(3):
        gathered[r * tiles : (r + 1) * tiles, :] = shown[r][0]
        gathered[(3 + r) * tiles : (4 + r) * tiles, :] = shown[r][1]
    last = pltpu.make_async_copy(gathered.at[0 : 6 * tiles], faces, sems.at[len(spans)])
    last.start()

    @pl.when(noted(card)[0])
    def _():
        for m in inner + outer:
            m.wait()

    @pl.when(jnp.logical_not(noted(card)[0]))
    def _():
        for m in moves:
            m.wait()

    last.wait()


SCALAR = pl.BlockSpec(memory_space=pltpu.SMEM)
BLOCK = pl.BlockSpec(memory_space=pltpu.VMEM)
FAR = pl.BlockSpec(memory_space=pltpu.HBM)


def run(body, blocks, outs, scratch, near=(), far=(), far_outs=(), aliases=None, flops=0):
    moved = sum(b.size * b.dtype.itemsize for b in blocks)
    blocks = [
        pltpu.with_memory_space_constraint(b, pltpu.HBM) if i in far else b
        for i, b in enumerate(blocks)
    ]
    spots = {**dict.fromkeys(far, FAR), **dict.fromkeys(near, SCALAR)}
    return pl.pallas_call(
        body,
        out_shape=[
            jax.ShapeDtypeStruct(s, jnp.float32) if isinstance(s, tuple) else s for s in outs
        ],
        in_specs=[spots.get(i, BLOCK) for i in range(len(blocks))],
        out_specs=[
            FAR if i in far_outs else BLOCK
            for i, s in enumerate(outs)
        ],
        scratch_shapes=[
            pltpu.VMEM(s, jnp.float32) if isinstance(s, tuple) else s for s in scratch
        ],
        input_output_aliases=aliases or {},
        compiler_params=pltpu.CompilerParams(vmem_limit_bytes=32 * 1024 * 1024),
        cost_estimate=pl.CostEstimate(flops=flops, bytes_accessed=moved, transcendentals=0),
    )(*blocks)


def local(nx, ny, state_now, state_prev, pml_flags, interfaces):
    _, s0, cross = state_now.shape
    side = math.isqrt(cross)
    t = {k: jnp.asarray(v) for k, v in make_tables(s0, side).items()}
    tiles = cross // 128
    planes = (3 * side, 128)
    packed = (3 * side // 2, 128)
    pads = (1 + interfaces.shape[0], 3, side + 2 * OFF, 128)
    gathered = (16 * tiles, 128)
    full = (s0, cross)
    count = cross // CHUNK
    place = position((nx, ny), lax.axis_index("gx"), lax.axis_index("gy")).reshape(1)
    card = (pml_flags, place)
    routes = [pairing(nx, ny, parity, g) for parity in (0, 1) for g in SHIFTS]

    def exchange(payloads):
        return [lax.ppermute(payloads[i], ("gx", "gy"), routes[i]) for i in range(6)]

    result = run(
        start_kernel,
        (
            *(pml_flags, place, interfaces, state_now, state_prev, t["cosine"]),
            *(t["collect"], t["inverse_one"], t["inverse_two"]),
        ),
        [packed] * 6 + [jax.ShapeDtypeStruct((8, 128), jnp.int32)] + [full] * 3,
        [
            *(planes, pads, gathered, planes),
            pltpu.SMEM(interfaces.shape, jnp.int32),
            pltpu.SemaphoreType.DMA((9 + count,)),
            *(pltpu.VMEM(t[k].shape, t[k].dtype) for k in ("collect", "inverse_one", "inverse_two")),
        ],
        near=(0, 1),
        far=range(2, 9),
    )
    payloads, (folds, now, before, cosine) = result[:6], result[6:]
    names = ("coupled", "forward_one", "forward_two", "inverse_one", "inverse_two", "face_third")
    tables = [t[k] for k in names]
    shared = [t[k] for k in ("collect", "inverse_one", "inverse_two", "rows", "down", "inside")]
    for step in range(STEPS):
        arrived = exchange(payloads)
        if step == 0:
            free, layers = run(
                functools.partial(free_kernel, False),
                (pml_flags, now, before, cosine, *shared),
                [full, planes],
                [gathered, planes],
                near=(0,),
                flops=10**9,
            )
        else:
            now, free, layers = run(
                functools.partial(free_kernel, True),
                (pml_flags, forces, free, now, cosine, t["gain"], t["inject"], *shared),
                [full, full, planes],
                [gathered, planes],
                near=(0,),
                aliases={2: 0},
                flops=10**9,
            )
        if step < STEPS - 1:
            forces, *payloads = run(
                force_kernel,
                (*card, folds, *arrived, layers, *tables),
                [planes] + [packed] * 6,
                [planes, pads],
                near=(0, 1),
            )
    state, faces = run(
        last_kernel,
        (*card, folds, *arrived, layers, *tables, free, t["gain"], t["inject"], t["rows"]),
        [(1, s0, cross), (6 * tiles, 128)],
        [*(planes, planes, pads, gathered, planes, full), pltpu.SemaphoreType.DMA((3 + count,))],
        near=(0, 1),
        far_outs=(0, 1),
    )
    return state, faces.reshape(1, 6, cross)


def solution(mesh):
    placed = (
        P(("gx", "gy"), None, None),
        P(("gx", "gy"), None, None),
        P(("gx", "gy")),
        P(("gx", "gy"), None),
    )
    return jax.shard_map(
        functools.partial(local, mesh.shape["gx"], mesh.shape["gy"]),
        mesh=mesh,
        in_specs=placed,
        out_specs=(P(("gx", "gy"), None, None), P(("gx", "gy"), None, None)),
        check_vma=False,
    )
```

```python
import functools
import math

import jax
import jax.numpy as jnp
import ml_dtypes
import numpy as np
from jax import lax
from jax.experimental import pallas as pl
from jax.experimental.pallas import tpu as pltpu
from jax.sharding import PartitionSpec as P

STEPS = 3
OFF = 16
COURANT = 0.4
DAMPING = 0.5
STENCIL = (-490.0, 270.0, -27.0, 2.0)
BLEND = ((1.5, -0.15, 1.0 / 90.0), (-0.15, 1.0 / 90.0, 0.0), (1.0 / 90.0, 0.0, 0.0))
SHIFTS = (-1, 0, 1)
ORDER = (1, 5, 0, 3, 4, 2)
CHUNK = 512
BF16 = ml_dtypes.bfloat16


def cosine_basis(count):
    freqs = np.arange(count)[:, None]
    cells = np.arange(count)[None, :]
    weight = np.where(freqs == 0, np.sqrt(1.0 / count), np.sqrt(2.0 / count))
    return weight * np.cos(math.pi * freqs * (cells + 0.5) / count)


def halves(values):
    high = values.astype(BF16)
    return high, (values - high.astype(np.float64)).astype(BF16)


def twice(block):
    zero = np.zeros_like(block)
    return np.block([[block, zero], [zero, block]])


def banded(count):
    distance = np.abs(np.arange(count)[:, None] - np.arange(count)[None, :])
    weights = np.zeros((count, count))
    for near in (1, 2, 3):
        weights[distance == near] = STENCIL[near]
    return weights


@functools.lru_cache(maxsize=None)
def make_tables(s0, side):
    along = cosine_basis(s0)
    cross = cosine_basis(side)
    wave = (
        ((math.pi * np.arange(s0) / s0) ** 2)[:, None, None]
        + ((math.pi * np.arange(side) / side) ** 2)[None, :, None]
        + ((math.pi * np.arange(side) / side) ** 2)[None, None, :]
    )
    rooted = np.sqrt(wave)
    safe = np.where(wave > 0.0, wave, 1.0)
    gain = np.where(
        wave > 0.0, 4.0 * np.sin(0.5 * COURANT * rooted) ** 2 / safe, COURANT * COURANT
    )
    twice_cosine = 2.0 * np.cos(COURANT * rooted)
    parity = np.arange(s0) % 2
    face = np.zeros((8, s0))
    for r in range(3):
        face[r] = along[:, r] * (parity == 0)
        face[3 + r] = along[:, r] * (parity == 1)
    face_high, face_low = halves(face)
    zero = np.zeros_like(face_low)
    collect = np.block([[face_high, face_high], [face_low, zero]])
    inject = np.concatenate([face_high.T, face_high.T, face_low.T, zero.T], axis=1)
    order = np.concatenate([np.arange(0, side, 2), np.arange(1, side, 2)])
    coupled = []
    for r in range(3):
        for s in range(r, 3):
            parts = [
                np.einsum("k,kab,k->ab", face[3 * o + r], gain, face[3 * o + s])[order] for o in (0, 1)
            ]
            coupled.append(np.concatenate(parts, axis=1))
    forward_one = np.concatenate([*([halves(cross[order])[0]] * 2), halves(cross[order])[1]], axis=1)
    inverse = cross[order].T
    inverse_one = np.concatenate([*([halves(inverse)[0]] * 2), halves(inverse)[1]], axis=1)
    forward_two = np.concatenate([*([halves(twice(cross.T))[0]] * 2), halves(twice(cross.T))[1]], axis=0)
    inverse_two = np.concatenate([*([halves(twice(cross))[0]] * 2), halves(twice(cross))[1]], axis=0)
    rate = DAMPING * ((np.arange(s0) + 0.5) / s0) ** 2
    first = (2.0 + COURANT * COURANT * 3.0 * STENCIL[0] / 180.0) / (1.0 + rate)
    second = -(1.0 - rate) / (1.0 + rate)
    third = COURANT * COURANT / (1.0 + rate)
    rows = [np.broadcast_to(v[:, None], (s0, 128)) for v in (first, second, third / 180.0)]
    ends = np.concatenate([third[:8], third[-8:]])
    down = np.concatenate([banded(s0)] * 2, axis=1).astype(BF16)
    inside = np.concatenate([twice(banded(side))] * 2, axis=0).astype(BF16)
    face_third = np.stack(
        [np.concatenate([np.full(side, third[r]), np.full(side, third[s0 - 1 - r])]) for r in range(3)]
    )
    face_third = np.concatenate([face_third, np.zeros((5, 2 * side))])
    f32 = np.float32
    return {
        "cosine": twice_cosine.reshape(s0, side * side).astype(f32),
        "gain": gain.reshape(s0, side * side).astype(f32),
        "collect": collect,
        "inject": inject,
        "coupled": np.concatenate(coupled, axis=0).astype(f32),
        "forward_one": forward_one,
        "forward_two": forward_two,
        "inverse_one": inverse_one,
        "inverse_two": inverse_two,
        "rows": np.concatenate(rows, axis=0).astype(f32),
        "ends": np.broadcast_to(ends[:, None], (16, 128)).astype(f32),
        "down": down,
        "inside": inside,
        "face_third": face_third.astype(f32),
    }


def pairing(nx, ny, parity, across):
    taken = {}
    for x in range(parity, nx - 1, 2):
        for y in range(ny):
            if 0 <= y + across < ny:
                taken[(x, y)] = (x + 1, y + across)
                taken[(x + 1, y + across)] = (x, y)
    rest = [(x, y) for x in range(nx) for y in range(ny) if (x, y) not in taken]
    while len(rest) > 1:
        x, y = rest.pop(0)
        mate = min(rest, key=lambda d: (abs(d[1] - y) + abs(d[0] // 2 - x // 2), d))
        if parity == 1 and x == 0:
            wrapped = [d for d in rest if d == (nx - 1, y - across)]
            mate = wrapped[0] if wrapped else mate
        rest.remove(mate)
        taken[(x, y)] = mate
        taken[mate] = (x, y)
    return [(x * ny + y, u * ny + v) for (x, y), (u, v) in sorted(taken.items())]


def noted(card):
    bits = card[1][0]
    return card[0][0] > 0, bits & 1 == 1, [bits & (2 << i) != 0 for i in range(len(SHIFTS))]


def position(shape, along, across):
    bits = 1 - along % 2
    for i, g in enumerate(SHIFTS):
        met = (along > 0) & (across - g >= 0) & (across - g < shape[1])
        bits = bits + jnp.where(met, 2 << i, 0)
    return bits


def folded(step, one, two, live):
    return (step + 1) + ((one + OFF) << 2) + ((two + OFF) << 8) + (jnp.where(live, 1, 0) << 14)


def joints(rows_folded, count):
    rows = []
    for n in range(count):
        bits = rows_folded[n, 0]
        rows.append(
            (
                (bits & 3) - 1,
                ((bits >> 2) & 63) - OFF,
                ((bits >> 8) & 63) - OFF,
                (bits >> 14) & 1 == 1,
            )
        )
    return rows


def in_turn(refs):
    return [refs[ORDER.index(i)] for i in range(len(ORDER))]


def left_lanes(shape):
    return lax.broadcasted_iota(jnp.int32, shape, len(shape) - 1) < shape[-1] // 2


def turned(block):
    return pltpu.roll(block, block.shape[-1] // 2, block.ndim - 1)


def two_halves(block):
    high = block.astype(jnp.bfloat16)
    low = (block - high.astype(jnp.float32)).astype(jnp.bfloat16)
    return high, low


def product(a, b):
    return jnp.dot(a, b, preferred_element_type=jnp.float32)


def over_rows(table, block):
    high, low = two_halves(block)
    return product(table, jnp.concatenate([high, low, high], axis=0))


def over_lanes(block, table):
    high, low = two_halves(block)
    return product(jnp.concatenate([high, low, high], axis=1), table)


def beside(planes):
    side = planes.shape[0] // 3
    return jnp.concatenate([planes[r * side : (r + 1) * side] for r in range(3)], axis=1)


def below(planes):
    wide = planes.shape[1] // 3
    return jnp.concatenate([planes[:, r * wide : (r + 1) * wide] for r in range(3)], axis=0)


def sum_difference(block):
    other = turned(block)
    return jnp.where(left_lanes(block.shape), block + other, other - block)


def mirrored_inverse(modes, inverse_one, inverse_two):
    cells = over_rows(inverse_one[...], beside(over_lanes(modes, inverse_two[...])))
    return sum_difference(below(cells))


def mirrored_forward(planes, forward_one, forward_two):
    cells = sum_difference(planes)
    return over_lanes(below(over_rows(forward_one[...], beside(cells))), forward_two[...])


def weave(first, second):
    left = left_lanes(first.shape)
    return jnp.where(left, first, turned(second)), jnp.where(left, turned(first), second)


def blended(planes):
    return [
        sum(BLEND[d][e] * planes[e] for e in range(3) if BLEND[d][e] != 0.0) for d in range(3)
    ]


def emit_payloads(layers, even, listed, outs, pads):
    side = layers.shape[0] // 3
    half = side // 2
    wide = layers.shape[1]
    left = left_lanes((half, wide))
    planes = [layers[r * side : (r + 1) * side] for r in range(3)]
    low = [jnp.where(left, p[:half], turned(p[half:])) for p in planes]
    low = jnp.concatenate(low, axis=0)
    whole = left_lanes((side, wide))
    for r, plane in enumerate(blended(planes)):
        pads[0, r, OFF : OFF + side] = jnp.where(whole, turned(plane), 0.0)
    packed = []
    for _, one, two, _ in listed:
        start = OFF + one
        roll = (wide - two) % wide
        opposite = (wide + side - two) % wide
        parts = []
        for r in range(3):
            top = pltpu.roll(pads[0, r, pl.ds(start, half)], roll, 1)
            bottom = pltpu.roll(pads[0, r, pl.ds(start + half, half)], opposite, 1)
            parts.append(jnp.where(left, top, bottom))
        packed.append(jnp.concatenate(parts, axis=0))
    for i, g in enumerate(SHIFTS):
        force = jnp.zeros_like(low)
        for part, (step, _, _, live) in zip(packed, listed):
            force = force + jnp.where((step == g) & live, part, 0.0)
        outs[i][...] = jnp.where(even, force, low)
        outs[3 + i][...] = jnp.where(even, low, force)


def clear_pads(pads):
    side = pads.shape[2] - 2 * OFF
    blank = jnp.zeros((OFF, pads.shape[3]), jnp.float32)
    for n in range(pads.shape[0]):
        for r in range(3):
            pads[n, r, 0:OFF] = blank
            pads[n, r, OFF + side : 2 * OFF + side] = blank


def take_forces(arrived, even, met, listed, pads):
    wide = arrived[0].shape[1]
    half = arrived[0].shape[0] // 3
    side = 2 * half
    left = left_lanes((half, wide))
    lows = [jnp.where(even, arrived[i][...], arrived[3 + i][...]) for i in range(3)]
    pushes = [jnp.where(even, arrived[3 + i][...], arrived[i][...]) for i in range(3)]
    pushed = jnp.zeros_like(lows[0])
    for i in range(3):
        pushed = pushed + jnp.where(met[i], pushes[i], 0.0)
    high = [None] * 3
    for s, (g, one, two, live) in enumerate(listed):
        chosen = jnp.where(g == 0, lows[1], jnp.where(g < 0, lows[0], lows[2]))
        chosen = jnp.where(live, chosen, 0.0)
        for r in range(3):
            part = chosen[r * half : (r + 1) * half]
            pads[1 + s, r, OFF : OFF + half] = jnp.where(left, part, 0.0)
            pads[1 + s, r, OFF + half : OFF + side] = jnp.where(left, turned(part), 0.0)
        start = OFF - one
        roll = (two + wide + side) % wide
        for r in range(3):
            moved = pltpu.roll(pads[1 + s, r, pl.ds(start, side)], roll, 1)
            high[r] = moved if high[r] is None else high[r] + moved
    high = blended(high)
    planes = []
    for r in range(3):
        part = pushed[r * half : (r + 1) * half]
        lower = jnp.concatenate([part, turned(part)], axis=0)
        planes.append(jnp.where(left_lanes((side, wide)), lower, high[r]))
    return jnp.concatenate(planes, axis=0)


def modal_response(force_modes, coupled):
    side = force_modes.shape[0] // 3
    planes = [force_modes[r * side : (r + 1) * side] for r in range(3)]
    index, n = {}, 0
    for r in range(3):
        for s in range(r, 3):
            index[r, s] = index[s, r] = n
            n += 1
    rows = []
    for r in range(3):
        total = None
        for s in range(3):
            i = index[r, s]
            term = coupled[i * side : (i + 1) * side, :] * planes[s]
            total = term if total is None else total + term
        rows.append(total)
    return jnp.concatenate(rows, axis=0)


def tile_count(ref):
    return ref.shape[1] // 128


def planes_of_modes(gathered, tiles):
    planes = []
    for r in range(3):
        planes += weave(
            gathered[r * tiles : (r + 1) * tiles, :], gathered[(3 + r) * tiles : (4 + r) * tiles, :]
        )
    return jnp.concatenate(planes, axis=0)


def collected(block, collect):
    high, low = two_halves(block)
    both = product(collect[...], jnp.concatenate([high, low], axis=0))
    return both[0:8] + both[8:16]


def scatter_tiles(rows, gathered, column):
    tiles = gathered.shape[0] // 8
    for i in range(rows.shape[1] // 128):
        gathered[pl.ds(column // 128 + i, 8, stride=tiles), :] = rows[:, i * 128 : (i + 1) * 128]


def gather_tiles(gathered, column, width):
    tiles = gathered.shape[0] // 8
    return jnp.concatenate(
        [gathered[pl.ds(column // 128 + i, 8, stride=tiles), :] for i in range(width // 128)], axis=1
    )


def pml_planes(state, gathered, woven):
    s0 = state.shape[0]
    tiles = tile_count(state)
    for start, base in ((0, 0), (s0 - 8, 8 * tiles)):
        for J in range(tiles):
            gathered[pl.ds(base + J, 8, stride=tiles), :] = state[
                start : start + 8, J * 128 : (J + 1) * 128
            ]
    for r in range(3):
        high = (8 + 7 - r) * tiles
        first, second = weave(
            gathered[r * tiles : (r + 1) * tiles, :], gathered[high : high + tiles, :]
        )
        woven[pl.ds(r * 2 * tiles, tiles, stride=2), :] = first
        woven[pl.ds(r * 2 * tiles + 1, tiles, stride=2), :] = second
    return woven[...]


def low_high_rows(planes, woven, tiles):
    woven[...] = planes
    rows = []
    for r in range(3):
        first = woven[pl.ds(r * 2 * tiles, tiles, stride=2), :]
        second = woven[pl.ds(r * 2 * tiles + 1, tiles, stride=2), :]
        rows.append(weave(first, second))
    return rows


def spread_pml_forces(planes, gathered, woven):
    tiles = gathered.shape[0] // 16
    rows = low_high_rows(planes, woven, tiles)
    blank = jnp.zeros((tiles, 128), jnp.float32)
    for s in range(8):
        gathered[s * tiles : (s + 1) * tiles, :] = rows[s][0] if s < 3 else blank
        gathered[(8 + s) * tiles : (9 + s) * tiles, :] = rows[7 - s][1] if s > 4 else blank


def spread_modal_forces(modes, gathered):
    tiles = gathered.shape[0] // 16
    side = modes.shape[0] // 3
    half = side // 2
    blank = jnp.zeros((tiles, 128), jnp.float32)
    for r in range(3):
        plane = modes[r * side : (r + 1) * side]
        even, odd = weave(plane[:half], plane[half:])
        gathered[r * tiles : (r + 1) * tiles, :] = even
        gathered[(3 + r) * tiles : (4 + r) * tiles, :] = odd
    for s in (6, 7):
        gathered[s * tiles : (s + 1) * tiles, :] = blank


def injected(gathered, inject, column, width):
    tiles = gathered.shape[0] // 16
    rows = jnp.concatenate(
        [gathered[pl.ds(column // 128 + i, 8, stride=tiles), :] for i in range(width // 128)], axis=1
    )
    high = rows.astype(jnp.bfloat16).astype(jnp.float32)
    stacked = jnp.concatenate([high, rows - high, high, jnp.zeros_like(rows)], axis=0)
    return product(inject[...], stacked.astype(jnp.bfloat16))


def pml_rows(gathered, column, width, base):
    tiles = gathered.shape[0] // 16
    return jnp.concatenate(
        [
            gathered[pl.ds(base * tiles + column // 128 + i, 8, stride=tiles), :]
            for i in range(width // 128)
        ],
        axis=1,
    )


def wide(rows, width):
    return jnp.concatenate([rows] * (width // 128), axis=1)


def near_sums(state, sums, column, width, down, inside):
    high, low = two_halves(state[:, column : column + width])
    parts = [
        product(
            jnp.concatenate(
                [high[:, i : i + 128], low[:, i : i + 128]], axis=1
            ),
            inside[...],
        )
        for i in range(0, width, 128)
    ]
    total = product(down[...], jnp.concatenate([high, low], axis=0)) + jnp.concatenate(parts, axis=1)
    sums[:, column : column + width] = total


def damped_step(state, before, sums, rows, free, column, width):
    s0, total = state.shape
    first, count = column // 128, width // 128
    left = left_lanes((8, 128))
    blank = jnp.zeros((8, 128), jnp.float32)
    for row in range(0, s0, 8):
        span = slice(row, row + 8)
        own, past, pull = [rows[n * s0 + row : n * s0 + row + 8, :] for n in range(3)]
        near, spun = {}, {}
        for J in range(first - 2, first + count + 2):
            inner = 0 <= J < total // 128
            near[J] = state[span, J * 128 : (J + 1) * 128] if inner else blank
            spun[J] = turned(near[J]) if inner else blank
        half = {
            J: jnp.where(left, spun[J - 1], spun[J]) for J in range(first - 1, first + count + 2)
        }
        for J in range(first, first + count):
            at = slice(J * 128, (J + 1) * 128)
            across = (
                STENCIL[1] * (half[J] + half[J + 1])
                + STENCIL[2] * (near[J - 1] + near[J + 1])
                + STENCIL[3] * (half[J - 1] + half[J + 2])
            )
            free[span, at] = (
                own * near[J] + past * before[span, at] + pull * (sums[span, at] + across)
            )


def copies(pairs, sems, first=0):
    return [
        pltpu.make_async_copy(source, target, sems.at[first + i])
        for i, (source, target) in enumerate(pairs)
    ]


def strips(ref, width=CHUNK):
    return [slice(column, column + width) for column in range(0, ref.shape[-1], width)]


def start_kernel(flags, place, listed, now, before, cosine, *refs):
    sources, outs, folds, refs = refs[:3], in_turn(refs[3:9]), refs[9], refs[10:]
    held, prior, factor, layers, pads, gathered, woven, rows, sems = refs[:9]
    collect, inverse_one, inverse_two = refs[9:]
    s0, total = held.shape
    tiles = total // 128
    spans = strips(held, 2 * CHUNK)
    first = copies([(listed, rows)], sems)
    tables = copies(zip(sources, (collect, inverse_one, inverse_two)), sems, 1)
    moves = copies([(now.at[0, :, p], held.at[:, p]) for p in spans], sems, 4)
    past = copies([(before.at[0], prior)], sems, 4 + len(spans))[0]
    more = copies([(cosine, factor)], sems, 5 + len(spans))[0]
    for m in tables[:1] + moves + tables[1:] + first:
        m.start()
    clear_pads(pads)
    for m in moves[: len(moves) // 2]:
        m.wait()
    past.start()
    _, even, _ = noted((flags, place))
    first[0].wait()
    entries = []
    for n in range(listed.shape[0]):
        entries.append((rows[n, 2], rows[n, 3], rows[n, 4], rows[n, 5] != 0))
        folds[n : n + 1, :] = jnp.full((1, 128), folded(*entries[n]), jnp.int32)

    for m in tables:
        m.wait()

    @pl.when(flags[0] > 0)
    def _():
        for m in moves[len(moves) // 2 :]:
            m.wait()
        layers[...] = pml_planes(held, gathered, woven)

    @pl.when(flags[0] <= 0)
    def _():
        more.start()
        for i, p in enumerate(spans):
            if i >= len(moves) // 2:
                moves[i].wait()
            scatter_tiles(collected(held[:, p], collect), gathered.at[0 : 8 * tiles], p.start)
        modes = planes_of_modes(gathered, tiles)
        layers[...] = mirrored_inverse(modes, inverse_one, inverse_two)

    emit_payloads(layers[...], even, entries, outs, pads)

    past.wait()

    @pl.when(flags[0] <= 0)
    def _():
        more.wait()


def free_kernel(pushed, flag, *refs):
    if pushed:
        forces, _, before, cosine, gain, inject, ends = refs[:7]
        refs = refs[7:]
        collect, inverse_one, inverse_two, rows, down, inside, whole = refs[:7]
    else:
        whole, before, cosine, collect, inverse_one, inverse_two, rows = refs[:7]
        down, inside = refs[7:9]
        refs = refs[2:]
    free, layers, gathered, woven, sums = refs[7:]
    s0, total = free.shape
    tiles = total // 128

    @pl.when(flag[0] > 0)
    def _():
        if pushed:
            spread_pml_forces(forces[...], gathered, woven)
            for p in strips(free):
                for n, at in enumerate((0, s0 - 8)):
                    scale = wide(ends[8 * n : 8 * n + 8, :], CHUNK)
                    push = pml_rows(gathered, p.start, CHUNK, 8 * n)
                    whole[at : at + 8, p] = whole[at : at + 8, p] + scale * push
        for p in strips(free):
            near_sums(whole, sums, p.start, CHUNK, down, inside)
        for p in strips(free, 2 * CHUNK):
            damped_step(whole, before, sums, rows, free, p.start, 2 * CHUNK)
        layers[...] = pml_planes(free, gathered, woven)

    @pl.when(flag[0] <= 0)
    def _():
        value = whole[...]
        if pushed:
            spread_modal_forces(forces[...], gathered)
            value = value + gain[...] * injected(gathered, inject, 0, total)
            whole[...] = value
        value = cosine[...] * value - before[...]
        free[...] = value
        scatter_tiles(collected(value, collect), gathered.at[0 : 8 * tiles], 0)
        layers[...] = mirrored_inverse(planes_of_modes(gathered, tiles), inverse_one, inverse_two)


def face_forces(card, folds, arrived, tables, forces, pads):
    clear_pads(pads)
    _, even, met = noted(card)
    push = take_forces(arrived, even, met, joints(folds, pads.shape[0] - 1), pads)

    @pl.when(noted(card)[0])
    def _():
        forces[...] = push

    @pl.when(jnp.logical_not(noted(card)[0]))
    def _():
        forces[...] = mirrored_forward(push, tables[1], tables[2])


def advance_layers(card, layers, tables, forces, next_layers):
    coupled, _, _, inverse_one, inverse_two, face_third = tables
    side = layers.shape[0] // 3

    @pl.when(noted(card)[0])
    def _():
        for r in range(3):
            span = slice(r * side, (r + 1) * side)
            next_layers[span, :] = layers[span, :] + face_third[r : r + 1, :] * forces[span, :]

    @pl.when(jnp.logical_not(noted(card)[0]))
    def _():
        answer = mirrored_inverse(modal_response(forces[...], coupled), inverse_one, inverse_two)
        next_layers[...] = layers[...] + answer


def force_kernel(*refs):
    card, folds, refs = refs[:2], refs[2], refs[3:]
    arrived, layers, tables = in_turn(refs[:6]), refs[6], refs[7:13]
    forces, outs, (next_layers, pads) = refs[13], in_turn(refs[14:20]), refs[20:]
    face_forces(card, folds, arrived, tables, forces, pads)
    advance_layers(card, layers, tables, forces, next_layers)
    listed = joints(folds, pads.shape[0] - 1)
    emit_payloads(next_layers[...], noted(card)[1], listed, outs, pads)


def last_kernel(*refs):
    card, folds, refs = refs[:2], refs[2], refs[3:]
    arrived, layers, tables = in_turn(refs[:6]), refs[6], refs[7:13]
    free, gain, inject, rims = refs[13:17]
    state, faces, forces, next_layers, pads, gathered, woven, held, sems = refs[17:]
    s0, total = free.shape
    tiles = total // 128
    spans = strips(free)
    middle = slice(8, s0 - 8)
    ends = (0, s0 - 8)
    inner = copies([(free.at[middle], state.at[0, middle])], sems)
    outer = copies(
        [(held.at[at : at + 8], state.at[0, at : at + 8]) for at in ends], sems, 1
    )
    moves = copies([(held.at[:, p], state.at[0, :, p]) for p in spans], sems)

    @pl.when(noted(card)[0])
    def _():
        inner[0].start()

    face_forces(card, folds, arrived, tables, forces, pads)

    @pl.when(noted(card)[0])
    def _():
        spread_pml_forces(forces[...], gathered, woven)
        for p in spans:
            for n, at in enumerate(ends):
                scale = wide(rims[8 * n : 8 * n + 8, :], CHUNK)
                push = pml_rows(gathered, p.start, CHUNK, 8 * n)
                held[at : at + 8, p] = free[at : at + 8, p] + scale * push
        for m in outer:
            m.start()

    @pl.when(jnp.logical_not(noted(card)[0]))
    def _():
        spread_modal_forces(forces[...], gathered)
        for m, p in zip(moves, spans):
            held[:, p] = free[:, p] + gain[:, p] * injected(gathered, inject, p.start, CHUNK)
            m.start()

    advance_layers(card, layers, tables, forces, next_layers)
    shown = low_high_rows(next_layers[...], woven, tiles)
    for r in range(3):
        gathered[r * tiles : (r + 1) * tiles, :] = shown[r][0]
        gathered[(3 + r) * tiles : (4 + r) * tiles, :] = shown[r][1]
    last = pltpu.make_async_copy(gathered.at[0 : 6 * tiles], faces, sems.at[len(spans)])
    last.start()

    @pl.when(noted(card)[0])
    def _():
        for m in inner + outer:
            m.wait()

    @pl.when(jnp.logical_not(noted(card)[0]))
    def _():
        for m in moves:
            m.wait()

    last.wait()


SCALAR = pl.BlockSpec(memory_space=pltpu.SMEM)
BLOCK = pl.BlockSpec(memory_space=pltpu.VMEM)
FAR = pl.BlockSpec(memory_space=pltpu.HBM)


def run(body, blocks, outs, scratch, near=(), far=(), far_outs=(), aliases=None, flops=0):
    moved = sum(b.size * b.dtype.itemsize for b in blocks)
    blocks = [
        pltpu.with_memory_space_constraint(b, pltpu.HBM) if i in far else b
        for i, b in enumerate(blocks)
    ]
    spots = {**dict.fromkeys(far, FAR), **dict.fromkeys(near, SCALAR)}
    return pl.pallas_call(
        body,
        out_shape=[
            jax.ShapeDtypeStruct(s, jnp.float32) if isinstance(s, tuple) else s for s in outs
        ],
        in_specs=[spots.get(i, BLOCK) for i in range(len(blocks))],
        out_specs=[
            FAR if i in far_outs else BLOCK
            for i, s in enumerate(outs)
        ],
        scratch_shapes=[
            pltpu.VMEM(s, jnp.float32) if isinstance(s, tuple) else s for s in scratch
        ],
        input_output_aliases=aliases or {},
        compiler_params=pltpu.CompilerParams(vmem_limit_bytes=32 * 1024 * 1024),
        cost_estimate=pl.CostEstimate(flops=flops, bytes_accessed=moved, transcendentals=0),
    )(*blocks)


def local(nx, ny, state_now, state_prev, pml_flags, interfaces):
    _, s0, cross = state_now.shape
    side = math.isqrt(cross)
    t = {k: jnp.asarray(v) for k, v in make_tables(s0, side).items()}
    tiles = cross // 128
    planes = (3 * side, 128)
    packed = (3 * side // 2, 128)
    pads = (1 + interfaces.shape[0], 3, side + 2 * OFF, 128)
    gathered = (16 * tiles, 128)
    full = (s0, cross)
    count = cross // CHUNK
    place = position((nx, ny), lax.axis_index("gx"), lax.axis_index("gy")).reshape(1)
    card = (pml_flags, place)
    routes = [pairing(nx, ny, parity, g) for parity in (0, 1) for g in SHIFTS]

    def exchange(payloads):
        return [lax.ppermute(payloads[k], ("gx", "gy"), routes[i]) for k, i in enumerate(ORDER)]

    result = run(
        start_kernel,
        (
            *(pml_flags, place, interfaces, state_now, state_prev, t["cosine"]),
            *(t["collect"], t["inverse_one"], t["inverse_two"]),
        ),
        [packed] * 6 + [jax.ShapeDtypeStruct((8, 128), jnp.int32)] + [full] * 3,
        [
            *(planes, pads, gathered, planes),
            pltpu.SMEM(interfaces.shape, jnp.int32),
            pltpu.SemaphoreType.DMA((9 + count,)),
            *(pltpu.VMEM(t[k].shape, t[k].dtype) for k in ("collect", "inverse_one", "inverse_two")),
        ],
        near=(0, 1),
        far=range(2, 9),
    )
    payloads, (folds, now, before, cosine) = result[:6], result[6:]
    names = ("coupled", "forward_one", "forward_two", "inverse_one", "inverse_two", "face_third")
    tables = [t[k] for k in names]
    shared = [t[k] for k in ("collect", "inverse_one", "inverse_two", "rows", "down", "inside")]
    for step in range(STEPS):
        arrived = exchange(payloads)
        if step == 0:
            free, layers = run(
                functools.partial(free_kernel, False),
                (pml_flags, now, before, cosine, *shared),
                [full, planes],
                [gathered, planes, full],
                near=(0,),
                flops=10**9,
            )
        else:
            now, free, layers = run(
                functools.partial(free_kernel, True),
                (pml_flags, forces, free, now, cosine, t["gain"], t["inject"], t["ends"], *shared),
                [full, full, planes],
                [gathered, planes, full],
                near=(0,),
                aliases={2: 0},
                flops=10**9,
            )
        if step < STEPS - 1:
            forces, *payloads = run(
                force_kernel,
                (*card, folds, *arrived, layers, *tables),
                [planes] + [packed] * 6,
                [planes, pads],
                near=(0, 1),
            )
    state, faces = run(
        last_kernel,
        (*card, folds, *arrived, layers, *tables, free, t["gain"], t["inject"], t["ends"]),
        [(1, s0, cross), (6 * tiles, 128)],
        [*(planes, planes, pads, gathered, planes, full), pltpu.SemaphoreType.DMA((3 + count,))],
        near=(0, 1),
        far_outs=(0, 1),
    )
    return state, faces.reshape(1, 6, cross)


def solution(mesh):
    placed = (
        P(("gx", "gy"), None, None),
        P(("gx", "gy"), None, None),
        P(("gx", "gy")),
        P(("gx", "gy"), None),
    )
    return jax.shard_map(
        functools.partial(local, mesh.shape["gx"], mesh.shape["gy"]),
        mesh=mesh,
        in_specs=placed,
        out_specs=(P(("gx", "gy"), None, None), P(("gx", "gy"), None, None)),
        check_vma=False,
    )
```

```python
import functools
import math

import jax
import jax.numpy as jnp
import ml_dtypes
import numpy as np
from jax import lax
from jax.experimental import pallas as pl
from jax.experimental.pallas import tpu as pltpu
from jax.sharding import PartitionSpec as P

STEPS = 3
OFF = 16
COURANT = 0.4
DAMPING = 0.5
STENCIL = (-490.0, 270.0, -27.0, 2.0)
BLEND = ((1.5, -0.15, 1.0 / 90.0), (-0.15, 1.0 / 90.0, 0.0), (1.0 / 90.0, 0.0, 0.0))
SHIFTS = (-1, 0, 1)
ORDER = (1, 5, 0, 3, 4, 2)
CHUNK = 512
BF16 = ml_dtypes.bfloat16


def cosine_basis(count):
    freqs = np.arange(count)[:, None]
    cells = np.arange(count)[None, :]
    weight = np.where(freqs == 0, np.sqrt(1.0 / count), np.sqrt(2.0 / count))
    return weight * np.cos(math.pi * freqs * (cells + 0.5) / count)


def halves(values):
    high = values.astype(BF16)
    return high, (values - high.astype(np.float64)).astype(BF16)


def twice(block):
    zero = np.zeros_like(block)
    return np.block([[block, zero], [zero, block]])


def banded(count):
    distance = np.abs(np.arange(count)[:, None] - np.arange(count)[None, :])
    weights = np.zeros((count, count))
    for near in (1, 2, 3):
        weights[distance == near] = STENCIL[near]
    return weights


@functools.lru_cache(maxsize=None)
def make_tables(s0, side):
    along = cosine_basis(s0)
    cross = cosine_basis(side)
    wave = (
        ((math.pi * np.arange(s0) / s0) ** 2)[:, None, None]
        + ((math.pi * np.arange(side) / side) ** 2)[None, :, None]
        + ((math.pi * np.arange(side) / side) ** 2)[None, None, :]
    )
    rooted = np.sqrt(wave)
    safe = np.where(wave > 0.0, wave, 1.0)
    gain = np.where(
        wave > 0.0, 4.0 * np.sin(0.5 * COURANT * rooted) ** 2 / safe, COURANT * COURANT
    )
    twice_cosine = 2.0 * np.cos(COURANT * rooted)
    parity = np.arange(s0) % 2
    face = np.zeros((8, s0))
    for r in range(3):
        face[r] = along[:, r] * (parity == 0)
        face[3 + r] = along[:, r] * (parity == 1)
    face_high, face_low = halves(face)
    zero = np.zeros_like(face_low)
    collect = np.block([[face_high, face_high], [face_low, zero]])
    inject = np.concatenate([face_high.T, face_high.T, face_low.T, zero.T], axis=1)
    order = np.concatenate([np.arange(0, side, 2), np.arange(1, side, 2)])
    coupled = []
    for r in range(3):
        for s in range(r, 3):
            parts = [
                np.einsum("k,kab,k->ab", face[3 * o + r], gain, face[3 * o + s])[order] for o in (0, 1)
            ]
            coupled.append(np.concatenate(parts, axis=1))
    forward_one = np.concatenate([*([halves(cross[order])[0]] * 2), halves(cross[order])[1]], axis=1)
    inverse = cross[order].T
    inverse_one = np.concatenate([*([halves(inverse)[0]] * 2), halves(inverse)[1]], axis=1)
    forward_two = np.concatenate([*([halves(twice(cross.T))[0]] * 2), halves(twice(cross.T))[1]], axis=0)
    inverse_two = np.concatenate([*([halves(twice(cross))[0]] * 2), halves(twice(cross))[1]], axis=0)
    rate = DAMPING * ((np.arange(s0) + 0.5) / s0) ** 2
    first = (2.0 + COURANT * COURANT * 3.0 * STENCIL[0] / 180.0) / (1.0 + rate)
    second = -(1.0 - rate) / (1.0 + rate)
    third = COURANT * COURANT / (1.0 + rate)
    rows = [np.broadcast_to(v[:, None], (s0, 128)) for v in (first, second, third / 180.0)]
    ends = np.concatenate([third[:8], third[-8:]])
    down = np.concatenate([banded(s0)] * 2, axis=1).astype(BF16)
    inside = np.concatenate([twice(banded(side))] * 2, axis=0).astype(BF16)
    face_third = np.stack(
        [np.concatenate([np.full(side, third[r]), np.full(side, third[s0 - 1 - r])]) for r in range(3)]
    )
    face_third = np.concatenate([face_third, np.zeros((5, 2 * side))])
    f32 = np.float32
    return {
        "cosine": twice_cosine.reshape(s0, side * side).astype(f32),
        "gain": gain.reshape(s0, side * side).astype(f32),
        "collect": collect,
        "inject": inject,
        "coupled": np.concatenate(coupled, axis=0).astype(f32),
        "forward_one": forward_one,
        "forward_two": forward_two,
        "inverse_one": inverse_one,
        "inverse_two": inverse_two,
        "rows": np.concatenate(rows, axis=0).astype(f32),
        "ends": np.broadcast_to(ends[:, None], (16, 128)).astype(f32),
        "down": down,
        "inside": inside,
        "face_third": face_third.astype(f32),
    }


def pairing(nx, ny, parity, across):
    taken = {}
    for x in range(parity, nx - 1, 2):
        for y in range(ny):
            if 0 <= y + across < ny:
                taken[(x, y)] = (x + 1, y + across)
                taken[(x + 1, y + across)] = (x, y)
    rest = [(x, y) for x in range(nx) for y in range(ny) if (x, y) not in taken]
    while len(rest) > 1:
        x, y = rest.pop(0)
        mate = min(rest, key=lambda d: (abs(d[1] - y) + abs(d[0] // 2 - x // 2), d))
        if parity == 1 and x == 0:
            wrapped = [d for d in rest if d == (nx - 1, y - across)]
            mate = wrapped[0] if wrapped else mate
        rest.remove(mate)
        taken[(x, y)] = mate
        taken[mate] = (x, y)
    return [(x * ny + y, u * ny + v) for (x, y), (u, v) in sorted(taken.items())]


def noted(card):
    bits = card[1][0]
    return card[0][0] > 0, bits & 1 == 1, [bits & (2 << i) != 0 for i in range(len(SHIFTS))]


def position(shape, along, across):
    bits = 1 - along % 2
    for i, g in enumerate(SHIFTS):
        met = (along > 0) & (across - g >= 0) & (across - g < shape[1])
        bits = bits + jnp.where(met, 2 << i, 0)
    return bits


def folded(step, one, two, live):
    return (step + 1) + ((one + OFF) << 2) + ((two + OFF) << 8) + (jnp.where(live, 1, 0) << 14)


def joints(rows_folded, count):
    rows = []
    for n in range(count):
        bits = rows_folded[n, 0]
        rows.append(
            (
                (bits & 3) - 1,
                ((bits >> 2) & 63) - OFF,
                ((bits >> 8) & 63) - OFF,
                (bits >> 14) & 1 == 1,
            )
        )
    return rows


def in_turn(refs):
    return [refs[ORDER.index(i)] for i in range(len(ORDER))]


def left_lanes(shape):
    return lax.broadcasted_iota(jnp.int32, shape, len(shape) - 1) < shape[-1] // 2


def turned(block):
    return pltpu.roll(block, block.shape[-1] // 2, block.ndim - 1)


def two_halves(block):
    high = block.astype(jnp.bfloat16)
    low = (block - high.astype(jnp.float32)).astype(jnp.bfloat16)
    return high, low


def product(a, b):
    return jnp.dot(a, b, preferred_element_type=jnp.float32)


def over_rows(table, block):
    high, low = two_halves(block)
    return product(table, jnp.concatenate([high, low, high], axis=0))


def over_lanes(block, table):
    high, low = two_halves(block)
    return product(jnp.concatenate([high, low, high], axis=1), table)


def beside(planes):
    side = planes.shape[0] // 3
    return jnp.concatenate([planes[r * side : (r + 1) * side] for r in range(3)], axis=1)


def below(planes):
    wide = planes.shape[1] // 3
    return jnp.concatenate([planes[:, r * wide : (r + 1) * wide] for r in range(3)], axis=0)


def sum_difference(block):
    other = turned(block)
    return jnp.where(left_lanes(block.shape), block + other, other - block)


def mirrored_inverse(modes, inverse_one, inverse_two):
    cells = over_rows(inverse_one[...], beside(over_lanes(modes, inverse_two[...])))
    return sum_difference(below(cells))


def mirrored_forward(planes, forward_one, forward_two):
    cells = sum_difference(planes)
    return over_lanes(below(over_rows(forward_one[...], beside(cells))), forward_two[...])


def weave(first, second):
    left = left_lanes(first.shape)
    return jnp.where(left, first, turned(second)), jnp.where(left, turned(first), second)


def blended(planes):
    return [
        sum(BLEND[d][e] * planes[e] for e in range(3) if BLEND[d][e] != 0.0) for d in range(3)
    ]


def emit_payloads(layers, even, listed, outs, pads):
    side = layers.shape[0] // 3
    half = side // 2
    wide = layers.shape[1]
    left = left_lanes((half, wide))
    planes = [layers[r * side : (r + 1) * side] for r in range(3)]
    low = [jnp.where(left, p[:half], turned(p[half:])) for p in planes]
    low = jnp.concatenate(low, axis=0)
    whole = left_lanes((side, wide))
    for r, plane in enumerate(blended(planes)):
        pads[0, r, OFF : OFF + side] = jnp.where(whole, turned(plane), 0.0)
    packed = []
    for _, one, two, _ in listed:
        start = OFF + one
        roll = (wide - two) % wide
        opposite = (wide + side - two) % wide
        parts = []
        for r in range(3):
            top = pltpu.roll(pads[0, r, pl.ds(start, half)], roll, 1)
            bottom = pltpu.roll(pads[0, r, pl.ds(start + half, half)], opposite, 1)
            parts.append(jnp.where(left, top, bottom))
        packed.append(jnp.concatenate(parts, axis=0))
    for i, g in enumerate(SHIFTS):
        force = jnp.zeros_like(low)
        for part, (step, _, _, live) in zip(packed, listed):
            force = force + jnp.where((step == g) & live, part, 0.0)
        outs[i][...] = jnp.where(even, force, low)
        outs[3 + i][...] = jnp.where(even, low, force)


def clear_pads(pads):
    side = pads.shape[2] - 2 * OFF
    blank = jnp.zeros((OFF, pads.shape[3]), jnp.float32)
    for n in range(pads.shape[0]):
        for r in range(3):
            pads[n, r, 0:OFF] = blank
            pads[n, r, OFF + side : 2 * OFF + side] = blank


def take_forces(arrived, even, met, listed, pads):
    wide = arrived[0].shape[1]
    half = arrived[0].shape[0] // 3
    side = 2 * half
    left = left_lanes((half, wide))
    lows = [jnp.where(even, arrived[i][...], arrived[3 + i][...]) for i in range(3)]
    pushes = [jnp.where(even, arrived[3 + i][...], arrived[i][...]) for i in range(3)]
    pushed = jnp.zeros_like(lows[0])
    for i in range(3):
        pushed = pushed + jnp.where(met[i], pushes[i], 0.0)
    high = [None] * 3
    for s, (g, one, two, live) in enumerate(listed):
        chosen = jnp.where(g == 0, lows[1], jnp.where(g < 0, lows[0], lows[2]))
        chosen = jnp.where(live, chosen, 0.0)
        for r in range(3):
            part = chosen[r * half : (r + 1) * half]
            pads[1 + s, r, OFF : OFF + half] = jnp.where(left, part, 0.0)
            pads[1 + s, r, OFF + half : OFF + side] = jnp.where(left, turned(part), 0.0)
        start = OFF - one
        roll = (two + wide + side) % wide
        for r in range(3):
            moved = pltpu.roll(pads[1 + s, r, pl.ds(start, side)], roll, 1)
            high[r] = moved if high[r] is None else high[r] + moved
    high = blended(high)
    planes = []
    for r in range(3):
        part = pushed[r * half : (r + 1) * half]
        lower = jnp.concatenate([part, turned(part)], axis=0)
        planes.append(jnp.where(left_lanes((side, wide)), lower, high[r]))
    return jnp.concatenate(planes, axis=0)


def modal_response(force_modes, coupled):
    side = force_modes.shape[0] // 3
    planes = [force_modes[r * side : (r + 1) * side] for r in range(3)]
    index, n = {}, 0
    for r in range(3):
        for s in range(r, 3):
            index[r, s] = index[s, r] = n
            n += 1
    rows = []
    for r in range(3):
        total = None
        for s in range(3):
            i = index[r, s]
            term = coupled[i * side : (i + 1) * side, :] * planes[s]
            total = term if total is None else total + term
        rows.append(total)
    return jnp.concatenate(rows, axis=0)


def tile_count(ref):
    return ref.shape[1] // 128


def planes_of_modes(gathered, tiles):
    planes = []
    for r in range(3):
        planes += weave(
            gathered[r * tiles : (r + 1) * tiles, :], gathered[(3 + r) * tiles : (4 + r) * tiles, :]
        )
    return jnp.concatenate(planes, axis=0)


def collected(block, collect):
    high, low = two_halves(block)
    both = product(collect[...], jnp.concatenate([high, low], axis=0))
    return both[0:8] + both[8:16]


def scatter_tiles(rows, gathered, column):
    tiles = gathered.shape[0] // 8
    for i in range(rows.shape[1] // 128):
        gathered[pl.ds(column // 128 + i, 8, stride=tiles), :] = rows[:, i * 128 : (i + 1) * 128]


def gather_tiles(gathered, column, width):
    tiles = gathered.shape[0] // 8
    return jnp.concatenate(
        [gathered[pl.ds(column // 128 + i, 8, stride=tiles), :] for i in range(width // 128)], axis=1
    )


def pml_planes(state, gathered, woven):
    s0 = state.shape[0]
    tiles = tile_count(state)
    for start, base in ((0, 0), (s0 - 8, 8 * tiles)):
        for J in range(tiles):
            gathered[pl.ds(base + J, 8, stride=tiles), :] = state[
                start : start + 8, J * 128 : (J + 1) * 128
            ]
    for r in range(3):
        high = (8 + 7 - r) * tiles
        first, second = weave(
            gathered[r * tiles : (r + 1) * tiles, :], gathered[high : high + tiles, :]
        )
        woven[pl.ds(r * 2 * tiles, tiles, stride=2), :] = first
        woven[pl.ds(r * 2 * tiles + 1, tiles, stride=2), :] = second
    return woven[...]


def low_high_rows(planes, woven, tiles):
    woven[...] = planes
    rows = []
    for r in range(3):
        first = woven[pl.ds(r * 2 * tiles, tiles, stride=2), :]
        second = woven[pl.ds(r * 2 * tiles + 1, tiles, stride=2), :]
        rows.append(weave(first, second))
    return rows


def spread_pml_forces(planes, gathered, woven):
    tiles = gathered.shape[0] // 16
    rows = low_high_rows(planes, woven, tiles)
    blank = jnp.zeros((tiles, 128), jnp.float32)
    for s in range(8):
        gathered[s * tiles : (s + 1) * tiles, :] = rows[s][0] if s < 3 else blank
        gathered[(8 + s) * tiles : (9 + s) * tiles, :] = rows[7 - s][1] if s > 4 else blank


def spread_modal_forces(modes, gathered):
    tiles = gathered.shape[0] // 16
    side = modes.shape[0] // 3
    half = side // 2
    blank = jnp.zeros((tiles, 128), jnp.float32)
    for r in range(3):
        plane = modes[r * side : (r + 1) * side]
        even, odd = weave(plane[:half], plane[half:])
        gathered[r * tiles : (r + 1) * tiles, :] = even
        gathered[(3 + r) * tiles : (4 + r) * tiles, :] = odd
    for s in (6, 7):
        gathered[s * tiles : (s + 1) * tiles, :] = blank


def injected(gathered, inject, column, width):
    tiles = gathered.shape[0] // 16
    rows = jnp.concatenate(
        [gathered[pl.ds(column // 128 + i, 8, stride=tiles), :] for i in range(width // 128)], axis=1
    )
    high = rows.astype(jnp.bfloat16).astype(jnp.float32)
    stacked = jnp.concatenate([high, rows - high, high, jnp.zeros_like(rows)], axis=0)
    return product(inject[...], stacked.astype(jnp.bfloat16))


def pml_rows(gathered, column, width, base):
    tiles = gathered.shape[0] // 16
    return jnp.concatenate(
        [
            gathered[pl.ds(base * tiles + column // 128 + i, 8, stride=tiles), :]
            for i in range(width // 128)
        ],
        axis=1,
    )


def wide(rows, width):
    return jnp.concatenate([rows] * (width // 128), axis=1)


def near_sums(state, sums, column, width, down, inside):
    high, low = two_halves(state[:, column : column + width])
    parts = [
        product(
            jnp.concatenate(
                [high[:, i : i + 128], low[:, i : i + 128]], axis=1
            ),
            inside[...],
        )
        for i in range(0, width, 128)
    ]
    total = product(down[...], jnp.concatenate([high, low], axis=0)) + jnp.concatenate(parts, axis=1)
    sums[:, column : column + width] = total


def damped_step(state, before, sums, rows, free, column, width):
    s0, total = state.shape
    first, count = column // 128, width // 128
    left = left_lanes((8, 128))
    blank = jnp.zeros((8, 128), jnp.float32)
    for row in range(0, s0, 8):
        span = slice(row, row + 8)
        own, past, pull = [rows[n * s0 + row : n * s0 + row + 8, :] for n in range(3)]
        near, spun = {}, {}
        for J in range(first - 2, first + count + 2):
            inner = 0 <= J < total // 128
            near[J] = state[span, J * 128 : (J + 1) * 128] if inner else blank
            spun[J] = turned(near[J]) if inner else blank
        half = {
            J: jnp.where(left, spun[J - 1], spun[J]) for J in range(first - 1, first + count + 2)
        }
        for J in range(first, first + count):
            at = slice(J * 128, (J + 1) * 128)
            across = (
                STENCIL[1] * (half[J] + half[J + 1])
                + STENCIL[2] * (near[J - 1] + near[J + 1])
                + STENCIL[3] * (half[J - 1] + half[J + 2])
            )
            free[span, at] = (
                own * near[J] + past * before[span, at] + pull * (sums[span, at] + across)
            )


def copies(pairs, sems, first=0):
    return [
        pltpu.make_async_copy(source, target, sems.at[first + i])
        for i, (source, target) in enumerate(pairs)
    ]


def strips(ref, width=CHUNK):
    return [slice(column, column + width) for column in range(0, ref.shape[-1], width)]


def start_kernel(flags, place, listed, now, before, cosine, *refs):
    sources, outs, folds, refs = refs[:3], in_turn(refs[3:9]), refs[9], refs[10:]
    held, prior, factor, layers, pads, gathered, woven, rows, sems = refs[:9]
    collect, inverse_one, inverse_two = refs[9:]
    total = held.shape[1]
    tiles = total // 128
    spans = strips(held, 2 * CHUNK)
    first = copies([(listed, rows)], sems)
    tables = copies(zip(sources, (collect, inverse_one, inverse_two)), sems, 1)
    moves = copies([(now.at[0, :, p], held.at[:, p]) for p in spans], sems, 4)
    past = copies([(before.at[0], prior)], sems, 4 + len(spans))[0]
    more = copies([(cosine, factor)], sems, 5 + len(spans))[0]
    for m in tables[:1] + moves + tables[1:] + first + [past]:
        m.start()

    @pl.when(flags[0] <= 0)
    def _():
        more.start()

    clear_pads(pads)

    @pl.when(flags[0] > 0)
    def _():
        for m in moves:
            m.wait()
        layers[...] = pml_planes(held, gathered, woven)
        for m in tables:
            m.wait()

    @pl.when(flags[0] <= 0)
    def _():
        tables[0].wait()
        for i, p in enumerate(spans):
            moves[i].wait()
            scatter_tiles(collected(held[:, p], collect), gathered.at[0 : 8 * tiles], p.start)
        for m in tables[1:]:
            m.wait()
        modes = planes_of_modes(gathered, tiles)
        layers[...] = mirrored_inverse(modes, inverse_one, inverse_two)

    first[0].wait()
    entries = []
    for n in range(listed.shape[0]):
        entries.append((rows[n, 2], rows[n, 3], rows[n, 4], rows[n, 5] != 0))
        folds[n : n + 1, :] = jnp.full((1, 128), folded(*entries[n]), jnp.int32)

    _, even, _ = noted((flags, place))
    emit_payloads(layers[...], even, entries, outs, pads)

    past.wait()

    @pl.when(flags[0] <= 0)
    def _():
        more.wait()


def first_kernel(flag, whole, before, cosine, *refs):
    collect, inverse_one, inverse_two, rows, down, inside = refs[:6]
    free, layers, gathered, woven, sums = refs[6:]
    tiles = free.shape[1] // 128
    spans = strips(free, 2 * CHUNK)

    @pl.when(flag[0] > 0)
    def _():
        for p in strips(free):
            near_sums(whole, sums, p.start, CHUNK, down, inside)
        for p in spans:
            damped_step(whole, before, sums, rows, free, p.start, 2 * CHUNK)
        layers[...] = pml_planes(free, gathered, woven)

    @pl.when(flag[0] <= 0)
    def _():
        value = cosine[...] * whole[...] - before[...]
        free[...] = value
        scatter_tiles(collected(value, collect), gathered.at[0 : 8 * tiles], 0)
        layers[...] = mirrored_inverse(planes_of_modes(gathered, tiles), inverse_one, inverse_two)


def free_kernel(flag, forces, _, before, cosine, gain, inject, ends, *refs):
    collect, inverse_one, inverse_two, rows, down, inside, whole = refs[:7]
    free, layers, gathered, woven, sums = refs[7:]
    s0, total = free.shape
    tiles = total // 128

    @pl.when(flag[0] > 0)
    def _():
        spread_pml_forces(forces[...], gathered, woven)
        for p in strips(free):
            for n, at in enumerate((0, s0 - 8)):
                scale = wide(ends[8 * n : 8 * n + 8, :], CHUNK)
                push = pml_rows(gathered, p.start, CHUNK, 8 * n)
                whole[at : at + 8, p] = whole[at : at + 8, p] + scale * push
        for p in strips(free):
            near_sums(whole, sums, p.start, CHUNK, down, inside)
        for p in strips(free, 2 * CHUNK):
            damped_step(whole, before, sums, rows, free, p.start, 2 * CHUNK)
        layers[...] = pml_planes(free, gathered, woven)

    @pl.when(flag[0] <= 0)
    def _():
        spread_modal_forces(forces[...], gathered)
        value = whole[...] + gain[...] * injected(gathered, inject, 0, total)
        whole[...] = value
        value = cosine[...] * value - before[...]
        free[...] = value
        scatter_tiles(collected(value, collect), gathered.at[0 : 8 * tiles], 0)
        layers[...] = mirrored_inverse(planes_of_modes(gathered, tiles), inverse_one, inverse_two)


def pushes(card, folds, arrived, pads):
    clear_pads(pads)
    _, even, met = noted(card)
    return take_forces(arrived, even, met, joints(folds, pads.shape[0] - 1), pads)


def damped_layers(push, layers, face_third):
    side = push.shape[0] // 3
    return jnp.concatenate(
        [
            layers[r * side : (r + 1) * side, :]
            + face_third[r : r + 1, :] * push[r * side : (r + 1) * side]
            for r in range(3)
        ],
        axis=0,
    )


def modal_layers(modes, layers, coupled, inverse_one, inverse_two):
    return layers[...] + mirrored_inverse(modal_response(modes, coupled), inverse_one, inverse_two)


def force_kernel(*refs):
    card, folds, refs = refs[:2], refs[2], refs[3:]
    arrived, layers, tables = in_turn(refs[:6]), refs[6], refs[7:13]
    forces, outs, (next_layers, pads) = refs[13], in_turn(refs[14:20]), refs[20:]
    coupled, forward_one, forward_two, inverse_one, inverse_two, face_third = tables
    damped, even, _ = noted(card)
    push = pushes(card, folds, arrived, pads)

    @pl.when(damped)
    def _():
        forces[...] = push
        next_layers[...] = damped_layers(push, layers, face_third)

    @pl.when(jnp.logical_not(damped))
    def _():
        modes = mirrored_forward(push, forward_one, forward_two)
        forces[...] = modes
        next_layers[...] = modal_layers(modes, layers, coupled, inverse_one, inverse_two)

    emit_payloads(next_layers[...], even, joints(folds, pads.shape[0] - 1), outs, pads)


def last_kernel(*refs):
    card, folds, refs = refs[:2], refs[2], refs[3:]
    arrived, layers, tables = in_turn(refs[:6]), refs[6], refs[7:13]
    free, gain, inject, rims = refs[13:17]
    state, faces, pads, gathered, shown, woven, held, sems = refs[17:]
    coupled, forward_one, forward_two, inverse_one, inverse_two, face_third = tables
    damped, _, _ = noted(card)
    s0, total = free.shape
    tiles = total // 128
    middle = slice(8, s0 - 8)
    ends = (0, s0 - 8)
    inner = copies([(free.at[middle], state.at[0, middle])], sems)
    outer = copies([(held.at[at : at + 8], state.at[0, at : at + 8]) for at in ends], sems, 1)
    broad = strips(free, 2 * CHUNK)
    moves = copies([(held.at[:, p], state.at[0, :, p]) for p in broad], sems)

    def show(values):
        for r, pair in enumerate(low_high_rows(values, woven, tiles)):
            for i, rows in enumerate(pair):
                shown[(3 * i + r) * tiles : (3 * i + r + 1) * tiles, :] = rows

    @pl.when(damped)
    def _():
        inner[0].start()

    push = pushes(card, folds, arrived, pads)

    @pl.when(damped)
    def _():
        spread_pml_forces(push, gathered, woven)
        for p in strips(free):
            for n, at in enumerate(ends):
                scale = wide(rims[8 * n : 8 * n + 8, :], CHUNK)
                moved = pml_rows(gathered, p.start, CHUNK, 8 * n)
                held[at : at + 8, p] = free[at : at + 8, p] + scale * moved
        for m in outer:
            m.start()
        show(damped_layers(push, layers, face_third))

    @pl.when(jnp.logical_not(damped))
    def _():
        modes = mirrored_forward(push, forward_one, forward_two)
        spread_modal_forces(modes, gathered)
        show(modal_layers(modes, layers, coupled, inverse_one, inverse_two))
        for m, p in zip(moves, broad):
            moved = injected(gathered, inject, p.start, 2 * CHUNK)
            held[:, p] = free[:, p] + gain[:, p] * moved
            m.start()

    last = pltpu.make_async_copy(shown, faces, sems.at[len(broad)])
    last.start()

    @pl.when(damped)
    def _():
        for m in inner + outer:
            m.wait()

    @pl.when(jnp.logical_not(damped))
    def _():
        for m in moves:
            m.wait()

    last.wait()


SCALAR = pl.BlockSpec(memory_space=pltpu.SMEM)
BLOCK = pl.BlockSpec(memory_space=pltpu.VMEM)
FAR = pl.BlockSpec(memory_space=pltpu.HBM)


def run(body, blocks, outs, scratch, near=(), far=(), far_outs=(), aliases=None, flops=0):
    moved = sum(b.size * b.dtype.itemsize for b in blocks)
    blocks = [
        pltpu.with_memory_space_constraint(b, pltpu.HBM) if i in far else b
        for i, b in enumerate(blocks)
    ]
    spots = {**dict.fromkeys(far, FAR), **dict.fromkeys(near, SCALAR)}
    return pl.pallas_call(
        body,
        out_shape=[
            jax.ShapeDtypeStruct(s, jnp.float32) if isinstance(s, tuple) else s for s in outs
        ],
        in_specs=[spots.get(i, BLOCK) for i in range(len(blocks))],
        out_specs=[
            FAR if i in far_outs else BLOCK
            for i, s in enumerate(outs)
        ],
        scratch_shapes=[
            pltpu.VMEM(s, jnp.float32) if isinstance(s, tuple) else s for s in scratch
        ],
        input_output_aliases=aliases or {},
        compiler_params=pltpu.CompilerParams(vmem_limit_bytes=32 * 1024 * 1024),
        cost_estimate=pl.CostEstimate(flops=flops, bytes_accessed=moved, transcendentals=0),
    )(*blocks)


def local(nx, ny, state_now, state_prev, pml_flags, interfaces):
    _, s0, cross = state_now.shape
    side = math.isqrt(cross)
    t = {k: jnp.asarray(v) for k, v in make_tables(s0, side).items()}
    tiles = cross // 128
    planes = (3 * side, 128)
    packed = (3 * side // 2, 128)
    pads = (1 + interfaces.shape[0], 3, side + 2 * OFF, 128)
    gathered = (16 * tiles, 128)
    full = (s0, cross)
    count = cross // CHUNK
    place = position((nx, ny), lax.axis_index("gx"), lax.axis_index("gy")).reshape(1)
    card = (pml_flags, place)
    routes = [pairing(nx, ny, parity, g) for parity in (0, 1) for g in SHIFTS]

    def exchange(payloads):
        return [lax.ppermute(payloads[k], ("gx", "gy"), routes[i]) for k, i in enumerate(ORDER)]

    *payloads, folds, now, prior, cosine = run(
        start_kernel,
        (
            *(pml_flags, place, interfaces, state_now, state_prev, t["cosine"]),
            *(t["collect"], t["inverse_one"], t["inverse_two"]),
        ),
        [packed] * 6 + [jax.ShapeDtypeStruct((8, 128), jnp.int32)] + [full] * 3,
        [
            *(planes, pads, gathered, planes),
            pltpu.SMEM(interfaces.shape, jnp.int32),
            pltpu.SemaphoreType.DMA((6 + count,)),
            *(pltpu.VMEM(t[k].shape, t[k].dtype) for k in ("collect", "inverse_one", "inverse_two")),
        ],
        near=(0, 1),
        far=range(2, 9),
    )
    names = ("coupled", "forward_one", "forward_two", "inverse_one", "inverse_two", "face_third")
    tables = [t[k] for k in names]
    shared = [t[k] for k in ("collect", "inverse_one", "inverse_two", "rows", "down", "inside")]
    for step in range(STEPS):
        arrived = exchange(payloads)
        if step == 0:
            free, layers = run(
                first_kernel,
                (pml_flags, now, prior, cosine, *shared),
                [full, planes],
                [gathered, planes, full],
                near=(0,),
                flops=10**9,
            )
        else:
            now, free, layers = run(
                free_kernel,
                (pml_flags, forces, free, now, cosine, t["gain"], t["inject"], t["ends"], *shared),
                [full, full, planes],
                [gathered, planes, full],
                near=(0,),
                aliases={2: 0},
                flops=10**9,
            )
        if step < STEPS - 1:
            forces, *payloads = run(
                force_kernel,
                (*card, folds, *arrived, layers, *tables),
                [planes] + [packed] * 6,
                [planes, pads],
                near=(0, 1),
            )
    state, faces = run(
        last_kernel,
        (*card, folds, *arrived, layers, *tables, free, t["gain"], t["inject"], t["ends"]),
        [(1, s0, cross), (6 * tiles, 128)],
        [
            *(pads, gathered, (6 * tiles, 128), planes, full),
            pltpu.SemaphoreType.DMA((3 + count,)),
        ],
        near=(0, 1),
        far_outs=(0, 1),
    )
    return state, faces.reshape(1, 6, cross)


def solution(mesh):
    placed = (
        P(("gx", "gy"), None, None),
        P(("gx", "gy"), None, None),
        P(("gx", "gy")),
        P(("gx", "gy"), None),
    )
    return jax.shard_map(
        functools.partial(local, mesh.shape["gx"], mesh.shape["gy"]),
        mesh=mesh,
        in_specs=placed,
        out_specs=(P(("gx", "gy"), None, None), P(("gx", "gy"), None, None)),
        check_vma=False,
    )
```

```python
import functools
import math

import jax
import jax.numpy as jnp
import ml_dtypes
import numpy as np
from jax import lax
from jax.experimental import pallas as pl
from jax.experimental.pallas import tpu as pltpu
from jax.sharding import PartitionSpec as P

STEPS = 3
OFF = 16
COURANT = 0.4
DAMPING = 0.5
STENCIL = (-490.0, 270.0, -27.0, 2.0)
BLEND = ((1.5, -0.15, 1.0 / 90.0), (-0.15, 1.0 / 90.0, 0.0), (1.0 / 90.0, 0.0, 0.0))
SHIFTS = (-1, 0, 1)
ORDER = (0, 5, 2, 3, 4, 1)
CHUNK = 512
BF16 = ml_dtypes.bfloat16


def cosine_basis(count):
    freqs = np.arange(count)[:, None]
    cells = np.arange(count)[None, :]
    weight = np.where(freqs == 0, np.sqrt(1.0 / count), np.sqrt(2.0 / count))
    return weight * np.cos(math.pi * freqs * (cells + 0.5) / count)


def halves(values):
    high = values.astype(BF16)
    return high, (values - high.astype(np.float64)).astype(BF16)


def twice(block):
    zero = np.zeros_like(block)
    return np.block([[block, zero], [zero, block]])


def banded(count):
    distance = np.abs(np.arange(count)[:, None] - np.arange(count)[None, :])
    weights = np.zeros((count, count))
    for near in (1, 2, 3):
        weights[distance == near] = STENCIL[near]
    return weights


@functools.lru_cache(maxsize=None)
def make_tables(s0, side):
    along = cosine_basis(s0)
    cross = cosine_basis(side)
    wave = (
        ((math.pi * np.arange(s0) / s0) ** 2)[:, None, None]
        + ((math.pi * np.arange(side) / side) ** 2)[None, :, None]
        + ((math.pi * np.arange(side) / side) ** 2)[None, None, :]
    )
    rooted = np.sqrt(wave)
    safe = np.where(wave > 0.0, wave, 1.0)
    gain = np.where(
        wave > 0.0, 4.0 * np.sin(0.5 * COURANT * rooted) ** 2 / safe, COURANT * COURANT
    )
    twice_cosine = 2.0 * np.cos(COURANT * rooted)
    parity = np.arange(s0) % 2
    face = np.zeros((8, s0))
    for r in range(3):
        face[r] = along[:, r] * (parity == 0)
        face[3 + r] = along[:, r] * (parity == 1)
    face_high, face_low = halves(face)
    zero = np.zeros_like(face_low)
    collect = np.block([[face_high, face_high], [face_low, zero]])
    inject = np.concatenate([face_high.T, face_high.T, face_low.T, zero.T], axis=1)
    order = np.concatenate([np.arange(0, side, 2), np.arange(1, side, 2)])
    coupled = []
    for r in range(3):
        for s in range(r, 3):
            parts = [
                np.einsum("k,kab,k->ab", face[3 * o + r], gain, face[3 * o + s])[order] for o in (0, 1)
            ]
            coupled.append(np.concatenate(parts, axis=1))
    forward_one = np.concatenate([*([halves(cross[order])[0]] * 2), halves(cross[order])[1]], axis=1)
    inverse = cross[order].T
    inverse_one = np.concatenate([*([halves(inverse)[0]] * 2), halves(inverse)[1]], axis=1)
    forward_two = np.concatenate([*([halves(twice(cross.T))[0]] * 2), halves(twice(cross.T))[1]], axis=0)
    inverse_two = np.concatenate([*([halves(twice(cross))[0]] * 2), halves(twice(cross))[1]], axis=0)
    rate = DAMPING * ((np.arange(s0) + 0.5) / s0) ** 2
    first = (2.0 + COURANT * COURANT * 3.0 * STENCIL[0] / 180.0) / (1.0 + rate)
    second = -(1.0 - rate) / (1.0 + rate)
    third = COURANT * COURANT / (1.0 + rate)
    rows = [np.broadcast_to(v[:, None], (s0, 128)) for v in (first, second, third / 180.0)]
    ends = np.concatenate([third[:8], third[-8:]])
    down = np.concatenate([banded(s0)] * 2, axis=1).astype(BF16)
    inside = np.concatenate([twice(banded(side))] * 2, axis=0).astype(BF16)
    face_third = np.stack(
        [np.concatenate([np.full(side, third[r]), np.full(side, third[s0 - 1 - r])]) for r in range(3)]
    )
    face_third = np.concatenate([face_third, np.zeros((5, 2 * side))])
    f32 = np.float32
    return {
        "cosine": twice_cosine.reshape(s0, side * side).astype(f32),
        "gain": gain.reshape(s0, side * side).astype(f32),
        "collect": collect,
        "inject": inject,
        "coupled": np.concatenate(coupled, axis=0).astype(f32),
        "forward_one": forward_one,
        "forward_two": forward_two,
        "inverse_one": inverse_one,
        "inverse_two": inverse_two,
        "rows": np.concatenate(rows, axis=0).astype(f32),
        "ends": np.broadcast_to(ends[:, None], (16, 128)).astype(f32),
        "down": down,
        "inside": inside,
        "face_third": face_third.astype(f32),
    }


def pairing(nx, ny, parity, across):
    taken = {}
    for x in range(parity, nx - 1, 2):
        for y in range(ny):
            if 0 <= y + across < ny:
                taken[(x, y)] = (x + 1, y + across)
                taken[(x + 1, y + across)] = (x, y)
    rest = [(x, y) for x in range(nx) for y in range(ny) if (x, y) not in taken]
    while len(rest) > 1:
        x, y = rest.pop(0)
        mate = min(rest, key=lambda d: (abs(d[1] - y) + abs(d[0] // 2 - x // 2), d))
        rest.remove(mate)
        taken[(x, y)] = mate
        taken[mate] = (x, y)
    return [(x * ny + y, u * ny + v) for (x, y), (u, v) in sorted(taken.items())]


def noted(card):
    bits = card[1][0]
    return card[0][0] > 0, bits & 1 == 1, [bits & (2 << i) != 0 for i in range(len(SHIFTS))]


def position(shape, along, across):
    bits = 1 - along % 2
    for i, g in enumerate(SHIFTS):
        met = (along > 0) & (across - g >= 0) & (across - g < shape[1])
        bits = bits + jnp.where(met, 2 << i, 0)
    return bits


def folded(step, one, two, live):
    return (step + 1) + ((one + OFF) << 2) + ((two + OFF) << 8) + (jnp.where(live, 1, 0) << 14)


def joints(rows_folded, count):
    rows = []
    for n in range(count):
        bits = rows_folded[n, 0]
        rows.append(
            (
                (bits & 3) - 1,
                ((bits >> 2) & 63) - OFF,
                ((bits >> 8) & 63) - OFF,
                (bits >> 14) & 1 == 1,
            )
        )
    return rows


def in_turn(refs):
    return [refs[ORDER.index(i)] for i in range(len(ORDER))]


def left_lanes(shape):
    return lax.broadcasted_iota(jnp.int32, shape, len(shape) - 1) < shape[-1] // 2


def turned(block):
    return pltpu.roll(block, block.shape[-1] // 2, block.ndim - 1)


def two_halves(block):
    high = block.astype(jnp.bfloat16)
    low = (block - high.astype(jnp.float32)).astype(jnp.bfloat16)
    return high, low


def product(a, b):
    return jnp.dot(a, b, preferred_element_type=jnp.float32)


def over_rows(table, block):
    high, low = two_halves(block)
    return product(table, jnp.concatenate([high, low, high], axis=0))


def over_lanes(block, table):
    high, low = two_halves(block)
    return product(jnp.concatenate([high, low, high], axis=1), table)


def beside(planes):
    side = planes.shape[0] // 3
    return jnp.concatenate([planes[r * side : (r + 1) * side] for r in range(3)], axis=1)


def below(planes):
    wide = planes.shape[1] // 3
    return jnp.concatenate([planes[:, r * wide : (r + 1) * wide] for r in range(3)], axis=0)


def sum_difference(block):
    other = turned(block)
    return jnp.where(left_lanes(block.shape), block + other, other - block)


def mirrored_inverse(modes, inverse_one, inverse_two):
    cells = over_rows(inverse_one[...], beside(over_lanes(modes, inverse_two[...])))
    return sum_difference(below(cells))


def mirrored_forward(planes, forward_one, forward_two):
    cells = sum_difference(planes)
    return over_lanes(below(over_rows(forward_one[...], beside(cells))), forward_two[...])


def weave(first, second):
    left = left_lanes(first.shape)
    return jnp.where(left, first, turned(second)), jnp.where(left, turned(first), second)


def blended(planes):
    return [
        sum(BLEND[d][e] * planes[e] for e in range(3) if BLEND[d][e] != 0.0) for d in range(3)
    ]


def emit_payloads(layers, even, listed, outs, pads):
    side = layers.shape[0] // 3
    half = side // 2
    wide = layers.shape[1]
    left = left_lanes((half, wide))
    planes = [layers[r * side : (r + 1) * side] for r in range(3)]
    low = [jnp.where(left, p[:half], turned(p[half:])) for p in planes]
    low = jnp.concatenate(low, axis=0)
    whole = left_lanes((side, wide))
    for r, plane in enumerate(blended(planes)):
        pads[0, r, OFF : OFF + side] = jnp.where(whole, turned(plane), 0.0)
    packed = []
    for _, one, two, _ in listed:
        start = OFF + one
        roll = (wide - two) % wide
        opposite = (wide + side - two) % wide
        parts = []
        for r in range(3):
            top = pltpu.roll(pads[0, r, pl.ds(start, half)], roll, 1)
            bottom = pltpu.roll(pads[0, r, pl.ds(start + half, half)], opposite, 1)
            parts.append(jnp.where(left, top, bottom))
        packed.append(jnp.concatenate(parts, axis=0))
    for i, g in enumerate(SHIFTS):
        force = jnp.zeros_like(low)
        for part, (step, _, _, live) in zip(packed, listed):
            force = force + jnp.where((step == g) & live, part, 0.0)
        outs[i][...] = jnp.where(even, force, low)
        outs[3 + i][...] = jnp.where(even, low, force)


def clear_pads(pads):
    side = pads.shape[2] - 2 * OFF
    blank = jnp.zeros((OFF, pads.shape[3]), jnp.float32)
    for n in range(pads.shape[0]):
        for r in range(3):
            pads[n, r, 0:OFF] = blank
            pads[n, r, OFF + side : 2 * OFF + side] = blank


def take_forces(arrived, even, met, listed, pads):
    wide = arrived[0].shape[1]
    half = arrived[0].shape[0] // 3
    side = 2 * half
    left = left_lanes((half, wide))
    lows = [jnp.where(even, arrived[i][...], arrived[3 + i][...]) for i in range(3)]
    pushes = [jnp.where(even, arrived[3 + i][...], arrived[i][...]) for i in range(3)]
    pushed = jnp.zeros_like(lows[0])
    for i in range(3):
        pushed = pushed + jnp.where(met[i], pushes[i], 0.0)
    high = [None] * 3
    for s, (g, one, two, live) in enumerate(listed):
        chosen = jnp.where(g == 0, lows[1], jnp.where(g < 0, lows[0], lows[2]))
        chosen = jnp.where(live, chosen, 0.0)
        for r in range(3):
            part = chosen[r * half : (r + 1) * half]
            pads[1 + s, r, OFF : OFF + half] = jnp.where(left, part, 0.0)
            pads[1 + s, r, OFF + half : OFF + side] = jnp.where(left, turned(part), 0.0)
        start = OFF - one
        roll = (two + wide + side) % wide
        for r in range(3):
            moved = pltpu.roll(pads[1 + s, r, pl.ds(start, side)], roll, 1)
            high[r] = moved if high[r] is None else high[r] + moved
    high = blended(high)
    planes = []
    for r in range(3):
        part = pushed[r * half : (r + 1) * half]
        lower = jnp.concatenate([part, turned(part)], axis=0)
        planes.append(jnp.where(left_lanes((side, wide)), lower, high[r]))
    return jnp.concatenate(planes, axis=0)


def modal_response(force_modes, coupled):
    side = force_modes.shape[0] // 3
    planes = [force_modes[r * side : (r + 1) * side] for r in range(3)]
    index, n = {}, 0
    for r in range(3):
        for s in range(r, 3):
            index[r, s] = index[s, r] = n
            n += 1
    rows = []
    for r in range(3):
        total = None
        for s in range(3):
            i = index[r, s]
            term = coupled[i * side : (i + 1) * side, :] * planes[s]
            total = term if total is None else total + term
        rows.append(total)
    return jnp.concatenate(rows, axis=0)


def tile_count(ref):
    return ref.shape[1] // 128


def planes_of_modes(gathered, tiles):
    planes = []
    for r in range(3):
        planes += weave(
            gathered[r * tiles : (r + 1) * tiles, :], gathered[(3 + r) * tiles : (4 + r) * tiles, :]
        )
    return jnp.concatenate(planes, axis=0)


def collected(block, collect):
    high, low = two_halves(block)
    both = product(collect[...], jnp.concatenate([high, low], axis=0))
    return both[0:8] + both[8:16]


def scatter_tiles(rows, gathered, column):
    tiles = gathered.shape[0] // 8
    for i in range(rows.shape[1] // 128):
        gathered[pl.ds(column // 128 + i, 8, stride=tiles), :] = rows[:, i * 128 : (i + 1) * 128]


def gather_tiles(gathered, column, width):
    tiles = gathered.shape[0] // 8
    return jnp.concatenate(
        [gathered[pl.ds(column // 128 + i, 8, stride=tiles), :] for i in range(width // 128)], axis=1
    )


def pml_planes(state, gathered, woven):
    s0 = state.shape[0]
    tiles = tile_count(state)
    for start, base in ((0, 0), (s0 - 8, 8 * tiles)):
        for J in range(tiles):
            gathered[pl.ds(base + J, 8, stride=tiles), :] = state[
                start : start + 8, J * 128 : (J + 1) * 128
            ]
    for r in range(3):
        high = (8 + 7 - r) * tiles
        first, second = weave(
            gathered[r * tiles : (r + 1) * tiles, :], gathered[high : high + tiles, :]
        )
        woven[pl.ds(r * 2 * tiles, tiles, stride=2), :] = first
        woven[pl.ds(r * 2 * tiles + 1, tiles, stride=2), :] = second
    return woven[...]


def low_high_rows(planes, woven, tiles):
    woven[...] = planes
    rows = []
    for r in range(3):
        first = woven[pl.ds(r * 2 * tiles, tiles, stride=2), :]
        second = woven[pl.ds(r * 2 * tiles + 1, tiles, stride=2), :]
        rows.append(weave(first, second))
    return rows


def spread_pml_forces(planes, gathered, woven):
    tiles = gathered.shape[0] // 16
    rows = low_high_rows(planes, woven, tiles)
    blank = jnp.zeros((tiles, 128), jnp.float32)
    for s in range(8):
        gathered[s * tiles : (s + 1) * tiles, :] = rows[s][0] if s < 3 else blank
        gathered[(8 + s) * tiles : (9 + s) * tiles, :] = rows[7 - s][1] if s > 4 else blank


def spread_modal_forces(modes, gathered):
    tiles = gathered.shape[0] // 16
    side = modes.shape[0] // 3
    half = side // 2
    blank = jnp.zeros((tiles, 128), jnp.float32)
    for r in range(3):
        plane = modes[r * side : (r + 1) * side]
        even, odd = weave(plane[:half], plane[half:])
        gathered[r * tiles : (r + 1) * tiles, :] = even
        gathered[(3 + r) * tiles : (4 + r) * tiles, :] = odd
    for s in (6, 7):
        gathered[s * tiles : (s + 1) * tiles, :] = blank


def injected(gathered, inject, column, width):
    tiles = gathered.shape[0] // 16
    rows = jnp.concatenate(
        [gathered[pl.ds(column // 128 + i, 8, stride=tiles), :] for i in range(width // 128)], axis=1
    )
    high = rows.astype(jnp.bfloat16).astype(jnp.float32)
    stacked = jnp.concatenate([high, rows - high, high, jnp.zeros_like(rows)], axis=0)
    return product(inject[...], stacked.astype(jnp.bfloat16))


def pml_rows(gathered, column, width, base):
    tiles = gathered.shape[0] // 16
    return jnp.concatenate(
        [
            gathered[pl.ds(base * tiles + column // 128 + i, 8, stride=tiles), :]
            for i in range(width // 128)
        ],
        axis=1,
    )


def wide(rows, width):
    return jnp.concatenate([rows] * (width // 128), axis=1)


def near_sums(state, sums, column, width, down, inside):
    high, low = two_halves(state[:, column : column + width])
    parts = [
        product(
            jnp.concatenate(
                [high[:, i : i + 128], low[:, i : i + 128]], axis=1
            ),
            inside[...],
        )
        for i in range(0, width, 128)
    ]
    total = product(down[...], jnp.concatenate([high, low], axis=0)) + jnp.concatenate(parts, axis=1)
    sums[:, column : column + width] = total


def damped_step(state, before, sums, rows, free, column, width):
    s0, total = state.shape
    first, count = column // 128, width // 128
    left = left_lanes((8, 128))
    blank = jnp.zeros((8, 128), jnp.float32)
    for row in range(0, s0, 8):
        span = slice(row, row + 8)
        own, past, pull = [rows[n * s0 + row : n * s0 + row + 8, :] for n in range(3)]
        near, spun = {}, {}
        for J in range(first - 2, first + count + 2):
            inner = 0 <= J < total // 128
            near[J] = state[span, J * 128 : (J + 1) * 128] if inner else blank
            spun[J] = turned(near[J]) if inner else blank
        half = {
            J: jnp.where(left, spun[J - 1], spun[J]) for J in range(first - 1, first + count + 2)
        }
        for J in range(first, first + count):
            at = slice(J * 128, (J + 1) * 128)
            across = (
                STENCIL[1] * (half[J] + half[J + 1])
                + STENCIL[2] * (near[J - 1] + near[J + 1])
                + STENCIL[3] * (half[J - 1] + half[J + 2])
            )
            free[span, at] = (
                own * near[J] + past * before[span, at] + pull * (sums[span, at] + across)
            )


def copies(pairs, sems, first=0):
    return [
        pltpu.make_async_copy(source, target, sems.at[first + i])
        for i, (source, target) in enumerate(pairs)
    ]


def strips(ref, width=CHUNK):
    return [slice(column, column + width) for column in range(0, ref.shape[-1], width)]


def start_kernel(flags, place, listed, now, before, cosine, *refs):
    sources, outs, folds, refs = refs[:3], in_turn(refs[3:9]), refs[9], refs[10:]
    held, prior, factor, layers, pads, gathered, woven, rows, sems = refs[:9]
    collect, inverse_one, inverse_two = refs[9:]
    total = held.shape[1]
    tiles = total // 128
    spans = strips(held, 2 * CHUNK)
    first = copies([(listed, rows)], sems)
    tables = copies(zip(sources, (collect, inverse_one, inverse_two)), sems, 1)
    moves = copies([(now.at[0, :, p], held.at[:, p]) for p in spans], sems, 4)
    past = copies([(before.at[0], prior)], sems, 4 + len(spans))[0]
    more = copies([(cosine, factor)], sems, 5 + len(spans))[0]
    for m in tables[:1] + moves + tables[1:] + first + [past]:
        m.start()

    @pl.when(flags[0] <= 0)
    def _():
        more.start()

    clear_pads(pads)

    @pl.when(flags[0] > 0)
    def _():
        for m in moves:
            m.wait()
        layers[...] = pml_planes(held, gathered, woven)
        for m in tables:
            m.wait()

    @pl.when(flags[0] <= 0)
    def _():
        tables[0].wait()
        for i, p in enumerate(spans):
            moves[i].wait()
            scatter_tiles(collected(held[:, p], collect), gathered.at[0 : 8 * tiles], p.start)
        for m in tables[1:]:
            m.wait()
        modes = planes_of_modes(gathered, tiles)
        layers[...] = mirrored_inverse(modes, inverse_one, inverse_two)

    first[0].wait()
    entries = []
    for n in range(listed.shape[0]):
        entries.append((rows[n, 2], rows[n, 3], rows[n, 4], rows[n, 5] != 0))
        folds[n : n + 1, :] = jnp.full((1, 128), folded(*entries[n]), jnp.int32)

    _, even, _ = noted((flags, place))
    emit_payloads(layers[...], even, entries, outs, pads)

    past.wait()

    @pl.when(flags[0] <= 0)
    def _():
        more.wait()


def first_kernel(flag, whole, before, cosine, *refs):
    collect, inverse_one, inverse_two, rows, down, inside = refs[:6]
    free, layers, gathered, woven, sums = refs[6:]
    tiles = free.shape[1] // 128
    spans = strips(free, 2 * CHUNK)

    @pl.when(flag[0] > 0)
    def _():
        for p in strips(free):
            near_sums(whole, sums, p.start, CHUNK, down, inside)
        for p in spans:
            damped_step(whole, before, sums, rows, free, p.start, 2 * CHUNK)
        layers[...] = pml_planes(free, gathered, woven)

    @pl.when(flag[0] <= 0)
    def _():
        value = cosine[...] * whole[...] - before[...]
        free[...] = value
        scatter_tiles(collected(value, collect), gathered.at[0 : 8 * tiles], 0)
        layers[...] = mirrored_inverse(planes_of_modes(gathered, tiles), inverse_one, inverse_two)


def free_kernel(flag, forces, _, before, cosine, gain, inject, ends, *refs):
    collect, inverse_one, inverse_two, rows, down, inside, whole = refs[:7]
    free, layers, gathered, woven, sums = refs[7:]
    s0, total = free.shape
    tiles = total // 128

    @pl.when(flag[0] > 0)
    def _():
        spread_pml_forces(forces[...], gathered, woven)
        for p in strips(free):
            for n, at in enumerate((0, s0 - 8)):
                scale = wide(ends[8 * n : 8 * n + 8, :], CHUNK)
                push = pml_rows(gathered, p.start, CHUNK, 8 * n)
                whole[at : at + 8, p] = whole[at : at + 8, p] + scale * push
        for p in strips(free):
            near_sums(whole, sums, p.start, CHUNK, down, inside)
        for p in strips(free, 2 * CHUNK):
            damped_step(whole, before, sums, rows, free, p.start, 2 * CHUNK)
        layers[...] = pml_planes(free, gathered, woven)

    @pl.when(flag[0] <= 0)
    def _():
        spread_modal_forces(forces[...], gathered)
        value = whole[...] + gain[...] * injected(gathered, inject, 0, total)
        whole[...] = value
        value = cosine[...] * value - before[...]
        free[...] = value
        scatter_tiles(collected(value, collect), gathered.at[0 : 8 * tiles], 0)
        layers[...] = mirrored_inverse(planes_of_modes(gathered, tiles), inverse_one, inverse_two)


def pushes(card, folds, arrived, pads):
    clear_pads(pads)
    _, even, met = noted(card)
    return take_forces(arrived, even, met, joints(folds, pads.shape[0] - 1), pads)


def damped_layers(push, layers, face_third):
    side = push.shape[0] // 3
    return jnp.concatenate(
        [
            layers[r * side : (r + 1) * side, :]
            + face_third[r : r + 1, :] * push[r * side : (r + 1) * side]
            for r in range(3)
        ],
        axis=0,
    )


def modal_layers(modes, layers, coupled, inverse_one, inverse_two):
    return layers[...] + mirrored_inverse(modal_response(modes, coupled), inverse_one, inverse_two)


def force_kernel(*refs):
    card, folds, refs = refs[:2], refs[2], refs[3:]
    arrived, layers, tables = in_turn(refs[:6]), refs[6], refs[7:13]
    forces, outs, (next_layers, pads) = refs[13], in_turn(refs[14:20]), refs[20:]
    coupled, forward_one, forward_two, inverse_one, inverse_two, face_third = tables
    damped, even, _ = noted(card)
    push = pushes(card, folds, arrived, pads)

    @pl.when(damped)
    def _():
        forces[...] = push
        next_layers[...] = damped_layers(push, layers, face_third)

    @pl.when(jnp.logical_not(damped))
    def _():
        modes = mirrored_forward(push, forward_one, forward_two)
        forces[...] = modes
        next_layers[...] = modal_layers(modes, layers, coupled, inverse_one, inverse_two)

    emit_payloads(next_layers[...], even, joints(folds, pads.shape[0] - 1), outs, pads)


def last_kernel(*refs):
    card, folds, refs = refs[:2], refs[2], refs[3:]
    arrived, layers, tables = in_turn(refs[:6]), refs[6], refs[7:13]
    free, gain, inject, rims = refs[13:17]
    state, faces, pads, gathered, shown, woven, held, sems = refs[17:]
    coupled, forward_one, forward_two, inverse_one, inverse_two, face_third = tables
    damped, _, _ = noted(card)
    s0, total = free.shape
    tiles = total // 128
    middle = slice(8, s0 - 8)
    ends = (0, s0 - 8)
    inner = copies([(free.at[middle], state.at[0, middle])], sems)
    outer = copies([(held.at[at : at + 8], state.at[0, at : at + 8]) for at in ends], sems, 1)
    broad = strips(free, 2 * CHUNK)
    moves = copies([(held.at[:, p], state.at[0, :, p]) for p in broad], sems)

    def show(values):
        for r, pair in enumerate(low_high_rows(values, woven, tiles)):
            for i, rows in enumerate(pair):
                shown[(3 * i + r) * tiles : (3 * i + r + 1) * tiles, :] = rows

    @pl.when(damped)
    def _():
        inner[0].start()

    push = pushes(card, folds, arrived, pads)

    @pl.when(damped)
    def _():
        spread_pml_forces(push, gathered, woven)
        for p in strips(free):
            for n, at in enumerate(ends):
                scale = wide(rims[8 * n : 8 * n + 8, :], CHUNK)
                moved = pml_rows(gathered, p.start, CHUNK, 8 * n)
                held[at : at + 8, p] = free[at : at + 8, p] + scale * moved
        for m in outer:
            m.start()
        show(damped_layers(push, layers, face_third))

    @pl.when(jnp.logical_not(damped))
    def _():
        modes = mirrored_forward(push, forward_one, forward_two)
        spread_modal_forces(modes, gathered)
        show(modal_layers(modes, layers, coupled, inverse_one, inverse_two))
        for m, p in zip(moves, broad):
            moved = injected(gathered, inject, p.start, 2 * CHUNK)
            held[:, p] = free[:, p] + gain[:, p] * moved
            m.start()

    last = pltpu.make_async_copy(shown, faces, sems.at[len(broad)])
    last.start()

    @pl.when(damped)
    def _():
        for m in inner + outer:
            m.wait()

    @pl.when(jnp.logical_not(damped))
    def _():
        for m in moves:
            m.wait()

    last.wait()


SCALAR = pl.BlockSpec(memory_space=pltpu.SMEM)
BLOCK = pl.BlockSpec(memory_space=pltpu.VMEM)
FAR = pl.BlockSpec(memory_space=pltpu.HBM)


def run(body, blocks, outs, scratch, near=(), far=(), far_outs=(), aliases=None, flops=0):
    moved = sum(b.size * b.dtype.itemsize for b in blocks)
    blocks = [
        pltpu.with_memory_space_constraint(b, pltpu.HBM) if i in far else b
        for i, b in enumerate(blocks)
    ]
    spots = {**dict.fromkeys(far, FAR), **dict.fromkeys(near, SCALAR)}
    return pl.pallas_call(
        body,
        out_shape=[
            jax.ShapeDtypeStruct(s, jnp.float32) if isinstance(s, tuple) else s for s in outs
        ],
        in_specs=[spots.get(i, BLOCK) for i in range(len(blocks))],
        out_specs=[
            FAR if i in far_outs else BLOCK
            for i, s in enumerate(outs)
        ],
        scratch_shapes=[
            pltpu.VMEM(s, jnp.float32) if isinstance(s, tuple) else s for s in scratch
        ],
        input_output_aliases=aliases or {},
        compiler_params=pltpu.CompilerParams(vmem_limit_bytes=32 * 1024 * 1024),
        cost_estimate=pl.CostEstimate(flops=flops, bytes_accessed=moved, transcendentals=0),
    )(*blocks)


def local(nx, ny, state_now, state_prev, pml_flags, interfaces):
    _, s0, cross = state_now.shape
    side = math.isqrt(cross)
    t = {k: jnp.asarray(v) for k, v in make_tables(s0, side).items()}
    tiles = cross // 128
    planes = (3 * side, 128)
    packed = (3 * side // 2, 128)
    pads = (1 + interfaces.shape[0], 3, side + 2 * OFF, 128)
    gathered = (16 * tiles, 128)
    full = (s0, cross)
    count = cross // CHUNK
    place = position((nx, ny), lax.axis_index("gx"), lax.axis_index("gy")).reshape(1)
    card = (pml_flags, place)
    routes = [pairing(nx, ny, parity, g) for parity in (0, 1) for g in SHIFTS]

    def exchange(payloads):
        return [lax.ppermute(payloads[k], ("gx", "gy"), routes[i]) for k, i in enumerate(ORDER)]

    *payloads, folds, now, prior, cosine = run(
        start_kernel,
        (
            *(pml_flags, place, interfaces, state_now, state_prev, t["cosine"]),
            *(t["collect"], t["inverse_one"], t["inverse_two"]),
        ),
        [packed] * 6 + [jax.ShapeDtypeStruct((8, 128), jnp.int32)] + [full] * 3,
        [
            *(planes, pads, gathered, planes),
            pltpu.SMEM(interfaces.shape, jnp.int32),
            pltpu.SemaphoreType.DMA((6 + count,)),
            *(pltpu.VMEM(t[k].shape, t[k].dtype) for k in ("collect", "inverse_one", "inverse_two")),
        ],
        near=(0, 1),
        far=range(2, 9),
    )
    names = ("coupled", "forward_one", "forward_two", "inverse_one", "inverse_two", "face_third")
    tables = [t[k] for k in names]
    shared = [t[k] for k in ("collect", "inverse_one", "inverse_two", "rows", "down", "inside")]
    for step in range(STEPS):
        arrived = exchange(payloads)
        if step == 0:
            free, layers = run(
                first_kernel,
                (pml_flags, now, prior, cosine, *shared),
                [full, planes],
                [gathered, planes, full],
                near=(0,),
                flops=10**9,
            )
        else:
            now, free, layers = run(
                free_kernel,
                (pml_flags, forces, free, now, cosine, t["gain"], t["inject"], t["ends"], *shared),
                [full, full, planes],
                [gathered, planes, full],
                near=(0,),
                aliases={2: 0},
                flops=10**9,
            )
        if step < STEPS - 1:
            forces, *payloads = run(
                force_kernel,
                (*card, folds, *arrived, layers, *tables),
                [planes] + [packed] * 6,
                [planes, pads],
                near=(0, 1),
            )
    state, faces = run(
        last_kernel,
        (*card, folds, *arrived, layers, *tables, free, t["gain"], t["inject"], t["ends"]),
        [(1, s0, cross), (6 * tiles, 128)],
        [
            *(pads, gathered, (6 * tiles, 128), planes, full),
            pltpu.SemaphoreType.DMA((3 + count,)),
        ],
        near=(0, 1),
        far_outs=(0, 1),
    )
    return state, faces.reshape(1, 6, cross)


def solution(mesh):
    placed = (
        P(("gx", "gy"), None, None),
        P(("gx", "gy"), None, None),
        P(("gx", "gy")),
        P(("gx", "gy"), None),
    )
    return jax.shard_map(
        functools.partial(local, mesh.shape["gx"], mesh.shape["gy"]),
        mesh=mesh,
        in_specs=placed,
        out_specs=(P(("gx", "gy"), None, None), P(("gx", "gy"), None, None)),
        check_vma=False,
    )
```

```python
import functools
import math

import jax
import jax.numpy as jnp
import ml_dtypes
import numpy as np
from jax import lax
from jax.experimental import pallas as pl
from jax.experimental.pallas import tpu as pltpu
from jax.sharding import PartitionSpec as P

STEPS = 3
OFF = 16
COURANT = 0.4
DAMPING = 0.5
STENCIL = (-490.0, 270.0, -27.0, 2.0)
BLEND = ((1.5, -0.15, 1.0 / 90.0), (-0.15, 1.0 / 90.0, 0.0), (1.0 / 90.0, 0.0, 0.0))
SHIFTS = (-1, 0, 1)
ORDER = (0, 5, 2, 3, 4, 1)
CHUNK = 512
BF16 = ml_dtypes.bfloat16


def cosine_basis(count):
    freqs = np.arange(count)[:, None]
    cells = np.arange(count)[None, :]
    weight = np.where(freqs == 0, np.sqrt(1.0 / count), np.sqrt(2.0 / count))
    return weight * np.cos(math.pi * freqs * (cells + 0.5) / count)


def halves(values):
    high = values.astype(BF16)
    return high, (values - high.astype(np.float64)).astype(BF16)


def twice(block):
    zero = np.zeros_like(block)
    return np.block([[block, zero], [zero, block]])


def banded(count):
    distance = np.abs(np.arange(count)[:, None] - np.arange(count)[None, :])
    weights = np.zeros((count, count))
    for near in (1, 2, 3):
        weights[distance == near] = STENCIL[near]
    return weights


@functools.lru_cache(maxsize=None)
def make_tables(s0, side):
    along = cosine_basis(s0)
    cross = cosine_basis(side)
    wave = (
        ((math.pi * np.arange(s0) / s0) ** 2)[:, None, None]
        + ((math.pi * np.arange(side) / side) ** 2)[None, :, None]
        + ((math.pi * np.arange(side) / side) ** 2)[None, None, :]
    )
    rooted = np.sqrt(wave)
    safe = np.where(wave > 0.0, wave, 1.0)
    gain = np.where(
        wave > 0.0, 4.0 * np.sin(0.5 * COURANT * rooted) ** 2 / safe, COURANT * COURANT
    )
    twice_cosine = 2.0 * np.cos(COURANT * rooted)
    parity = np.arange(s0) % 2
    face = np.zeros((8, s0))
    for r in range(3):
        face[r] = along[:, r] * (parity == 0)
        face[3 + r] = along[:, r] * (parity == 1)
    face_high, face_low = halves(face)
    zero = np.zeros_like(face_low)
    collect = np.block([[face_high, face_high], [face_low, zero]])
    inject = np.concatenate([face_high.T, face_high.T, face_low.T, zero.T], axis=1)
    order = np.concatenate([np.arange(0, side, 2), np.arange(1, side, 2)])
    coupled = []
    for r in range(3):
        for s in range(r, 3):
            parts = [
                np.einsum("k,kab,k->ab", face[3 * o + r], gain, face[3 * o + s])[order] for o in (0, 1)
            ]
            coupled.append(np.concatenate(parts, axis=1))
    forward_one = np.concatenate([*([halves(cross[order])[0]] * 2), halves(cross[order])[1]], axis=1)
    inverse = cross[order].T
    inverse_one = np.concatenate([*([halves(inverse)[0]] * 2), halves(inverse)[1]], axis=1)
    forward_two = np.concatenate([*([halves(twice(cross.T))[0]] * 2), halves(twice(cross.T))[1]], axis=0)
    inverse_two = np.concatenate([*([halves(twice(cross))[0]] * 2), halves(twice(cross))[1]], axis=0)
    rate = DAMPING * ((np.arange(s0) + 0.5) / s0) ** 2
    first = (2.0 + COURANT * COURANT * 3.0 * STENCIL[0] / 180.0) / (1.0 + rate)
    second = -(1.0 - rate) / (1.0 + rate)
    third = COURANT * COURANT / (1.0 + rate)
    rows = [np.broadcast_to(v[:, None], (s0, 128)) for v in (first, second, third / 180.0)]
    ends = np.concatenate([third[:8], third[-8:]])
    down = np.concatenate([banded(s0)] * 2, axis=1).astype(BF16)
    inside = np.concatenate([twice(banded(side))] * 2, axis=0).astype(BF16)
    face_third = np.stack(
        [np.concatenate([np.full(side, third[r]), np.full(side, third[s0 - 1 - r])]) for r in range(3)]
    )
    face_third = np.concatenate([face_third, np.zeros((5, 2 * side))])
    f32 = np.float32
    return {
        "cosine": twice_cosine.reshape(s0, side * side).astype(f32),
        "gain": gain.reshape(s0, side * side).astype(f32),
        "collect": collect,
        "inject": inject,
        "coupled": np.concatenate(coupled, axis=0).astype(f32),
        "forward_one": forward_one,
        "forward_two": forward_two,
        "inverse_one": inverse_one,
        "inverse_two": inverse_two,
        "rows": np.concatenate(rows, axis=0).astype(f32),
        "ends": np.broadcast_to(ends[:, None], (16, 128)).astype(f32),
        "down": down,
        "inside": inside,
        "face_third": face_third.astype(f32),
    }


def pairing(nx, ny, parity, across):
    taken = {}
    for x in range(parity, nx - 1, 2):
        for y in range(ny):
            if 0 <= y + across < ny:
                taken[(x, y)] = (x + 1, y + across)
                taken[(x + 1, y + across)] = (x, y)
    rest = [(x, y) for x in range(nx) for y in range(ny) if (x, y) not in taken]
    while len(rest) > 1:
        x, y = rest.pop(0)
        mate = min(rest, key=lambda d: (abs(d[1] - y) + abs(d[0] // 2 - x // 2), d))
        rest.remove(mate)
        taken[(x, y)] = mate
        taken[mate] = (x, y)
    return [(x * ny + y, u * ny + v) for (x, y), (u, v) in sorted(taken.items())]


def noted(card):
    bits = card[1][0]
    return card[0][0] > 0, bits & 1 == 1, [bits & (2 << i) != 0 for i in range(len(SHIFTS))]


def position(shape, along, across):
    bits = 1 - along % 2
    for i, g in enumerate(SHIFTS):
        met = (along > 0) & (across - g >= 0) & (across - g < shape[1])
        bits = bits + jnp.where(met, 2 << i, 0)
    return bits


def folded(step, one, two, live):
    return (step + 1) + ((one + OFF) << 2) + ((two + OFF) << 8) + (jnp.where(live, 1, 0) << 14)


def joints(rows_folded, count):
    rows = []
    for n in range(count):
        bits = rows_folded[n, 0]
        rows.append(
            (
                (bits & 3) - 1,
                ((bits >> 2) & 63) - OFF,
                ((bits >> 8) & 63) - OFF,
                (bits >> 14) & 1 == 1,
            )
        )
    return rows


def in_turn(refs):
    return [refs[ORDER.index(i)] for i in range(len(ORDER))]


def left_lanes(shape):
    return lax.broadcasted_iota(jnp.int32, shape, len(shape) - 1) < shape[-1] // 2


def turned(block):
    return pltpu.roll(block, block.shape[-1] // 2, block.ndim - 1)


def two_halves(block):
    high = block.astype(jnp.bfloat16)
    low = (block - high.astype(jnp.float32)).astype(jnp.bfloat16)
    return high, low


def product(a, b):
    return jnp.dot(a, b, preferred_element_type=jnp.float32)


def over_rows(table, block):
    high, low = two_halves(block)
    return product(table, jnp.concatenate([high, low, high], axis=0))


def over_lanes(block, table):
    high, low = two_halves(block)
    return product(jnp.concatenate([high, low, high], axis=1), table)


def beside(planes):
    side = planes.shape[0] // 3
    return jnp.concatenate([planes[r * side : (r + 1) * side] for r in range(3)], axis=1)


def below(planes):
    wide = planes.shape[1] // 3
    return jnp.concatenate([planes[:, r * wide : (r + 1) * wide] for r in range(3)], axis=0)


def sum_difference(block):
    other = turned(block)
    return jnp.where(left_lanes(block.shape), block + other, other - block)


def mirrored_inverse(modes, inverse_one, inverse_two):
    cells = over_rows(inverse_one[...], beside(over_lanes(modes, inverse_two[...])))
    return sum_difference(below(cells))


def mirrored_forward(planes, forward_one, forward_two):
    cells = sum_difference(planes)
    return over_lanes(below(over_rows(forward_one[...], beside(cells))), forward_two[...])


def weave(first, second):
    left = left_lanes(first.shape)
    return jnp.where(left, first, turned(second)), jnp.where(left, turned(first), second)


def blended(planes):
    return [
        sum(BLEND[d][e] * planes[e] for e in range(3) if BLEND[d][e] != 0.0) for d in range(3)
    ]


def emit_payloads(layers, even, listed, outs, pads):
    side = layers.shape[0] // 3
    half = side // 2
    wide = layers.shape[1]
    left = left_lanes((half, wide))
    planes = [layers[r * side : (r + 1) * side] for r in range(3)]
    low = [jnp.where(left, p[:half], turned(p[half:])) for p in planes]
    low = jnp.concatenate(low, axis=0)
    whole = left_lanes((side, wide))
    for r, plane in enumerate(blended(planes)):
        pads[0, r, OFF : OFF + side] = jnp.where(whole, turned(plane), 0.0)
    packed = []
    for _, one, two, _ in listed:
        start = OFF + one
        roll = (wide - two) % wide
        opposite = (wide + side - two) % wide
        parts = []
        for r in range(3):
            top = pltpu.roll(pads[0, r, pl.ds(start, half)], roll, 1)
            bottom = pltpu.roll(pads[0, r, pl.ds(start + half, half)], opposite, 1)
            parts.append(jnp.where(left, top, bottom))
        packed.append(jnp.concatenate(parts, axis=0))
    for i, g in enumerate(SHIFTS):
        force = jnp.zeros_like(low)
        for part, (step, _, _, live) in zip(packed, listed):
            force = force + jnp.where((step == g) & live, part, 0.0)
        outs[i][...] = jnp.where(even, force, low)
        outs[3 + i][...] = jnp.where(even, low, force)


def clear_pads(pads):
    side = pads.shape[2] - 2 * OFF
    blank = jnp.zeros((OFF, pads.shape[3]), jnp.float32)
    for n in range(pads.shape[0]):
        for r in range(3):
            pads[n, r, 0:OFF] = blank
            pads[n, r, OFF + side : 2 * OFF + side] = blank


def take_forces(arrived, even, met, listed, pads):
    wide = arrived[0].shape[1]
    half = arrived[0].shape[0] // 3
    side = 2 * half
    left = left_lanes((half, wide))
    lows = [jnp.where(even, arrived[i][...], arrived[3 + i][...]) for i in range(3)]
    pushes = [jnp.where(even, arrived[3 + i][...], arrived[i][...]) for i in range(3)]
    pushed = jnp.zeros_like(lows[0])
    for i in range(3):
        pushed = pushed + jnp.where(met[i], pushes[i], 0.0)
    high = [None] * 3
    for s, (g, one, two, live) in enumerate(listed):
        chosen = jnp.where(g == 0, lows[1], jnp.where(g < 0, lows[0], lows[2]))
        chosen = jnp.where(live, chosen, 0.0)
        for r in range(3):
            part = chosen[r * half : (r + 1) * half]
            pads[1 + s, r, OFF : OFF + half] = jnp.where(left, part, 0.0)
            pads[1 + s, r, OFF + half : OFF + side] = jnp.where(left, turned(part), 0.0)
        start = OFF - one
        roll = (two + wide + side) % wide
        for r in range(3):
            moved = pltpu.roll(pads[1 + s, r, pl.ds(start, side)], roll, 1)
            high[r] = moved if high[r] is None else high[r] + moved
    high = blended(high)
    planes = []
    for r in range(3):
        part = pushed[r * half : (r + 1) * half]
        lower = jnp.concatenate([part, turned(part)], axis=0)
        planes.append(jnp.where(left_lanes((side, wide)), lower, high[r]))
    return jnp.concatenate(planes, axis=0)


def modal_response(force_modes, coupled):
    side = force_modes.shape[0] // 3
    planes = [force_modes[r * side : (r + 1) * side] for r in range(3)]
    index, n = {}, 0
    for r in range(3):
        for s in range(r, 3):
            index[r, s] = index[s, r] = n
            n += 1
    rows = []
    for r in range(3):
        total = None
        for s in range(3):
            i = index[r, s]
            term = coupled[i * side : (i + 1) * side, :] * planes[s]
            total = term if total is None else total + term
        rows.append(total)
    return jnp.concatenate(rows, axis=0)


def tile_count(ref):
    return ref.shape[1] // 128


def planes_of_modes(gathered, tiles):
    planes = []
    for r in range(3):
        planes += weave(
            gathered[r * tiles : (r + 1) * tiles, :], gathered[(3 + r) * tiles : (4 + r) * tiles, :]
        )
    return jnp.concatenate(planes, axis=0)


def collected(block, collect):
    high, low = two_halves(block)
    both = product(collect[...], jnp.concatenate([high, low], axis=0))
    return both[0:8] + both[8:16]


def scatter_tiles(rows, gathered, column):
    tiles = gathered.shape[0] // 8
    for i in range(rows.shape[1] // 128):
        gathered[pl.ds(column // 128 + i, 8, stride=tiles), :] = rows[:, i * 128 : (i + 1) * 128]


def gather_tiles(gathered, column, width):
    tiles = gathered.shape[0] // 8
    return jnp.concatenate(
        [gathered[pl.ds(column // 128 + i, 8, stride=tiles), :] for i in range(width // 128)], axis=1
    )


def pml_planes(state, gathered, woven):
    s0 = state.shape[0]
    tiles = tile_count(state)
    for start, base in ((0, 0), (s0 - 8, 8 * tiles)):
        for J in range(tiles):
            gathered[pl.ds(base + J, 8, stride=tiles), :] = state[
                start : start + 8, J * 128 : (J + 1) * 128
            ]
    for r in range(3):
        high = (8 + 7 - r) * tiles
        first, second = weave(
            gathered[r * tiles : (r + 1) * tiles, :], gathered[high : high + tiles, :]
        )
        woven[pl.ds(r * 2 * tiles, tiles, stride=2), :] = first
        woven[pl.ds(r * 2 * tiles + 1, tiles, stride=2), :] = second
    return woven[...]


def low_high_rows(planes, woven, tiles):
    woven[...] = planes
    rows = []
    for r in range(3):
        first = woven[pl.ds(r * 2 * tiles, tiles, stride=2), :]
        second = woven[pl.ds(r * 2 * tiles + 1, tiles, stride=2), :]
        rows.append(weave(first, second))
    return rows


def spread_pml_forces(planes, gathered, woven):
    tiles = gathered.shape[0] // 16
    rows = low_high_rows(planes, woven, tiles)
    blank = jnp.zeros((tiles, 128), jnp.float32)
    for s in range(8):
        gathered[s * tiles : (s + 1) * tiles, :] = rows[s][0] if s < 3 else blank
        gathered[(8 + s) * tiles : (9 + s) * tiles, :] = rows[7 - s][1] if s > 4 else blank


def spread_modal_forces(modes, gathered):
    tiles = gathered.shape[0] // 16
    side = modes.shape[0] // 3
    half = side // 2
    blank = jnp.zeros((tiles, 128), jnp.float32)
    for r in range(3):
        plane = modes[r * side : (r + 1) * side]
        even, odd = weave(plane[:half], plane[half:])
        gathered[r * tiles : (r + 1) * tiles, :] = even
        gathered[(3 + r) * tiles : (4 + r) * tiles, :] = odd
    for s in (6, 7):
        gathered[s * tiles : (s + 1) * tiles, :] = blank


def injected(gathered, inject, column, width):
    tiles = gathered.shape[0] // 16
    rows = jnp.concatenate(
        [gathered[pl.ds(column // 128 + i, 8, stride=tiles), :] for i in range(width // 128)], axis=1
    )
    high = rows.astype(jnp.bfloat16).astype(jnp.float32)
    stacked = jnp.concatenate([high, rows - high, high, jnp.zeros_like(rows)], axis=0)
    return product(inject[...], stacked.astype(jnp.bfloat16))


def pml_rows(gathered, column, width, base):
    tiles = gathered.shape[0] // 16
    return jnp.concatenate(
        [
            gathered[pl.ds(base * tiles + column // 128 + i, 8, stride=tiles), :]
            for i in range(width // 128)
        ],
        axis=1,
    )


def wide(rows, width):
    return jnp.concatenate([rows] * (width // 128), axis=1)


def near_sums(state, sums, column, width, down, inside):
    high, low = two_halves(state[:, column : column + width])
    parts = [
        product(
            jnp.concatenate(
                [high[:, i : i + 128], low[:, i : i + 128]], axis=1
            ),
            inside[...],
        )
        for i in range(0, width, 128)
    ]
    total = product(down[...], jnp.concatenate([high, low], axis=0)) + jnp.concatenate(parts, axis=1)
    sums[:, column : column + width] = total


def damped_step(state, before, sums, rows, free, column, width):
    s0, total = state.shape
    first, count = column // 128, width // 128
    left = left_lanes((8, 128))
    blank = jnp.zeros((8, 128), jnp.float32)
    for row in range(0, s0, 8):
        span = slice(row, row + 8)
        own, past, pull = [rows[n * s0 + row : n * s0 + row + 8, :] for n in range(3)]
        near, spun = {}, {}
        for J in range(first - 2, first + count + 2):
            inner = 0 <= J < total // 128
            near[J] = state[span, J * 128 : (J + 1) * 128] if inner else blank
            spun[J] = turned(near[J]) if inner else blank
        half = {
            J: jnp.where(left, spun[J - 1], spun[J]) for J in range(first - 1, first + count + 2)
        }
        for J in range(first, first + count):
            at = slice(J * 128, (J + 1) * 128)
            across = (
                STENCIL[1] * (half[J] + half[J + 1])
                + STENCIL[2] * (near[J - 1] + near[J + 1])
                + STENCIL[3] * (half[J - 1] + half[J + 2])
            )
            free[span, at] = (
                own * near[J] + past * before[span, at] + pull * (sums[span, at] + across)
            )


def copies(pairs, sems, first=0):
    return [
        pltpu.make_async_copy(source, target, sems.at[first + i])
        for i, (source, target) in enumerate(pairs)
    ]


def strips(ref, width=CHUNK):
    return [slice(column, column + width) for column in range(0, ref.shape[-1], width)]


def start_kernel(flags, place, listed, now, before, cosine, *refs):
    sources, outs, folds, refs = refs[:3], in_turn(refs[3:9]), refs[9], refs[10:]
    held, prior, factor, layers, pads, gathered, woven, rows, sems = refs[:9]
    collect, inverse_one, inverse_two = refs[9:]
    total = held.shape[1]
    tiles = total // 128
    spans = strips(held)
    first = copies([(listed, rows)], sems)
    tables = copies(zip(sources, (collect, inverse_one, inverse_two)), sems, 1)
    moves = copies([(now.at[0, :, p], held.at[:, p]) for p in spans], sems, 4)
    past = copies([(before.at[0], prior)], sems, 4 + len(spans))[0]
    more = copies([(cosine, factor)], sems, 5 + len(spans))[0]
    for m in tables[:1] + moves + tables[1:] + first + [past]:
        m.start()

    @pl.when(flags[0] <= 0)
    def _():
        more.start()

    clear_pads(pads)

    @pl.when(flags[0] > 0)
    def _():
        for m in moves:
            m.wait()
        layers[...] = pml_planes(held, gathered, woven)
        for m in tables:
            m.wait()

    @pl.when(flags[0] <= 0)
    def _():
        tables[0].wait()
        for i, p in enumerate(spans):
            moves[i].wait()
            scatter_tiles(collected(held[:, p], collect), gathered.at[0 : 8 * tiles], p.start)
        for m in tables[1:]:
            m.wait()
        modes = planes_of_modes(gathered, tiles)
        layers[...] = mirrored_inverse(modes, inverse_one, inverse_two)

    first[0].wait()
    entries = []
    for n in range(listed.shape[0]):
        entries.append((rows[n, 2], rows[n, 3], rows[n, 4], rows[n, 5] != 0))
        folds[n : n + 1, :] = jnp.full((1, 128), folded(*entries[n]), jnp.int32)

    _, even, _ = noted((flags, place))
    emit_payloads(layers[...], even, entries, outs, pads)

    past.wait()

    @pl.when(flags[0] <= 0)
    def _():
        more.wait()


def first_kernel(flag, whole, before, cosine, *refs):
    collect, inverse_one, inverse_two, rows, down, inside = refs[:6]
    free, layers, gathered, woven, sums = refs[6:]
    tiles = free.shape[1] // 128
    spans = strips(free, 2 * CHUNK)

    @pl.when(flag[0] > 0)
    def _():
        for p in strips(free):
            near_sums(whole, sums, p.start, CHUNK, down, inside)
        for p in spans:
            damped_step(whole, before, sums, rows, free, p.start, 2 * CHUNK)
        layers[...] = pml_planes(free, gathered, woven)

    @pl.when(flag[0] <= 0)
    def _():
        value = cosine[...] * whole[...] - before[...]
        free[...] = value
        scatter_tiles(collected(value, collect), gathered.at[0 : 8 * tiles], 0)
        layers[...] = mirrored_inverse(planes_of_modes(gathered, tiles), inverse_one, inverse_two)


def free_kernel(flag, forces, _, before, cosine, gain, inject, ends, *refs):
    collect, inverse_one, inverse_two, rows, down, inside, whole = refs[:7]
    free, layers, gathered, woven, sums = refs[7:]
    s0, total = free.shape
    tiles = total // 128

    @pl.when(flag[0] > 0)
    def _():
        spread_pml_forces(forces[...], gathered, woven)
        for p in strips(free):
            for n, at in enumerate((0, s0 - 8)):
                scale = wide(ends[8 * n : 8 * n + 8, :], CHUNK)
                push = pml_rows(gathered, p.start, CHUNK, 8 * n)
                whole[at : at + 8, p] = whole[at : at + 8, p] + scale * push
        for p in strips(free):
            near_sums(whole, sums, p.start, CHUNK, down, inside)
        for p in strips(free, 2 * CHUNK):
            damped_step(whole, before, sums, rows, free, p.start, 2 * CHUNK)
        layers[...] = pml_planes(free, gathered, woven)

    @pl.when(flag[0] <= 0)
    def _():
        spread_modal_forces(forces[...], gathered)
        value = whole[...] + gain[...] * injected(gathered, inject, 0, total)
        whole[...] = value
        value = cosine[...] * value - before[...]
        free[...] = value
        scatter_tiles(collected(value, collect), gathered.at[0 : 8 * tiles], 0)
        layers[...] = mirrored_inverse(planes_of_modes(gathered, tiles), inverse_one, inverse_two)


def pushes(card, folds, arrived, pads):
    clear_pads(pads)
    _, even, met = noted(card)
    return take_forces(arrived, even, met, joints(folds, pads.shape[0] - 1), pads)


def damped_layers(push, layers, face_third):
    side = push.shape[0] // 3
    return jnp.concatenate(
        [
            layers[r * side : (r + 1) * side, :]
            + face_third[r : r + 1, :] * push[r * side : (r + 1) * side]
            for r in range(3)
        ],
        axis=0,
    )


def modal_layers(modes, layers, coupled, inverse_one, inverse_two):
    return layers[...] + mirrored_inverse(modal_response(modes, coupled), inverse_one, inverse_two)


def force_kernel(*refs):
    card, folds, refs = refs[:2], refs[2], refs[3:]
    arrived, layers, tables = in_turn(refs[:6]), refs[6], refs[7:13]
    forces, outs, (next_layers, pads) = refs[13], in_turn(refs[14:20]), refs[20:]
    coupled, forward_one, forward_two, inverse_one, inverse_two, face_third = tables
    damped, even, _ = noted(card)
    push = pushes(card, folds, arrived, pads)

    @pl.when(damped)
    def _():
        forces[...] = push
        next_layers[...] = damped_layers(push, layers, face_third)

    @pl.when(jnp.logical_not(damped))
    def _():
        modes = mirrored_forward(push, forward_one, forward_two)
        forces[...] = modes
        next_layers[...] = modal_layers(modes, layers, coupled, inverse_one, inverse_two)

    emit_payloads(next_layers[...], even, joints(folds, pads.shape[0] - 1), outs, pads)


def last_kernel(*refs):
    card, folds, refs = refs[:2], refs[2], refs[3:]
    arrived, layers, tables = in_turn(refs[:6]), refs[6], refs[7:13]
    free, gain, inject, rims = refs[13:17]
    state, faces, pads, gathered, shown, woven, held, sems = refs[17:]
    coupled, forward_one, forward_two, inverse_one, inverse_two, face_third = tables
    damped, _, _ = noted(card)
    s0, total = free.shape
    tiles = total // 128
    middle = slice(8, s0 - 8)
    ends = (0, s0 - 8)
    inner = copies([(free.at[middle], state.at[0, middle])], sems)
    outer = copies([(held.at[at : at + 8], state.at[0, at : at + 8]) for at in ends], sems, 1)
    broad = strips(free, 2 * CHUNK)
    moves = copies([(held.at[:, p], state.at[0, :, p]) for p in broad], sems)

    def show(values):
        for r, pair in enumerate(low_high_rows(values, woven, tiles)):
            for i, rows in enumerate(pair):
                shown[(3 * i + r) * tiles : (3 * i + r + 1) * tiles, :] = rows

    @pl.when(damped)
    def _():
        inner[0].start()

    push = pushes(card, folds, arrived, pads)

    @pl.when(damped)
    def _():
        spread_pml_forces(push, gathered, woven)
        for p in strips(free):
            for n, at in enumerate(ends):
                scale = wide(rims[8 * n : 8 * n + 8, :], CHUNK)
                moved = pml_rows(gathered, p.start, CHUNK, 8 * n)
                held[at : at + 8, p] = free[at : at + 8, p] + scale * moved
        for m in outer:
            m.start()
        show(damped_layers(push, layers, face_third))

    @pl.when(jnp.logical_not(damped))
    def _():
        modes = mirrored_forward(push, forward_one, forward_two)
        spread_modal_forces(modes, gathered)
        show(modal_layers(modes, layers, coupled, inverse_one, inverse_two))
        for m, p in zip(moves, broad):
            moved = injected(gathered, inject, p.start, 2 * CHUNK)
            held[:, p] = free[:, p] + gain[:, p] * moved
            m.start()

    last = pltpu.make_async_copy(shown, faces, sems.at[len(broad)])
    last.start()

    @pl.when(damped)
    def _():
        for m in inner + outer:
            m.wait()

    @pl.when(jnp.logical_not(damped))
    def _():
        for m in moves:
            m.wait()

    last.wait()


SCALAR = pl.BlockSpec(memory_space=pltpu.SMEM)
BLOCK = pl.BlockSpec(memory_space=pltpu.VMEM)
FAR = pl.BlockSpec(memory_space=pltpu.HBM)


def run(body, blocks, outs, scratch, near=(), far=(), far_outs=(), aliases=None, flops=0):
    moved = sum(b.size * b.dtype.itemsize for b in blocks)
    blocks = [
        pltpu.with_memory_space_constraint(b, pltpu.HBM) if i in far else b
        for i, b in enumerate(blocks)
    ]
    spots = {**dict.fromkeys(far, FAR), **dict.fromkeys(near, SCALAR)}
    return pl.pallas_call(
        body,
        out_shape=[
            jax.ShapeDtypeStruct(s, jnp.float32) if isinstance(s, tuple) else s for s in outs
        ],
        in_specs=[spots.get(i, BLOCK) for i in range(len(blocks))],
        out_specs=[
            FAR if i in far_outs else BLOCK
            for i, s in enumerate(outs)
        ],
        scratch_shapes=[
            pltpu.VMEM(s, jnp.float32) if isinstance(s, tuple) else s for s in scratch
        ],
        input_output_aliases=aliases or {},
        compiler_params=pltpu.CompilerParams(vmem_limit_bytes=32 * 1024 * 1024),
        cost_estimate=pl.CostEstimate(flops=flops, bytes_accessed=moved, transcendentals=0),
    )(*blocks)


def local(nx, ny, state_now, state_prev, pml_flags, interfaces):
    _, s0, cross = state_now.shape
    side = math.isqrt(cross)
    t = {k: jnp.asarray(v) for k, v in make_tables(s0, side).items()}
    tiles = cross // 128
    planes = (3 * side, 128)
    packed = (3 * side // 2, 128)
    pads = (1 + interfaces.shape[0], 3, side + 2 * OFF, 128)
    gathered = (16 * tiles, 128)
    full = (s0, cross)
    count = cross // CHUNK
    place = position((nx, ny), lax.axis_index("gx"), lax.axis_index("gy")).reshape(1)
    card = (pml_flags, place)
    routes = [pairing(nx, ny, parity, g) for parity in (0, 1) for g in SHIFTS]

    def exchange(payloads):
        return [lax.ppermute(payloads[k], ("gx", "gy"), routes[i]) for k, i in enumerate(ORDER)]

    *payloads, folds, now, prior, cosine = run(
        start_kernel,
        (
            *(pml_flags, place, interfaces, state_now, state_prev, t["cosine"]),
            *(t["collect"], t["inverse_one"], t["inverse_two"]),
        ),
        [packed] * 6 + [jax.ShapeDtypeStruct((8, 128), jnp.int32)] + [full] * 3,
        [
            *(planes, pads, gathered, planes),
            pltpu.SMEM(interfaces.shape, jnp.int32),
            pltpu.SemaphoreType.DMA((6 + count,)),
            *(pltpu.VMEM(t[k].shape, t[k].dtype) for k in ("collect", "inverse_one", "inverse_two")),
        ],
        near=(0, 1),
        far=range(2, 9),
    )
    names = ("coupled", "forward_one", "forward_two", "inverse_one", "inverse_two", "face_third")
    tables = [t[k] for k in names]
    shared = [t[k] for k in ("collect", "inverse_one", "inverse_two", "rows", "down", "inside")]
    for step in range(STEPS):
        arrived = exchange(payloads)
        if step == 0:
            free, layers = run(
                first_kernel,
                (pml_flags, now, prior, cosine, *shared),
                [full, planes],
                [gathered, planes, full],
                near=(0,),
                flops=10**9,
            )
        else:
            now, free, layers = run(
                free_kernel,
                (pml_flags, forces, free, now, cosine, t["gain"], t["inject"], t["ends"], *shared),
                [full, full, planes],
                [gathered, planes, full],
                near=(0,),
                aliases={2: 0},
                flops=10**9,
            )
        if step < STEPS - 1:
            forces, *payloads = run(
                force_kernel,
                (*card, folds, *arrived, layers, *tables),
                [planes] + [packed] * 6,
                [planes, pads],
                near=(0, 1),
            )
    state, faces = run(
        last_kernel,
        (*card, folds, *arrived, layers, *tables, free, t["gain"], t["inject"], t["ends"]),
        [(1, s0, cross), (6 * tiles, 128)],
        [
            *(pads, gathered, (6 * tiles, 128), planes, full),
            pltpu.SemaphoreType.DMA((3 + count,)),
        ],
        near=(0, 1),
        far_outs=(0, 1),
    )
    return state, faces.reshape(1, 6, cross)


def solution(mesh):
    placed = (
        P(("gx", "gy"), None, None),
        P(("gx", "gy"), None, None),
        P(("gx", "gy")),
        P(("gx", "gy"), None),
    )
    return jax.shard_map(
        functools.partial(local, mesh.shape["gx"], mesh.shape["gy"]),
        mesh=mesh,
        in_specs=placed,
        out_specs=(P(("gx", "gy"), None, None), P(("gx", "gy"), None, None)),
        check_vma=False,
    )
```

```python
import functools
import math

import jax
import jax.numpy as jnp
import ml_dtypes
import numpy as np
from jax import lax
from jax.experimental import pallas as pl
from jax.experimental.pallas import tpu as pltpu
from jax.sharding import PartitionSpec as P

STEPS = 3
OFF = 16
COURANT = 0.4
DAMPING = 0.5
STENCIL = (-490.0, 270.0, -27.0, 2.0)
BLEND = ((1.5, -0.15, 1.0 / 90.0), (-0.15, 1.0 / 90.0, 0.0), (1.0 / 90.0, 0.0, 0.0))
SHIFTS = (-1, 0, 1)
ORDER = (0, 5, 2, 3, 4, 1)
CHUNK = 512
BF16 = ml_dtypes.bfloat16


def cosine_basis(count):
    freqs = np.arange(count)[:, None]
    cells = np.arange(count)[None, :]
    weight = np.where(freqs == 0, np.sqrt(1.0 / count), np.sqrt(2.0 / count))
    return weight * np.cos(math.pi * freqs * (cells + 0.5) / count)


def halves(values):
    high = values.astype(BF16)
    return high, (values - high.astype(np.float64)).astype(BF16)


def twice(block):
    zero = np.zeros_like(block)
    return np.block([[block, zero], [zero, block]])


def banded(count):
    distance = np.abs(np.arange(count)[:, None] - np.arange(count)[None, :])
    weights = np.zeros((count, count))
    for near in (1, 2, 3):
        weights[distance == near] = STENCIL[near]
    return weights


@functools.lru_cache(maxsize=None)
def make_tables(s0, side):
    along = cosine_basis(s0)
    cross = cosine_basis(side)
    wave = (
        ((math.pi * np.arange(s0) / s0) ** 2)[:, None, None]
        + ((math.pi * np.arange(side) / side) ** 2)[None, :, None]
        + ((math.pi * np.arange(side) / side) ** 2)[None, None, :]
    )
    rooted = np.sqrt(wave)
    safe = np.where(wave > 0.0, wave, 1.0)
    gain = np.where(
        wave > 0.0, 4.0 * np.sin(0.5 * COURANT * rooted) ** 2 / safe, COURANT * COURANT
    )
    twice_cosine = 2.0 * np.cos(COURANT * rooted)
    parity = np.arange(s0) % 2
    face = np.zeros((8, s0))
    for r in range(3):
        face[r] = along[:, r] * (parity == 0)
        face[3 + r] = along[:, r] * (parity == 1)
    face_high, face_low = halves(face)
    zero = np.zeros_like(face_low)
    collect = np.block([[face_high, face_high], [face_low, zero]])
    inject = np.concatenate([face_high.T, face_high.T, face_low.T, zero.T], axis=1)
    order = np.concatenate([np.arange(0, side, 2), np.arange(1, side, 2)])
    coupled = []
    for r in range(3):
        for s in range(r, 3):
            parts = [
                np.einsum("k,kab,k->ab", face[3 * o + r], gain, face[3 * o + s])[order] for o in (0, 1)
            ]
            coupled.append(np.concatenate(parts, axis=1))
    forward_one = np.concatenate([*([halves(cross[order])[0]] * 2), halves(cross[order])[1]], axis=1)
    inverse = cross[order].T
    inverse_one = np.concatenate([*([halves(inverse)[0]] * 2), halves(inverse)[1]], axis=1)
    forward_two = np.concatenate([*([halves(twice(cross.T))[0]] * 2), halves(twice(cross.T))[1]], axis=0)
    inverse_two = np.concatenate([*([halves(twice(cross))[0]] * 2), halves(twice(cross))[1]], axis=0)
    rate = DAMPING * ((np.arange(s0) + 0.5) / s0) ** 2
    first = (2.0 + COURANT * COURANT * 3.0 * STENCIL[0] / 180.0) / (1.0 + rate)
    second = -(1.0 - rate) / (1.0 + rate)
    third = COURANT * COURANT / (1.0 + rate)
    rows = [np.broadcast_to(v[:, None], (s0, 128)) for v in (first, second, third / 180.0)]
    ends = np.concatenate([third[:8], third[-8:]])
    down = np.concatenate([banded(s0)] * 2, axis=1).astype(BF16)
    inside = np.concatenate([twice(banded(side))] * 2, axis=0).astype(BF16)
    face_third = np.stack(
        [np.concatenate([np.full(side, third[r]), np.full(side, third[s0 - 1 - r])]) for r in range(3)]
    )
    face_third = np.concatenate([face_third, np.zeros((5, 2 * side))])
    f32 = np.float32
    return {
        "cosine": twice_cosine.reshape(s0, side * side).astype(f32),
        "gain": gain.reshape(s0, side * side).astype(f32),
        "collect": collect,
        "inject": inject,
        "coupled": np.concatenate(coupled, axis=0).astype(f32),
        "forward_one": forward_one,
        "forward_two": forward_two,
        "inverse_one": inverse_one,
        "inverse_two": inverse_two,
        "rows": np.concatenate(rows, axis=0).astype(f32),
        "ends": np.broadcast_to(ends[:, None], (16, 128)).astype(f32),
        "down": down,
        "inside": inside,
        "face_third": face_third.astype(f32),
    }


def pairing(nx, ny, parity, across):
    taken = {}
    for x in range(parity, nx - 1, 2):
        for y in range(ny):
            if 0 <= y + across < ny:
                taken[(x, y)] = (x + 1, y + across)
                taken[(x + 1, y + across)] = (x, y)
    rest = [(x, y) for x in range(nx) for y in range(ny) if (x, y) not in taken]
    while len(rest) > 1:
        x, y = rest.pop(0)
        mate = min(rest, key=lambda d: (abs(d[1] - y) + abs(d[0] // 2 - x // 2), d))
        rest.remove(mate)
        taken[(x, y)] = mate
        taken[mate] = (x, y)
    return [(x * ny + y, u * ny + v) for (x, y), (u, v) in sorted(taken.items())]


def noted(card):
    bits = card[1][0]
    return card[0][0] > 0, bits & 1 == 1, [bits & (2 << i) != 0 for i in range(len(SHIFTS))]


def position(shape, along, across):
    bits = 1 - along % 2
    for i, g in enumerate(SHIFTS):
        met = (along > 0) & (across - g >= 0) & (across - g < shape[1])
        bits = bits + jnp.where(met, 2 << i, 0)
    return bits


def folded(step, one, two, live):
    return (step + 1) + ((one + OFF) << 2) + ((two + OFF) << 8) + (jnp.where(live, 1, 0) << 14)


def joints(rows_folded, count):
    rows = []
    for n in range(count):
        bits = rows_folded[n, 0]
        rows.append(
            (
                (bits & 3) - 1,
                ((bits >> 2) & 63) - OFF,
                ((bits >> 8) & 63) - OFF,
                (bits >> 14) & 1 == 1,
            )
        )
    return rows


def in_turn(refs):
    return [refs[ORDER.index(i)] for i in range(len(ORDER))]


def left_lanes(shape):
    return lax.broadcasted_iota(jnp.int32, shape, len(shape) - 1) < shape[-1] // 2


def turned(block):
    return pltpu.roll(block, block.shape[-1] // 2, block.ndim - 1)


def two_halves(block):
    high = block.astype(jnp.bfloat16)
    low = (block - high.astype(jnp.float32)).astype(jnp.bfloat16)
    return high, low


def product(a, b):
    return jnp.dot(a, b, preferred_element_type=jnp.float32)


def over_rows(table, block):
    high, low = two_halves(block)
    return product(table, jnp.concatenate([high, low, high], axis=0))


def over_lanes(block, table):
    high, low = two_halves(block)
    return product(jnp.concatenate([high, low, high], axis=1), table)


def beside(planes):
    side = planes.shape[0] // 3
    return jnp.concatenate([planes[r * side : (r + 1) * side] for r in range(3)], axis=1)


def below(planes):
    wide = planes.shape[1] // 3
    return jnp.concatenate([planes[:, r * wide : (r + 1) * wide] for r in range(3)], axis=0)


def sum_difference(block):
    other = turned(block)
    return jnp.where(left_lanes(block.shape), block + other, other - block)


def mirrored_inverse(modes, inverse_one, inverse_two):
    cells = over_rows(inverse_one[...], beside(over_lanes(modes, inverse_two[...])))
    return sum_difference(below(cells))


def mirrored_forward(planes, forward_one, forward_two):
    cells = sum_difference(planes)
    return over_lanes(below(over_rows(forward_one[...], beside(cells))), forward_two[...])


def weave(first, second):
    left = left_lanes(first.shape)
    return jnp.where(left, first, turned(second)), jnp.where(left, turned(first), second)


def blended(planes):
    return [
        sum(BLEND[d][e] * planes[e] for e in range(3) if BLEND[d][e] != 0.0) for d in range(3)
    ]


def emit_payloads(layers, even, listed, outs, pads):
    side = layers.shape[0] // 3
    half = side // 2
    wide = layers.shape[1]
    left = left_lanes((half, wide))
    planes = [layers[r * side : (r + 1) * side] for r in range(3)]
    low = [jnp.where(left, p[:half], turned(p[half:])) for p in planes]
    low = jnp.concatenate(low, axis=0)
    whole = left_lanes((side, wide))
    for r, plane in enumerate(blended(planes)):
        pads[0, r, OFF : OFF + side] = jnp.where(whole, turned(plane), 0.0)
    packed = []
    for _, one, two, _ in listed:
        start = OFF + one
        roll = (wide - two) % wide
        opposite = (wide + side - two) % wide
        parts = []
        for r in range(3):
            top = pltpu.roll(pads[0, r, pl.ds(start, half)], roll, 1)
            bottom = pltpu.roll(pads[0, r, pl.ds(start + half, half)], opposite, 1)
            parts.append(jnp.where(left, top, bottom))
        packed.append(jnp.concatenate(parts, axis=0))
    for i, g in enumerate(SHIFTS):
        force = jnp.zeros_like(low)
        for part, (step, _, _, live) in zip(packed, listed):
            force = force + jnp.where((step == g) & live, part, 0.0)
        outs[i][...] = jnp.where(even, force, low)
        outs[3 + i][...] = jnp.where(even, low, force)


def clear_pads(pads):
    side = pads.shape[2] - 2 * OFF
    blank = jnp.zeros((OFF, pads.shape[3]), jnp.float32)
    for n in range(pads.shape[0]):
        for r in range(3):
            pads[n, r, 0:OFF] = blank
            pads[n, r, OFF + side : 2 * OFF + side] = blank


def take_forces(arrived, even, met, listed, pads):
    wide = arrived[0].shape[1]
    half = arrived[0].shape[0] // 3
    side = 2 * half
    left = left_lanes((half, wide))
    lows = [jnp.where(even, arrived[i][...], arrived[3 + i][...]) for i in range(3)]
    pushes = [jnp.where(even, arrived[3 + i][...], arrived[i][...]) for i in range(3)]
    pushed = jnp.zeros_like(lows[0])
    for i in range(3):
        pushed = pushed + jnp.where(met[i], pushes[i], 0.0)
    high = [None] * 3
    for s, (g, one, two, live) in enumerate(listed):
        chosen = jnp.where(g == 0, lows[1], jnp.where(g < 0, lows[0], lows[2]))
        chosen = jnp.where(live, chosen, 0.0)
        for r in range(3):
            part = chosen[r * half : (r + 1) * half]
            pads[1 + s, r, OFF : OFF + half] = jnp.where(left, part, 0.0)
            pads[1 + s, r, OFF + half : OFF + side] = jnp.where(left, turned(part), 0.0)
        start = OFF - one
        roll = (two + wide + side) % wide
        for r in range(3):
            moved = pltpu.roll(pads[1 + s, r, pl.ds(start, side)], roll, 1)
            high[r] = moved if high[r] is None else high[r] + moved
    high = blended(high)
    planes = []
    for r in range(3):
        part = pushed[r * half : (r + 1) * half]
        lower = jnp.concatenate([part, turned(part)], axis=0)
        planes.append(jnp.where(left_lanes((side, wide)), lower, high[r]))
    return jnp.concatenate(planes, axis=0)


def modal_response(force_modes, coupled):
    side = force_modes.shape[0] // 3
    planes = [force_modes[r * side : (r + 1) * side] for r in range(3)]
    index, n = {}, 0
    for r in range(3):
        for s in range(r, 3):
            index[r, s] = index[s, r] = n
            n += 1
    rows = []
    for r in range(3):
        total = None
        for s in range(3):
            i = index[r, s]
            term = coupled[i * side : (i + 1) * side, :] * planes[s]
            total = term if total is None else total + term
        rows.append(total)
    return jnp.concatenate(rows, axis=0)


def tile_count(ref):
    return ref.shape[1] // 128


def planes_of_modes(gathered, tiles):
    planes = []
    for r in range(3):
        planes += weave(
            gathered[r * tiles : (r + 1) * tiles, :], gathered[(3 + r) * tiles : (4 + r) * tiles, :]
        )
    return jnp.concatenate(planes, axis=0)


def collected(block, collect):
    high, low = two_halves(block)
    both = product(collect[...], jnp.concatenate([high, low], axis=0))
    return both[0:8] + both[8:16]


def scatter_tiles(rows, gathered, column):
    tiles = gathered.shape[0] // 8
    for i in range(rows.shape[1] // 128):
        gathered[pl.ds(column // 128 + i, 8, stride=tiles), :] = rows[:, i * 128 : (i + 1) * 128]


def gather_tiles(gathered, column, width):
    tiles = gathered.shape[0] // 8
    return jnp.concatenate(
        [gathered[pl.ds(column // 128 + i, 8, stride=tiles), :] for i in range(width // 128)], axis=1
    )


def pml_planes(state, gathered, woven):
    s0 = state.shape[0]
    tiles = tile_count(state)
    for start, base in ((0, 0), (s0 - 8, 8 * tiles)):
        for J in range(tiles):
            gathered[pl.ds(base + J, 8, stride=tiles), :] = state[
                start : start + 8, J * 128 : (J + 1) * 128
            ]
    for r in range(3):
        high = (8 + 7 - r) * tiles
        first, second = weave(
            gathered[r * tiles : (r + 1) * tiles, :], gathered[high : high + tiles, :]
        )
        woven[pl.ds(r * 2 * tiles, tiles, stride=2), :] = first
        woven[pl.ds(r * 2 * tiles + 1, tiles, stride=2), :] = second
    return woven[...]


def low_high_rows(planes, woven, tiles):
    woven[...] = planes
    rows = []
    for r in range(3):
        first = woven[pl.ds(r * 2 * tiles, tiles, stride=2), :]
        second = woven[pl.ds(r * 2 * tiles + 1, tiles, stride=2), :]
        rows.append(weave(first, second))
    return rows


def spread_pml_forces(planes, gathered, woven):
    tiles = gathered.shape[0] // 16
    rows = low_high_rows(planes, woven, tiles)
    blank = jnp.zeros((tiles, 128), jnp.float32)
    for s in range(8):
        gathered[s * tiles : (s + 1) * tiles, :] = rows[s][0] if s < 3 else blank
        gathered[(8 + s) * tiles : (9 + s) * tiles, :] = rows[7 - s][1] if s > 4 else blank


def spread_modal_forces(modes, gathered):
    tiles = gathered.shape[0] // 16
    side = modes.shape[0] // 3
    half = side // 2
    blank = jnp.zeros((tiles, 128), jnp.float32)
    for r in range(3):
        plane = modes[r * side : (r + 1) * side]
        even, odd = weave(plane[:half], plane[half:])
        gathered[r * tiles : (r + 1) * tiles, :] = even
        gathered[(3 + r) * tiles : (4 + r) * tiles, :] = odd
    for s in (6, 7):
        gathered[s * tiles : (s + 1) * tiles, :] = blank


def injected(gathered, inject, column, width):
    tiles = gathered.shape[0] // 16
    rows = jnp.concatenate(
        [gathered[pl.ds(column // 128 + i, 8, stride=tiles), :] for i in range(width // 128)], axis=1
    )
    high = rows.astype(jnp.bfloat16).astype(jnp.float32)
    stacked = jnp.concatenate([high, rows - high, high, jnp.zeros_like(rows)], axis=0)
    return product(inject[...], stacked.astype(jnp.bfloat16))


def pml_rows(gathered, column, width, base):
    tiles = gathered.shape[0] // 16
    return jnp.concatenate(
        [
            gathered[pl.ds(base * tiles + column // 128 + i, 8, stride=tiles), :]
            for i in range(width // 128)
        ],
        axis=1,
    )


def wide(rows, width):
    return jnp.concatenate([rows] * (width // 128), axis=1)


def near_sums(state, sums, column, width, down, inside):
    high, low = two_halves(state[:, column : column + width])
    parts = [
        product(
            jnp.concatenate(
                [high[:, i : i + 128], low[:, i : i + 128]], axis=1
            ),
            inside[...],
        )
        for i in range(0, width, 128)
    ]
    total = product(down[...], jnp.concatenate([high, low], axis=0)) + jnp.concatenate(parts, axis=1)
    sums[:, column : column + width] = total


def damped_step(state, before, sums, rows, free, column, width):
    s0, total = state.shape
    first, count = column // 128, width // 128
    left = left_lanes((8, 128))
    blank = jnp.zeros((8, 128), jnp.float32)
    for row in range(0, s0, 8):
        span = slice(row, row + 8)
        own, past, pull = [rows[n * s0 + row : n * s0 + row + 8, :] for n in range(3)]
        near, spun = {}, {}
        for J in range(first - 2, first + count + 2):
            inner = 0 <= J < total // 128
            near[J] = state[span, J * 128 : (J + 1) * 128] if inner else blank
            spun[J] = turned(near[J]) if inner else blank
        half = {
            J: jnp.where(left, spun[J - 1], spun[J]) for J in range(first - 1, first + count + 2)
        }
        for J in range(first, first + count):
            at = slice(J * 128, (J + 1) * 128)
            across = (
                STENCIL[1] * (half[J] + half[J + 1])
                + STENCIL[2] * (near[J - 1] + near[J + 1])
                + STENCIL[3] * (half[J - 1] + half[J + 2])
            )
            free[span, at] = (
                own * near[J] + past * before[span, at] + pull * (sums[span, at] + across)
            )


def copies(pairs, sems, first=0):
    return [
        pltpu.make_async_copy(source, target, sems.at[first + i])
        for i, (source, target) in enumerate(pairs)
    ]


def strips(ref, width=CHUNK):
    return [slice(column, column + width) for column in range(0, ref.shape[-1], width)]


def start_kernel(flags, place, listed, now, before, cosine, *refs):
    sources, outs, folds, refs = refs[:3], in_turn(refs[3:9]), refs[9], refs[10:]
    held, prior, factor, layers, pads, gathered, woven, rows, sems = refs[:9]
    collect, inverse_one, inverse_two = refs[9:]
    total = held.shape[1]
    tiles = total // 128
    spans = strips(held)
    first = copies([(listed, rows)], sems)
    tables = copies(zip(sources, (collect, inverse_one, inverse_two)), sems, 1)
    moves = copies([(now.at[0, :, p], held.at[:, p]) for p in spans], sems, 4)
    past = copies([(before.at[0], prior)], sems, 4 + len(spans))[0]
    more = copies([(cosine, factor)], sems, 5 + len(spans))[0]
    for m in tables[:1] + moves + tables[1:] + first + [past]:
        m.start()

    @pl.when(flags[0] <= 0)
    def _():
        more.start()

    clear_pads(pads)

    @pl.when(flags[0] > 0)
    def _():
        for m in moves:
            m.wait()
        layers[...] = pml_planes(held, gathered, woven)
        for m in tables:
            m.wait()

    @pl.when(flags[0] <= 0)
    def _():
        tables[0].wait()
        for i, p in enumerate(spans):
            moves[i].wait()
            scatter_tiles(collected(held[:, p], collect), gathered.at[0 : 8 * tiles], p.start)
        for m in tables[1:]:
            m.wait()
        modes = planes_of_modes(gathered, tiles)
        layers[...] = mirrored_inverse(modes, inverse_one, inverse_two)

    first[0].wait()
    entries = []
    for n in range(listed.shape[0]):
        entries.append((rows[n, 2], rows[n, 3], rows[n, 4], rows[n, 5] != 0))
        folds[n : n + 1, :] = jnp.full((1, 128), folded(*entries[n]), jnp.int32)

    _, even, _ = noted((flags, place))
    emit_payloads(layers[...], even, entries, outs, pads)

    past.wait()

    @pl.when(flags[0] <= 0)
    def _():
        more.wait()


def first_kernel(flag, whole, before, cosine, *refs):
    collect, inverse_one, inverse_two, rows, down, inside = refs[:6]
    free, layers, gathered, woven, sums = refs[6:]
    tiles = free.shape[1] // 128
    spans = strips(free, 2 * CHUNK)

    @pl.when(flag[0] > 0)
    def _():
        for p in strips(free):
            near_sums(whole, sums, p.start, CHUNK, down, inside)
        for p in spans:
            damped_step(whole, before, sums, rows, free, p.start, 2 * CHUNK)
        layers[...] = pml_planes(free, gathered, woven)

    @pl.when(flag[0] <= 0)
    def _():
        value = cosine[...] * whole[...] - before[...]
        free[...] = value
        scatter_tiles(collected(value, collect), gathered.at[0 : 8 * tiles], 0)
        layers[...] = mirrored_inverse(planes_of_modes(gathered, tiles), inverse_one, inverse_two)


def free_kernel(flag, forces, _, before, cosine, gain, inject, ends, *refs):
    collect, inverse_one, inverse_two, rows, down, inside, whole = refs[:7]
    free, layers, gathered, woven, sums = refs[7:]
    s0, total = free.shape
    tiles = total // 128

    @pl.when(flag[0] > 0)
    def _():
        spread_pml_forces(forces[...], gathered, woven)
        for p in strips(free):
            for n, at in enumerate((0, s0 - 8)):
                scale = wide(ends[8 * n : 8 * n + 8, :], CHUNK)
                push = pml_rows(gathered, p.start, CHUNK, 8 * n)
                whole[at : at + 8, p] = whole[at : at + 8, p] + scale * push
        for p in strips(free):
            near_sums(whole, sums, p.start, CHUNK, down, inside)
        for p in strips(free, 2 * CHUNK):
            damped_step(whole, before, sums, rows, free, p.start, 2 * CHUNK)
        layers[...] = pml_planes(free, gathered, woven)

    @pl.when(flag[0] <= 0)
    def _():
        spread_modal_forces(forces[...], gathered)
        value = whole[...] + gain[...] * injected(gathered, inject, 0, total)
        whole[...] = value
        value = cosine[...] * value - before[...]
        free[...] = value
        scatter_tiles(collected(value, collect), gathered.at[0 : 8 * tiles], 0)
        layers[...] = mirrored_inverse(planes_of_modes(gathered, tiles), inverse_one, inverse_two)


def pushes(card, folds, arrived, pads):
    clear_pads(pads)
    _, even, met = noted(card)
    return take_forces(arrived, even, met, joints(folds, pads.shape[0] - 1), pads)


def damped_layers(push, layers, face_third):
    side = push.shape[0] // 3
    return jnp.concatenate(
        [
            layers[r * side : (r + 1) * side, :]
            + face_third[r : r + 1, :] * push[r * side : (r + 1) * side]
            for r in range(3)
        ],
        axis=0,
    )


def modal_layers(modes, layers, coupled, inverse_one, inverse_two):
    return layers[...] + mirrored_inverse(modal_response(modes, coupled), inverse_one, inverse_two)


def force_kernel(*refs):
    card, folds, refs = refs[:2], refs[2], refs[3:]
    arrived, layers, tables = in_turn(refs[:6]), refs[6], refs[7:13]
    forces, outs, (next_layers, pads) = refs[13], in_turn(refs[14:20]), refs[20:]
    coupled, forward_one, forward_two, inverse_one, inverse_two, face_third = tables
    damped, even, _ = noted(card)
    push = pushes(card, folds, arrived, pads)

    @pl.when(damped)
    def _():
        forces[...] = push
        next_layers[...] = damped_layers(push, layers, face_third)

    @pl.when(jnp.logical_not(damped))
    def _():
        modes = mirrored_forward(push, forward_one, forward_two)
        forces[...] = modes
        next_layers[...] = modal_layers(modes, layers, coupled, inverse_one, inverse_two)

    emit_payloads(next_layers[...], even, joints(folds, pads.shape[0] - 1), outs, pads)


def last_kernel(*refs):
    card, folds, refs = refs[:2], refs[2], refs[3:]
    arrived, layers, tables = in_turn(refs[:6]), refs[6], refs[7:13]
    free, gain, inject, rims = refs[13:17]
    state, faces, pads, gathered, shown, woven, held, sems = refs[17:]
    coupled, forward_one, forward_two, inverse_one, inverse_two, face_third = tables
    damped, _, _ = noted(card)
    s0, total = free.shape
    tiles = total // 128
    middle = slice(8, s0 - 8)
    ends = (0, s0 - 8)
    inner = copies([(free.at[middle], state.at[0, middle])], sems)
    outer = copies([(held.at[at : at + 8], state.at[0, at : at + 8]) for at in ends], sems, 1)
    broad = strips(free, 2 * CHUNK)
    moves = copies([(held.at[:, p], state.at[0, :, p]) for p in broad], sems)

    def show(values):
        for r, pair in enumerate(low_high_rows(values, woven, tiles)):
            for i, rows in enumerate(pair):
                shown[(3 * i + r) * tiles : (3 * i + r + 1) * tiles, :] = rows

    @pl.when(damped)
    def _():
        inner[0].start()

    push = pushes(card, folds, arrived, pads)

    @pl.when(damped)
    def _():
        spread_pml_forces(push, gathered, woven)
        for p in strips(free):
            for n, at in enumerate(ends):
                scale = wide(rims[8 * n : 8 * n + 8, :], CHUNK)
                moved = pml_rows(gathered, p.start, CHUNK, 8 * n)
                held[at : at + 8, p] = free[at : at + 8, p] + scale * moved
        for m in outer:
            m.start()
        show(damped_layers(push, layers, face_third))

    @pl.when(jnp.logical_not(damped))
    def _():
        modes = mirrored_forward(push, forward_one, forward_two)
        spread_modal_forces(modes, gathered)
        for i, (m, p) in enumerate(zip(moves, broad)):
            if i == len(broad) // 2:
                show(modal_layers(modes, layers, coupled, inverse_one, inverse_two))
            moved = injected(gathered, inject, p.start, 2 * CHUNK)
            held[:, p] = free[:, p] + gain[:, p] * moved
            m.start()

    last = pltpu.make_async_copy(shown, faces, sems.at[len(broad)])
    last.start()

    @pl.when(damped)
    def _():
        for m in inner + outer:
            m.wait()

    @pl.when(jnp.logical_not(damped))
    def _():
        for m in moves:
            m.wait()

    last.wait()


SCALAR = pl.BlockSpec(memory_space=pltpu.SMEM)
BLOCK = pl.BlockSpec(memory_space=pltpu.VMEM)
FAR = pl.BlockSpec(memory_space=pltpu.HBM)


def run(body, blocks, outs, scratch, near=(), far=(), far_outs=(), aliases=None, flops=0):
    moved = sum(b.size * b.dtype.itemsize for b in blocks)
    blocks = [
        pltpu.with_memory_space_constraint(b, pltpu.HBM) if i in far else b
        for i, b in enumerate(blocks)
    ]
    spots = {**dict.fromkeys(far, FAR), **dict.fromkeys(near, SCALAR)}
    return pl.pallas_call(
        body,
        out_shape=[
            jax.ShapeDtypeStruct(s, jnp.float32) if isinstance(s, tuple) else s for s in outs
        ],
        in_specs=[spots.get(i, BLOCK) for i in range(len(blocks))],
        out_specs=[
            FAR if i in far_outs else BLOCK
            for i, s in enumerate(outs)
        ],
        scratch_shapes=[
            pltpu.VMEM(s, jnp.float32) if isinstance(s, tuple) else s for s in scratch
        ],
        input_output_aliases=aliases or {},
        compiler_params=pltpu.CompilerParams(vmem_limit_bytes=32 * 1024 * 1024),
        cost_estimate=pl.CostEstimate(flops=flops, bytes_accessed=moved, transcendentals=0),
    )(*blocks)


def local(nx, ny, state_now, state_prev, pml_flags, interfaces):
    _, s0, cross = state_now.shape
    side = math.isqrt(cross)
    t = {k: jnp.asarray(v) for k, v in make_tables(s0, side).items()}
    tiles = cross // 128
    planes = (3 * side, 128)
    packed = (3 * side // 2, 128)
    pads = (1 + interfaces.shape[0], 3, side + 2 * OFF, 128)
    gathered = (16 * tiles, 128)
    full = (s0, cross)
    count = cross // CHUNK
    place = position((nx, ny), lax.axis_index("gx"), lax.axis_index("gy")).reshape(1)
    card = (pml_flags, place)
    routes = [pairing(nx, ny, parity, g) for parity in (0, 1) for g in SHIFTS]

    def exchange(payloads):
        return [lax.ppermute(payloads[k], ("gx", "gy"), routes[i]) for k, i in enumerate(ORDER)]

    *payloads, folds, now, prior, cosine = run(
        start_kernel,
        (
            *(pml_flags, place, interfaces, state_now, state_prev, t["cosine"]),
            *(t["collect"], t["inverse_one"], t["inverse_two"]),
        ),
        [packed] * 6 + [jax.ShapeDtypeStruct((8, 128), jnp.int32)] + [full] * 3,
        [
            *(planes, pads, gathered, planes),
            pltpu.SMEM(interfaces.shape, jnp.int32),
            pltpu.SemaphoreType.DMA((6 + count,)),
            *(pltpu.VMEM(t[k].shape, t[k].dtype) for k in ("collect", "inverse_one", "inverse_two")),
        ],
        near=(0, 1),
        far=range(2, 9),
    )
    names = ("coupled", "forward_one", "forward_two", "inverse_one", "inverse_two", "face_third")
    tables = [t[k] for k in names]
    shared = [t[k] for k in ("collect", "inverse_one", "inverse_two", "rows", "down", "inside")]
    for step in range(STEPS):
        arrived = exchange(payloads)
        if step == 0:
            free, layers = run(
                first_kernel,
                (pml_flags, now, prior, cosine, *shared),
                [full, planes],
                [gathered, planes, full],
                near=(0,),
                flops=10**9,
            )
        else:
            now, free, layers = run(
                free_kernel,
                (pml_flags, forces, free, now, cosine, t["gain"], t["inject"], t["ends"], *shared),
                [full, full, planes],
                [gathered, planes, full],
                near=(0,),
                aliases={2: 0},
                flops=10**9,
            )
        if step < STEPS - 1:
            forces, *payloads = run(
                force_kernel,
                (*card, folds, *arrived, layers, *tables),
                [planes] + [packed] * 6,
                [planes, pads],
                near=(0, 1),
            )
    state, faces = run(
        last_kernel,
        (*card, folds, *arrived, layers, *tables, free, t["gain"], t["inject"], t["ends"]),
        [(1, s0, cross), (6 * tiles, 128)],
        [
            *(pads, gathered, (6 * tiles, 128), planes, full),
            pltpu.SemaphoreType.DMA((3 + count,)),
        ],
        near=(0, 1),
        far_outs=(0, 1),
    )
    return state, faces.reshape(1, 6, cross)


def solution(mesh):
    placed = (
        P(("gx", "gy"), None, None),
        P(("gx", "gy"), None, None),
        P(("gx", "gy")),
        P(("gx", "gy"), None),
    )
    return jax.shard_map(
        functools.partial(local, mesh.shape["gx"], mesh.shape["gy"]),
        mesh=mesh,
        in_specs=placed,
        out_specs=(P(("gx", "gy"), None, None), P(("gx", "gy"), None, None)),
        check_vma=False,
    )
```
